1024 devices in a mesh: gx: 16 (over z_hi, y), gy: 16 (over z_lo, core), gz: 4 (over x).
Axes of the slice: x: 4, y: 4, z: 32 (z_hi: 4, z_lo: 8; z = z_hi * 8 + z_lo), core: 2. Of those that a mesh axis runs over, the one named last changes fastest.
Arguments:
- initial: float32 [128, 512, 2048], P('gz', 'gx', 'gy'), may hold values from -6 to 6
- source: float32 [128, 512, 2048], P('gz', 'gx', 'gy'), may hold values from -24 to 24
- permeability: float32 [128, 512, 2048], P('gz', 'gx', 'gy'), may hold values from 0.5 to 4
- velocity: bfloat16 [3, 128, 512, 2048], P(None, 'gz', 'gx', 'gy'), may hold values from -4 to 4
Outputs:
- updated: float32 [128, 512, 2048], P('gz', 'gx', 'gy')
The draws below stay inside these ranges and needn't reach their ends.
All inputs are finite; a program needn't handle non-finite values.
Results may differ from the reference program's by a relative error of at most 0.0003.
Values sent between devices are 32-bit elements; how exact they have to be, the bound alone decides.
No kernel may reach another device: no remote copies, remote signals or barrier semaphores. Data moves between devices by JAX's collectives and lax.ppermute only.
A program may use at most 64 MiB of HBM per device.

```python
import math
import jax
import jax.numpy as jnp

FACTOR = 8
DEGREE = 4
SWEEPS = 4
NZ = 128
NX = 512
NY = 2048


def block_levels(rng, dims, shards, least, largest):
    def one(dim, shards_of):
        draws = jax.random.uniform(jax.random.fold_in(jax.random.fold_in(rng, 6), dim), (shards_of,), jnp.float32, least / len(shards), largest / len(shards))
        return jnp.repeat(jnp.exp(draws), dims[dim] // shards_of).reshape((-1,) + (1,) * (len(dims) - dim - 1))

    loudness = one(*shards[0])
    for cut in shards[1:]:
        loudness = loudness * one(*cut)
    return loudness


def gaussian(key, extent, deviation, bound, split=(), dtype=jnp.bfloat16):
    factor_of = block_levels(key, extent, split, -0.22, 0.18) if split else 1.0
    entries = jax.random.normal(key, extent, jnp.float32) * deviation * factor_of
    return jnp.minimum(jnp.maximum(entries, -bound), bound).astype(dtype)


def setup_inputs(seed: int = 0) -> dict:
    keys = jax.random.split(jax.random.key(seed), 5)
    initial = gaussian(keys[0], (NZ, NX, NY), 1.0, 6.0, ((0, 4), (1, 16), (2, 16)), jnp.float32)
    source = gaussian(keys[1], (NZ, NX, NY), 4.0, 24.0, ((0, 4), (1, 16), (2, 16)), jnp.float32)
    permeability = jnp.clip(jnp.exp(math.log(4.0) - 2.0794415 * jax.random.uniform(keys[2], (NZ, NX, NY), jnp.float32) ** block_levels(keys[2], (NZ, NX, NY), ((0, 4), (1, 16), (2, 16)), -0.2, 0.2)), 0.5, 4.0)
    velocity = gaussian(keys[3], (3, NZ, NX, NY), 1.0, 4.0, ((1, 4), (2, 16), (3, 16)))
    return {"initial": initial, "source": source, "permeability": permeability, "velocity": velocity}


THETA = 1.15
DELTA = 0.85
OMEGA = 0.8


def stencil(padded, field, permeability, speeds):
    lows = [padded[:-2, 1:-1, 1:-1], padded[1:-1, :-2, 1:-1], padded[1:-1, 1:-1, :-2]]
    highs = [padded[2:, 1:-1, 1:-1], padded[1:-1, 2:, 1:-1], padded[1:-1, 1:-1, 2:]]
    total = permeability * (6.0 * field - (lows[0] + highs[0] + lows[1] + highs[1] + lows[2] + highs[2]))
    for axis_k in range(3):
        speed = speeds[axis_k]
        total = total + jnp.maximum(speed, 0.0) * (field - lows[axis_k]) + jnp.minimum(speed, 0.0) * (highs[axis_k] - field)
    return total


def coarse_sweep(padded, errors, coarse_res, coarse_perm):
    beside_all = padded[:-2, 1:-1, 1:-1] + padded[2:, 1:-1, 1:-1] + padded[1:-1, :-2, 1:-1] + padded[1:-1, 2:, 1:-1] + padded[1:-1, 1:-1, :-2] + padded[1:-1, 1:-1, 2:]
    applied = coarse_perm * (6.0 * errors - beside_all)
    return errors + OMEGA * (coarse_res - applied) / (6.0 * coarse_perm)


def block_sum(field):
    depth, width, length = field.shape
    return field.reshape(depth // FACTOR, FACTOR, width // FACTOR, FACTOR, length // FACTOR, FACTOR).sum(axis=(1, 3, 5))


def prolong(coarse):
    depth, width, length = coarse.shape
    wide = jnp.broadcast_to(coarse[:, None, :, None, :, None], (depth, FACTOR, width, FACTOR, length, FACTOR))
    return wide.reshape(depth * FACTOR, width * FACTOR, length * FACTOR)


def reference(initial, source, permeability, velocity):
    speeds = velocity.astype(jnp.float32)
    jacobi_diag = 6.0 * permeability + jnp.abs(speeds[0]) + jnp.abs(speeds[1]) + jnp.abs(speeds[2])

    def operate(field):
        return stencil(jnp.pad(field, 1), field, permeability, speeds)

    start_res = source - operate(initial)
    coarse_res = block_sum(start_res)
    coarse_perm = block_sum(permeability) * (64.0 / (FACTOR * FACTOR * FACTOR))
    errors = jnp.zeros_like(coarse_res)
    for sweep_index in range(SWEEPS):
        errors = coarse_sweep(jnp.pad(errors, 1), errors, coarse_res, coarse_perm)
    sigma = THETA / DELTA
    rho = 1.0 / sigma
    residual = start_res
    direction = residual / (THETA * jacobi_diag)
    smooth = jnp.zeros_like(initial)
    for degree_index in range(DEGREE):
        smooth = smooth + direction
        if degree_index + 1 < DEGREE:
            residual = residual - operate(direction)
            rho_new = 1.0 / (2.0 * sigma - rho)
            direction = rho_new * rho * direction + (2.0 * rho_new / DELTA) * residual / jacobi_diag
            rho = rho_new
    return initial + smooth + prolong(errors)
```

```python
import jax
import jax.numpy as jnp
from jax import lax
from jax.experimental import pallas as pl
from jax.experimental.pallas import tpu as pltpu
from jax.sharding import PartitionSpec as P

THETA = 1.15
DELTA = 0.85
OMEGA = 0.8
F32 = jnp.float32

NZ, NX, NY = 32, 32, 128
FULL = (NZ, NX, NY)

SIGMA = THETA / DELTA
RHO0 = 1.0 / SIGMA
RHO1 = 1.0 / (2.0 * SIGMA - RHO0)
RHO2 = 1.0 / (2.0 * SIGMA - RHO1)
RHO3 = 1.0 / (2.0 * SIGMA - RHO2)
A = (RHO1 * RHO0, RHO2 * RHO1, RHO3 * RHO2)
B = (2.0 * RHO1 / DELTA, 2.0 * RHO2 / DELTA, 2.0 * RHO3 / DELTA)

ZM1 = 136
YM1 = 40
XM1 = 104
ZM2 = 80
YM2 = 48
XM2 = 88


def iota(shape, dim):
    return lax.broadcasted_iota(jnp.int32, shape, dim)


def plane():
    return iota((NX, NY), 0), iota((NX, NY), 1)


def parity(axis):
    return lax.rem(lax.axis_index(axis), 2)


def put_out(stage, even, odd, axis):
    odd_one = parity(axis)
    even[...] = stage[1 - odd_one]
    odd[...] = stage[odd_one]


def take_in(halo, even, odd, axis):
    odd_one = parity(axis)
    halo[1 - odd_one] = even[...]
    halo[odd_one] = odd[...]


def to_column(row_values):
    row, lane = plane()
    spread = jnp.where(lane == row, jnp.broadcast_to(row_values, (NX, NY)), 0.0)
    return jnp.sum(spread, axis=1, keepdims=True)


def shift_lanes(x, amount):
    return pltpu.roll(x, amount % NY if isinstance(amount, int) else amount, 1)


def own_neighbours(field, g, z):
    here = field[z]
    total = g[0, z] * field[jnp.maximum(z - 1, 0)] + g[1, z] * field[jnp.minimum(z + 1, NZ - 1)]
    total += g[2, z] * pltpu.roll(here, 1, 0) + g[3, z] * pltpu.roll(here, NX - 1, 0)
    total += g[4, z] * pltpu.roll(here, 1, 1) + g[5, z] * pltpu.roll(here, NY - 1, 1)
    return total


def from_faces(z, zp, xp, yp):
    row, lane = plane()
    total = jnp.where(lane == 0, pltpu.roll(yp[0], lax.rem(NY - z, NY), 1), 0.0)
    total = jnp.where(lane == NY - 1, pltpu.roll(yp[1], NY - 1 - z, 1), total)
    total += jnp.where(row == 0, xp[0, pl.ds(z, 1), :], 0.0)
    total += jnp.where(row == NX - 1, xp[1, pl.ds(z, 1), :], 0.0)
    total += jnp.where(z == 0, zp[0], 0.0) + jnp.where(z == NZ - 1, zp[1], 0.0)
    return total


def pack(into, values, z, source, base):
    _, lane = plane()
    return jnp.where(lane == base + z, pltpu.roll(values, lax.rem(base + z + NY - source, NY), 1), into)


def first_kernel(u, f, p, w, g, diag, s, perm_sum, gzf, even, odd, yp, xp, stage):
    row, lane = plane()
    row8, lane8 = iota((8, NY), 0), iota((8, NY), 1)
    perm_sum[...] = jnp.zeros_like(perm_sum)

    def couplings(z):
        perm = p[z]
        speeds = [w[k, z].astype(F32) for k in range(3)]
        total = 6.0 * perm + jnp.abs(speeds[0]) + jnp.abs(speeds[1]) + jnp.abs(speeds[2])
        inverse = 1.0 / total
        pairs = []
        for speed in speeds:
            pairs.append((perm + jnp.maximum(speed, 0.0)) * inverse)
            pairs.append((perm - jnp.minimum(speed, 0.0)) * inverse)
        return perm, total, inverse, pairs

    def layer(z, carry):
        ylo, yhi, elo0, elo1, ehi0, ehi1 = carry
        perm, total, inverse, c = couplings(z)
        g[0, z] = jnp.where(z == 0, 0.0, c[0])
        g[1, z] = jnp.where(z == NZ - 1, 0.0, c[1])
        g[2, z] = jnp.where(row == 0, 0.0, c[2])
        g[3, z] = jnp.where(row == NX - 1, 0.0, c[3])
        g[4, z] = jnp.where(lane == 0, 0.0, c[4])
        g[5, z] = jnp.where(lane == NY - 1, 0.0, c[5])
        diag[z] = total
        here = u[z]
        res = f[z] * inverse - here + own_neighbours(u, g, z)
        s[z] = res
        perm_sum[z // 8] += perm
        for side, r, coupling in ((0, 0, c[2]), (1, NX - 1, c[3])):
            xp[side, pl.ds(z, 1), :] = here[r : r + 1]
            xp[side, pl.ds(NZ + z, 1), :] = res[r : r + 1]
            xp[side, pl.ds(2 * NZ + z, 1), :] = coupling[r : r + 1]
        for base, values, coupling in ((0, here, None), (32, res, None), (64, None, c)):
            ylo = pack(ylo, coupling[4] if coupling else values, z, 0, base)
            yhi = pack(yhi, coupling[5] if coupling else values, z, NY - 1, base)
        to_lo, to_hi = z, lax.rem(z + 1, NY)
        pick = lane8 == z
        elo0 = jnp.where(pick, pltpu.roll(c[2][0:8], to_lo, 1), elo0)
        elo1 = jnp.where(pick, pltpu.roll(c[3][NX - 8 :], to_lo, 1), elo1)
        ehi0 = jnp.where(pick, pltpu.roll(c[2][0:8], to_hi, 1), ehi0)
        ehi1 = jnp.where(pick, pltpu.roll(c[3][NX - 8 :], to_hi, 1), ehi1)
        return ylo, yhi, elo0, elo1, ehi0, ehi1

    zero, zero8 = jnp.zeros((NX, NY), F32), jnp.zeros((8, NY), F32)
    ylo, yhi, elo0, elo1, ehi0, ehi1 = lax.fori_loop(0, NZ, layer, (zero, zero, zero8, zero8, zero8, zero8))
    for side, body, first, last in ((0, ylo, elo0, elo1), (1, yhi, ehi0, ehi1)):
        yp[side, 0:NX, :] = body
        yp[side, NX:YM1, :] = jnp.where(row8 == 0, first[0:1], 0.0) + jnp.where(row8 == 1, last[7:8], 0.0)
        xp[side, 3 * NZ : XM1, :] = zero8
    for side, z in ((0, 0), (1, NZ - 1)):
        _, _, _, c = couplings(z)
        gzf[side] = c[side]
        stage[side, 0:32, :] = u[z]
        stage[side, 32:64, :] = s[z]
        stage[side, 64:96, :] = c[side]
        edges = jnp.where(lane == 0, c[4], 0.0) + jnp.where(lane == 1, pltpu.roll(c[5], 2, 1), 0.0)
        stage[side, 96:128, :] = edges
        stage[side, 128:136, :] = jnp.where(row8 == 0, c[2][0:1], 0.0) + jnp.where(row8 == 1, c[3][NX - 1 :], 0.0)
    put_out(stage, even, odd, "gz")


def y_body(yp, gzf, zh, side):
    _, lane = plane()
    source = 0 if side == 0 else NY - 1
    body = yp[side, 0:NX, :]
    for end, at in ((0, 32), (1, 63)):
        halo = zh[end, 0:32, :]
        body += jnp.where(lane == at, shift_lanes(gzf[end] * halo, at - source), 0.0)
        body = jnp.where(lane == 96 + end, shift_lanes(halo, 96 + end - source), body)
    return body


def first_y_kernel(zeven, zodd, gzf, yp, zh, even, odd, stage):
    take_in(zh, zeven, zodd, "gz")
    for side in (0, 1):
        stage[side, 0:NX, :] = y_body(yp, gzf, zh, side)
        stage[side, NX:YM1, :] = yp[side, NX:YM1, :]
    put_out(stage, even, odd, "gy")


def x_rows(xp, side, gzf, gy, zh, yh):
    row, lane = plane()
    row8 = iota((8, NY), 0)
    x = 0 if side == 0 else NX - 1
    res = xp[side, 32:64, :]
    lines = jnp.zeros((8, NY), F32)
    for end, at in ((0, 0), (1, NZ - 1)):
        line = zh[end, x : x + 1, :]
        res += jnp.where(row == at, gzf[end, x : x + 1, :] * line, 0.0)
        lines = jnp.where(row8 == end, line, lines)
    for end, at in ((0, 0), (1, NY - 1)):
        line = yh[end, x : x + 1, :]
        res += jnp.where(lane == at, to_column(gy[end][x : x + 1] * line), 0.0)
        lines = jnp.where(row8 == 2 + end, line, lines)
    return res, lines


def y_couplings(yp):
    return [shift_lanes(yp[side, 0:NX, :], 64) for side in (0, 1)]


def first_x_kernel(yeven, yodd, gzf, yp, xp, zh, yh, even, odd, stage):
    take_in(yh, yeven, yodd, "gy")
    gy = y_couplings(yp)
    for side in (0, 1):
        res, lines = x_rows(xp, side, gzf, gy, zh, yh)
        stage[side, 0:32, :] = xp[side, 0:32, :]
        stage[side, 32:64, :] = res
        stage[side, 64:96, :] = xp[side, 64:96, :]
        stage[side, 96:104, :] = lines
    put_out(stage, even, odd, "gx")


def z_halo_residual(side, res, zh1, xh, lines, yh, mine):
    row, lane = plane()
    x_edges = zh1[side, 128:136, :]
    y_edges = zh1[side, 96:128, :]
    total = res + zh1[side, 64:96, :] * mine
    total += jnp.where(row == 0, x_edges[0:1] * xh[0, lines + side : lines + side + 1, :], 0.0)
    total += jnp.where(row == NX - 1, x_edges[1:2] * xh[1, lines + side : lines + side + 1, :], 0.0)
    low = y_edges[:, 0:1] * yh[0, 0:NX, 96 + side : 97 + side]
    high = y_edges[:, 1:2] * yh[1, 0:NX, 96 + side : 97 + side]
    return total + jnp.where(lane == 0, low, 0.0) + jnp.where(lane == NY - 1, high, 0.0)


def y_halo_residual(side, res, yh1, xh, lines, mine):
    row, _ = plane()
    total = res + shift_lanes(yh1[side, 0:NX, :], 64) * mine
    at = lines + 2 + side
    total += jnp.where(row == 0, yh1[side, NX : NX + 1, :] * xh[0, at : at + 1, :], 0.0)
    total += jnp.where(row == NX - 1, yh1[side, NX + 1 : NX + 2, :] * xh[1, at : at + 1, :], 0.0)
    return total


def group_sums(x):
    return jnp.sum(x.reshape(4, 8, NY), axis=1)


def exact_dot(a, b):
    return jnp.dot(a, b, precision=lax.Precision.HIGHEST, preferred_element_type=F32)


def second_kernel(
    u, g, diag, s1, perm_sum, gzf, yp, xp, zh, yh, xeven, xodd,
    xh, s, d, acc, b, yp2, xp2, even, odd,
    s0, d0, cross, cross2, rsum, rows, stage,
):
    row, lane = plane()
    take_in(xh, xeven, xodd, "gx")
    gy = y_couplings(yp)
    zp, yq, zp2, yq2 = [], [], [], []
    for side, z in ((0, 0), (1, NZ - 1)):
        zp.append(gzf[side] * zh[side, 0:32, :])
        yq.append(gy[side] * yh[side, 0:NX, :])
        gx = xp[side, 64:96, :]
        cross[side] = gx * xh[side, 0:32, :]
        dz = z_halo_residual(side, zh[side, 32:64, :], zh, xh, 96, yh, u[z]) * (1.0 / THETA)
        dy = y_halo_residual(side, shift_lanes(yh[side, 0:NX, :], 96), yh, xh, 96, yp[side, 0:NX, :]) * (1.0 / THETA)
        dx = (xh[side, 32:64, :] + xh[side, 64:96, :] * xp[side, 0:32, :]) * (1.0 / THETA)
        zp2.append(gzf[side] * dz)
        yq2.append(gy[side] * dy)
        cross2[side] = gx * dx
    rsum[...] = jnp.zeros_like(rsum)

    def start(z, carry):
        res = s1[z] + from_faces(z, zp, cross, yq)
        s0[z] = res
        d0[z] = res * (1.0 / THETA)
        rsum[z // 8] += res * diag[z]
        return carry

    lax.fori_loop(0, NZ, start, 0)
    for block in range(4):
        rows[0, 4 * block : 4 * block + 4, :] = group_sums(rsum[block])
        rows[1, 4 * block : 4 * block + 4, :] = group_sums(perm_sum[block])
    select = jnp.where(iota((NY, NY), 0) // 8 == iota((NY, NY), 1), 1.0, 0.0)
    lane16 = iota((16, NY), 1)
    weights = jnp.where(lane16 < 16, exact_dot(rows[1], select), 1.0)
    rhs = jnp.where(lane16 < 16, (OMEGA * 8.0 / 6.0) * exact_dot(rows[0], select) / weights, 0.0)
    b[...] = rhs

    def step(z, carry):
        before = d0[z]
        res = s0[z] - before + own_neighbours(d0, g, z) + from_faces(z, zp2, cross2, yq2)
        after = A[0] * before + B[0] * res
        s0[z] = res
        d[z] = after
        acc[z] = u[z] + before + after
        return carry

    lax.fori_loop(0, NZ, step, 0)

    def partial(z, carry):
        ylo, yhi = carry
        here = d[z]
        res = s0[z] - here + own_neighbours(d, g, z)
        s[z] = res
        for side, r in ((0, 0), (1, NX - 1)):
            xp2[side, pl.ds(z, 1), :] = here[r : r + 1]
            xp2[side, pl.ds(NZ + z, 1), :] = res[r : r + 1]
        for base, values in ((0, here), (32, res)):
            ylo = pack(ylo, values, z, 0, base)
            yhi = pack(yhi, values, z, NY - 1, base)
        return ylo, yhi

    zero = jnp.zeros((NX, NY), F32)
    ylo, yhi = lax.fori_loop(0, NZ, partial, (zero, zero))
    yp2[0] = ylo
    yp2[1] = yhi
    for side, z in ((0, 0), (1, NZ - 1)):
        stage[side, 0:32, :] = d[z]
        stage[side, 32:64, :] = s[z]
        stage[side, 64:80, :] = rhs
    put_out(stage, even, odd, "gz")


def second_y_kernel(zeven, zodd, gzf, yp2, b, zh2, even, odd, b3, stage):
    take_in(zh2, zeven, zodd, "gz")
    lane16 = iota((16, NY), 1)
    wide = jnp.where(lane16 < 32, b[...], 0.0)
    for end in (0, 1):
        base = 32 * (end + 1)
        inside = (lane16 >= base) & (lane16 < base + 16)
        wide = jnp.where(inside, pltpu.roll(zh2[end, 64:80, :], base, 1), wide)
    b3[...] = wide
    for side in (0, 1):
        stage[side, 0:NX, :] = y_body(yp2, gzf, zh2, side)
        stage[side, NX:YM2, :] = wide
    put_out(stage, even, odd, "gy")


def second_x_kernel(yeven, yodd, gzf, yp, xp2, b3, zh2, yh2, even, odd, bw, stage):
    take_in(yh2, yeven, yodd, "gy")
    gy = y_couplings(yp)
    within = lax.rem(iota((16, NY), 1), 32)
    wide = jnp.where((within >= 3) & (within < 19), pltpu.roll(b3[...], 3, 1), 0.0)
    wide = jnp.where(within < 3, pltpu.roll(yh2[0, NX:YM2, :], NY - 13, 1), wide)
    wide = jnp.where((within >= 19) & (within < 22), pltpu.roll(yh2[1, NX:YM2, :], 19, 1), wide)
    bw[...] = wide
    for side in (0, 1):
        res, lines = x_rows(xp2, side, gzf, gy, zh2, yh2)
        stage[side, 0:32, :] = xp2[side, 0:32, :]
        stage[side, 32:64, :] = res
        stage[side, 64:72, :] = lines
        stage[side, 72:88, :] = wide
    put_out(stage, even, odd, "gx")


def coarse_solve(bw, xh2, ext, err, spread):
    ext[...] = jnp.zeros_like(ext)
    lane4 = iota((4, NY), 1)

    def blocks(values, z):
        if z < 3:
            at, shift = 4 * (z + 1), 32
        elif z < 7:
            at, shift = 4 * (z - 3), 0
        else:
            at, shift = 4 * (z - 7), 64
        rows = values[at : at + 4]
        rows = pltpu.roll(rows, NY - shift, 1) if shift else rows
        return jnp.where(lane4 < 22, rows, 0.0)

    mine, low, high = bw[...], xh2[0, 72:88, :], xh2[1, 72:88, :]
    for z in range(10):
        ext[z, 0:3, :] = blocks(low, z)[1:4]
        ext[z, 3:7, :] = blocks(mine, z)
        ext[z, 7:10, :] = blocks(high, z)[0:3]
    x, y = iota((16, NY), 0), iota((16, NY), 1)
    at_z, at_x, at_y = lax.axis_index("gz"), lax.axis_index("gx"), lax.axis_index("gy")
    last_z, last_x, last_y = lax.axis_size("gz") - 1, lax.axis_size("gx") - 1, lax.axis_size("gy") - 1
    inside = (x < 10) & (y < 22)
    inside &= ((x >= 3) | (at_x > 0)) & ((x < 7) | (at_x < last_x))
    inside &= ((y >= 3) | (at_y > 0)) & ((y < 19) | (at_y < last_y))
    keep = jnp.where(inside, 1.0, 0.0)
    keep_low = jnp.where(at_z > 0, keep, 0.0)
    keep_high = jnp.where(at_z < last_z, keep, 0.0)
    rhs = [ext[z] for z in range(10)]
    e = rhs
    for sweep in range(3):
        lo, hi = sweep + 1, 9 - sweep
        new = []
        for z in range(10):
            if z < lo or z >= hi:
                new.append(e[z])
                continue
            c = e[z]
            beside = e[z - 1] + e[z + 1] + pltpu.roll(c, 1, 0) + pltpu.roll(c, 15, 0) + pltpu.roll(c, 1, 1) + pltpu.roll(c, NY - 1, 1)
            v = (1.0 - OMEGA) * c + (OMEGA / 6.0) * beside + rhs[z]
            new.append(v * (keep_low if z < 3 else keep_high if z >= 7 else keep))
        e = new
    for z in range(4):
        err[4 * z : 4 * z + 4, :] = e[z + 3][3:7]
    select = jnp.where(iota((NY, NY), 0) == iota((NY, NY), 1) // 8 + 3, 1.0, 0.0)
    fine = exact_dot(err[...], select)
    for z in range(4):
        spread[z] = jnp.broadcast_to(fine[4 * z : 4 * z + 4][:, None, :], (4, 8, NY)).reshape(NX, NY)


def third_kernel(
    g, s2, d1, acc, gzf, yp, xp, zh, yh, xh, yp2, xp2, zh2, yh2, bw, xeven, xodd,
    out,
    xh2, s, d, cross, cross2, ext, err, spread,
):
    take_in(xh2, xeven, xodd, "gx")
    gy = y_couplings(yp)
    zp, yq, zp2, yq2 = [], [], [], []
    for side, z in ((0, 0), (1, NZ - 1)):
        zu, yu, xu = zh2[side, 0:32, :], yh2[side, 0:NX, :], xh2[side, 0:32, :]
        zp.append(gzf[side] * zu)
        yq.append(gy[side] * yu)
        gx = xp[side, 64:96, :]
        cross[side] = gx * xu
        dz = A[1] * zu + B[1] * z_halo_residual(side, zh2[side, 32:64, :], zh, xh2, 64, yh2, d1[z])
        dy = A[1] * yu + B[1] * y_halo_residual(side, shift_lanes(yu, 96), yh, xh2, 64, yp2[side])
        dx = A[1] * xu + B[1] * (xh2[side, 32:64, :] + xh[side, 64:96, :] * xp2[side, 0:32, :])
        zp2.append(gzf[side] * dz)
        yq2.append(gy[side] * dy)
        cross2[side] = gx * dx
    coarse_solve(bw, xh2, ext, err, spread)

    def step(z, carry):
        res = s2[z] + from_faces(z, zp, cross, yq)
        s[z] = res
        d[z] = A[1] * d1[z] + B[1] * res
        return carry

    lax.fori_loop(0, NZ, step, 0)

    def finish(z, carry):
        before = d[z]
        res = s[z] - before + own_neighbours(d, g, z) + from_faces(z, zp2, cross2, yq2)
        out[z] = acc[z] + before + (A[2] * before + B[2] * res) + spread[z // 8]
        return carry

    lax.fori_loop(0, NZ, finish, 0)


VM = pl.BlockSpec(memory_space=pltpu.VMEM)


def call(kernel, name, n_in, outs, scratch):
    return pl.pallas_call(
        kernel,
        out_shape=[jax.ShapeDtypeStruct(shape, F32) for shape in outs],
        in_specs=[VM] * n_in,
        out_specs=[VM] * len(outs),
        scratch_shapes=[pltpu.VMEM(shape, F32) for shape in scratch],
        compiler_params=pltpu.CompilerParams(vmem_limit_bytes=32 * 2**20),
        name=name,
    )


def swap(even, odd, axis):
    count = lax.axis_size(axis)
    results = []
    for first, values in ((0, even), (1, odd)):
        pairs = []
        for i in range(first, count - 1, 2):
            pairs += [(i, i + 1), (i + 1, i)]
        results.append(lax.ppermute(values, axis, pairs))
    return results


def per_device(u, f, p, w):
    face = (2, 32, NY)
    g, diag, s, perm_sum, gzf, even, odd, yp, xp = call(
        first_kernel, "faces", 4,
        [(6,) + FULL, FULL, FULL, (4, NX, NY), face, (ZM1, NY), (ZM1, NY), (2, YM1, NY), (2, XM1, NY)],
        [(2, ZM1, NY)],
    )(u, f, p, w)
    even, odd = swap(even, odd, "gz")
    zh, even, odd = call(
        first_y_kernel, "y_message", 4, [(2, ZM1, NY), (YM1, NY), (YM1, NY)], [(2, YM1, NY)]
    )(even, odd, gzf, yp)
    even, odd = swap(even, odd, "gy")
    yh, even, odd = call(
        first_x_kernel, "x_message", 6, [(2, YM1, NY), (XM1, NY), (XM1, NY)], [(2, XM1, NY)]
    )(even, odd, gzf, yp, xp, zh)
    even, odd = swap(even, odd, "gx")
    xh, s, d1, acc, b, yp2, xp2, even, odd = call(
        second_kernel, "two_steps", 12,
        [(2, XM1, NY), FULL, FULL, FULL, (16, NY), (2, NX, NY), (2, 64, NY), (ZM2, NY), (ZM2, NY)],
        [FULL, FULL, face, face, (4, NX, NY), (2, 16, NY), (2, ZM2, NY)],
    )(u, g, diag, s, perm_sum, gzf, yp, xp, zh, yh, even, odd)
    even, odd = swap(even, odd, "gz")
    zh2, even, odd, b3 = call(
        second_y_kernel, "y_message_2", 5, [(2, ZM2, NY), (YM2, NY), (YM2, NY), (16, NY)], [(2, YM2, NY)]
    )(even, odd, gzf, yp2, b)
    even, odd = swap(even, odd, "gy")
    yh2, even, odd, bw = call(
        second_x_kernel, "x_message_2", 7, [(2, YM2, NY), (XM2, NY), (XM2, NY), (16, NY)], [(2, XM2, NY)]
    )(even, odd, gzf, yp, xp2, b3, zh2)
    even, odd = swap(even, odd, "gx")
    (out,) = call(
        third_kernel, "last_steps", 17, [FULL],
        [(2, XM2, NY), FULL, FULL, face, face, (10, 16, NY), (16, NY), (4, NX, NY)],
    )(g, s, d1, acc, gzf, yp, xp, zh, yh, xh, yp2, xp2, zh2, yh2, bw, even, odd)
    return out


def solution(mesh):
    placed = (
        P("gz", "gx", "gy"),
        P("gz", "gx", "gy"),
        P("gz", "gx", "gy"),
        P(None, "gz", "gx", "gy"),
    )
    return jax.shard_map(
        per_device, mesh=mesh, in_specs=placed, out_specs=P("gz", "gx", "gy"), check_vma=False
    )
```

```python
import jax
import jax.numpy as jnp
from jax import lax
from jax.experimental import pallas as pl
from jax.experimental.pallas import tpu as pltpu
from jax.sharding import PartitionSpec as P

THETA = 1.15
DELTA = 0.85
OMEGA = 0.8
F32 = jnp.float32

NZ, NX, NY = 32, 32, 128
FULL = (NZ, NX, NY)

SIGMA = THETA / DELTA
RHO0 = 1.0 / SIGMA
RHO1 = 1.0 / (2.0 * SIGMA - RHO0)
RHO2 = 1.0 / (2.0 * SIGMA - RHO1)
RHO3 = 1.0 / (2.0 * SIGMA - RHO2)
A = (RHO1 * RHO0, RHO2 * RHO1, RHO3 * RHO2)
B = (2.0 * RHO1 / DELTA, 2.0 * RHO2 / DELTA, 2.0 * RHO3 / DELTA)

ZM1 = 136
YM1 = 40
XM1 = 104
ZM2 = 80
YM2 = 48
XM2 = 88


def iota(shape, dim):
    return lax.broadcasted_iota(jnp.int32, shape, dim)


def plane():
    return iota((NX, NY), 0), iota((NX, NY), 1)


def parity(axis):
    return lax.rem(lax.axis_index(axis), 2)


def put_out(stage, even, odd, axis):
    odd_one = parity(axis)
    even[...] = stage[1 - odd_one]
    odd[...] = stage[odd_one]


def take_in(halo, even, odd, axis):
    odd_one = parity(axis)
    halo[1 - odd_one] = even[...]
    halo[odd_one] = odd[...]


def to_column(row_values):
    row, lane = plane()
    spread = jnp.where(lane == row, jnp.broadcast_to(row_values, (NX, NY)), 0.0)
    return jnp.sum(spread, axis=1, keepdims=True)


def shift_lanes(x, amount):
    return pltpu.roll(x, amount % NY if isinstance(amount, int) else amount, 1)


def own_neighbours(field, g, z):
    here = field[z]
    total = g[0, z] * field[jnp.maximum(z - 1, 0)] + g[1, z] * field[jnp.minimum(z + 1, NZ - 1)]
    total += g[2, z] * pltpu.roll(here, 1, 0) + g[3, z] * pltpu.roll(here, NX - 1, 0)
    total += g[4, z] * pltpu.roll(here, 1, 1) + g[5, z] * pltpu.roll(here, NY - 1, 1)
    return total


def from_faces(z, zp, xp, yp):
    row, lane = plane()
    total = jnp.where(lane == 0, pltpu.roll(yp[0], lax.rem(NY - z, NY), 1), 0.0)
    total = jnp.where(lane == NY - 1, pltpu.roll(yp[1], NY - 1 - z, 1), total)
    total += jnp.where(row == 0, xp[0, pl.ds(z, 1), :], 0.0)
    total += jnp.where(row == NX - 1, xp[1, pl.ds(z, 1), :], 0.0)
    total += jnp.where(z == 0, zp[0], 0.0) + jnp.where(z == NZ - 1, zp[1], 0.0)
    return total


def pack(into, values, z, source, base):
    _, lane = plane()
    return jnp.where(lane == base + z, pltpu.roll(values, lax.rem(base + z + NY - source, NY), 1), into)


def couplings(perm, speeds):
    total = 6.0 * perm + jnp.abs(speeds[0]) + jnp.abs(speeds[1]) + jnp.abs(speeds[2])
    inverse = 1.0 / total
    pairs = []
    for speed in speeds:
        pairs.append((perm + jnp.maximum(speed, 0.0)) * inverse)
        pairs.append((perm - jnp.minimum(speed, 0.0)) * inverse)
    return total, inverse, pairs


def face_kernel(u, f, p, w, gzf, even, odd, planes, speed_planes, stage, sems):
    row, lane = plane()
    row8 = iota((8, NY), 0)
    copies = []
    for side, z, inner in ((0, 0, 1), (1, NZ - 1, NZ - 2)):
        for k, source in enumerate((u.at[z], u.at[inner], f.at[z], p.at[z])):
            copies.append(pltpu.make_async_copy(source, planes.at[side, k], sems.at[side, k]))
        for k in range(3):
            copies.append(pltpu.make_async_copy(w.at[k, z], speed_planes.at[side, k], sems.at[side, 4 + k]))
    for copy in copies:
        copy.start()
    for copy in copies:
        copy.wait()
    for side in (0, 1):
        here, inner = planes[side, 0], planes[side, 1]
        _, inverse, c = couplings(planes[side, 3], [speed_planes[side, k].astype(F32) for k in range(3)])
        res = planes[side, 2] * inverse - here + c[1 - side] * inner
        res += jnp.where(row == 0, 0.0, c[2]) * pltpu.roll(here, 1, 0)
        res += jnp.where(row == NX - 1, 0.0, c[3]) * pltpu.roll(here, NX - 1, 0)
        res += jnp.where(lane == 0, 0.0, c[4]) * pltpu.roll(here, 1, 1)
        res += jnp.where(lane == NY - 1, 0.0, c[5]) * pltpu.roll(here, NY - 1, 1)
        gzf[side] = c[side]
        stage[side, 0:32, :] = here
        stage[side, 32:64, :] = res
        stage[side, 64:96, :] = c[side]
        stage[side, 96:128, :] = jnp.where(lane == 0, c[4], 0.0) + jnp.where(lane == 1, pltpu.roll(c[5], 2, 1), 0.0)
        stage[side, 128:136, :] = jnp.where(row8 == 0, c[2][0:1], 0.0) + jnp.where(row8 == 1, c[3][NX - 1 :], 0.0)
    put_out(stage, even, odd, "gz")


def first_kernel(u_far, f_far, p_far, w_far, g, diag, s, perm_sum, yp, xp, u, f, p, w, sems):
    row, lane = plane()
    row8, lane8 = iota((8, NY), 0), iota((8, NY), 1)
    copies = []
    for part in range(4):
        rows = pl.ds(8 * part, 8)
        copies.append([
            pltpu.make_async_copy(u_far.at[rows], u.at[rows], sems.at[part, 0]),
            pltpu.make_async_copy(f_far.at[rows], f.at[rows], sems.at[part, 1]),
            pltpu.make_async_copy(p_far.at[rows], p.at[rows], sems.at[part, 2]),
            pltpu.make_async_copy(w_far.at[:, rows], w.at[:, rows], sems.at[part, 3]),
        ])
    for part in range(4):
        copies[part][0].start()
    for part in range(4):
        for copy in copies[part][1:]:
            copy.start()
    perm_sum[...] = jnp.zeros_like(perm_sum)

    def layer(z, carry):
        ylo, yhi, elo0, elo1, ehi0, ehi1 = carry
        perm = p[z]
        total, inverse, c = couplings(perm, [w[k, z].astype(F32) for k in range(3)])
        g[0, z] = jnp.where(z == 0, 0.0, c[0])
        g[1, z] = jnp.where(z == NZ - 1, 0.0, c[1])
        g[2, z] = jnp.where(row == 0, 0.0, c[2])
        g[3, z] = jnp.where(row == NX - 1, 0.0, c[3])
        g[4, z] = jnp.where(lane == 0, 0.0, c[4])
        g[5, z] = jnp.where(lane == NY - 1, 0.0, c[5])
        diag[z] = total
        here = u[z]
        res = f[z] * inverse - here + own_neighbours(u, g, z)
        s[z] = res
        perm_sum[z // 8] += perm
        for side, r, coupling in ((0, 0, c[2]), (1, NX - 1, c[3])):
            xp[side, pl.ds(z, 1), :] = here[r : r + 1]
            xp[side, pl.ds(NZ + z, 1), :] = res[r : r + 1]
            xp[side, pl.ds(2 * NZ + z, 1), :] = coupling[r : r + 1]
        for base, values, coupling in ((0, here, None), (32, res, None), (64, None, c)):
            ylo = pack(ylo, coupling[4] if coupling else values, z, 0, base)
            yhi = pack(yhi, coupling[5] if coupling else values, z, NY - 1, base)
        to_lo, to_hi = z, lax.rem(z + 1, NY)
        pick = lane8 == z
        elo0 = jnp.where(pick, pltpu.roll(c[2][0:8], to_lo, 1), elo0)
        elo1 = jnp.where(pick, pltpu.roll(c[3][NX - 8 :], to_lo, 1), elo1)
        ehi0 = jnp.where(pick, pltpu.roll(c[2][0:8], to_hi, 1), ehi0)
        ehi1 = jnp.where(pick, pltpu.roll(c[3][NX - 8 :], to_hi, 1), ehi1)
        return ylo, yhi, elo0, elo1, ehi0, ehi1

    zero, zero8 = jnp.zeros((NX, NY), F32), jnp.zeros((8, NY), F32)
    start = (zero, zero, zero8, zero8, zero8, zero8)
    for part in range(4):
        copies[part][0].wait()
    for part in range(4):
        for copy in copies[part][1:]:
            copy.wait()
        start = lax.fori_loop(8 * part, 8 * part + 8, layer, start, unroll=4)
    ylo, yhi, elo0, elo1, ehi0, ehi1 = start
    for side, body, first, last in ((0, ylo, elo0, elo1), (1, yhi, ehi0, ehi1)):
        yp[side, 0:NX, :] = body
        yp[side, NX:YM1, :] = jnp.where(row8 == 0, first[0:1], 0.0) + jnp.where(row8 == 1, last[7:8], 0.0)
        xp[side, 3 * NZ : XM1, :] = zero8


def y_body(yp, gzf, zh, side):
    _, lane = plane()
    source = 0 if side == 0 else NY - 1
    body = yp[side, 0:NX, :]
    for end, at in ((0, 32), (1, 63)):
        halo = zh[end, 0:32, :]
        body += jnp.where(lane == at, shift_lanes(gzf[end] * halo, at - source), 0.0)
        body = jnp.where(lane == 96 + end, shift_lanes(halo, 96 + end - source), body)
    return body


def first_y_kernel(zeven, zodd, gzf, yp, zh, even, odd, stage):
    take_in(zh, zeven, zodd, "gz")
    for side in (0, 1):
        stage[side, 0:NX, :] = y_body(yp, gzf, zh, side)
        stage[side, NX:YM1, :] = yp[side, NX:YM1, :]
    put_out(stage, even, odd, "gy")


def x_rows(xp, side, gzf, gy, zh, yh):
    row, lane = plane()
    row8 = iota((8, NY), 0)
    x = 0 if side == 0 else NX - 1
    res = xp[side, 32:64, :]
    lines = jnp.zeros((8, NY), F32)
    for end, at in ((0, 0), (1, NZ - 1)):
        line = zh[end, x : x + 1, :]
        res += jnp.where(row == at, gzf[end, x : x + 1, :] * line, 0.0)
        lines = jnp.where(row8 == end, line, lines)
    for end, at in ((0, 0), (1, NY - 1)):
        line = yh[end, x : x + 1, :]
        res += jnp.where(lane == at, to_column(gy[end][x : x + 1] * line), 0.0)
        lines = jnp.where(row8 == 2 + end, line, lines)
    return res, lines


def y_couplings(yp):
    return [shift_lanes(yp[side, 0:NX, :], 64) for side in (0, 1)]


def first_x_kernel(yeven, yodd, gzf, yp, xp, zh, yh, even, odd, stage):
    take_in(yh, yeven, yodd, "gy")
    gy = y_couplings(yp)
    for side in (0, 1):
        res, lines = x_rows(xp, side, gzf, gy, zh, yh)
        stage[side, 0:32, :] = xp[side, 0:32, :]
        stage[side, 32:64, :] = res
        stage[side, 64:96, :] = xp[side, 64:96, :]
        stage[side, 96:104, :] = lines
    put_out(stage, even, odd, "gx")


def z_halo_residual(side, res, zh1, xh, lines, yh, mine):
    row, lane = plane()
    x_edges = zh1[side, 128:136, :]
    y_edges = zh1[side, 96:128, :]
    total = res + zh1[side, 64:96, :] * mine
    total += jnp.where(row == 0, x_edges[0:1] * xh[0, lines + side : lines + side + 1, :], 0.0)
    total += jnp.where(row == NX - 1, x_edges[1:2] * xh[1, lines + side : lines + side + 1, :], 0.0)
    low = y_edges[:, 0:1] * yh[0, 0:NX, 96 + side : 97 + side]
    high = y_edges[:, 1:2] * yh[1, 0:NX, 96 + side : 97 + side]
    return total + jnp.where(lane == 0, low, 0.0) + jnp.where(lane == NY - 1, high, 0.0)


def y_halo_residual(side, res, yh1, xh, lines, mine):
    row, _ = plane()
    total = res + shift_lanes(yh1[side, 0:NX, :], 64) * mine
    at = lines + 2 + side
    total += jnp.where(row == 0, yh1[side, NX : NX + 1, :] * xh[0, at : at + 1, :], 0.0)
    total += jnp.where(row == NX - 1, yh1[side, NX + 1 : NX + 2, :] * xh[1, at : at + 1, :], 0.0)
    return total


def group_sums(x):
    return jnp.sum(x.reshape(4, 8, NY), axis=1)


def exact_dot(a, b):
    return jnp.dot(a, b, precision=lax.Precision.HIGHEST, preferred_element_type=F32)


def second_kernel(
    u, g, diag, s1, perm_sum, gzf, yp, xp, zh, yh, xeven, xodd,
    xh, s, d, acc, b, even, odd,
    s0, d0, cross, cross2, rsum, rows, stage,
):
    row, lane = plane()
    take_in(xh, xeven, xodd, "gx")
    gy = y_couplings(yp)
    zp, yq, zp2, yq2 = [], [], [], []
    for side, z in ((0, 0), (1, NZ - 1)):
        zp.append(gzf[side] * zh[side, 0:32, :])
        yq.append(gy[side] * yh[side, 0:NX, :])
        gx = xp[side, 64:96, :]
        cross[side] = gx * xh[side, 0:32, :]
        dz = z_halo_residual(side, zh[side, 32:64, :], zh, xh, 96, yh, u[z]) * (1.0 / THETA)
        dy = y_halo_residual(side, shift_lanes(yh[side, 0:NX, :], 96), yh, xh, 96, yp[side, 0:NX, :]) * (1.0 / THETA)
        dx = (xh[side, 32:64, :] + xh[side, 64:96, :] * xp[side, 0:32, :]) * (1.0 / THETA)
        zp2.append(gzf[side] * dz)
        yq2.append(gy[side] * dy)
        cross2[side] = gx * dx
    rsum[...] = jnp.zeros_like(rsum)

    def start(z, carry):
        res = s1[z] + from_faces(z, zp, cross, yq)
        s0[z] = res
        d0[z] = res * (1.0 / THETA)
        rsum[z // 8] += res * diag[z]
        return carry

    lax.fori_loop(0, NZ, start, 0, unroll=8)
    for block in range(4):
        rows[0, 4 * block : 4 * block + 4, :] = group_sums(rsum[block])
        rows[1, 4 * block : 4 * block + 4, :] = group_sums(perm_sum[block])
    select = jnp.where(iota((NY, NY), 0) // 8 == iota((NY, NY), 1), 1.0, 0.0)
    lane16 = iota((16, NY), 1)
    weights = jnp.where(lane16 < 16, exact_dot(rows[1], select), 1.0)
    rhs = jnp.where(lane16 < 16, (OMEGA * 8.0 / 6.0) * exact_dot(rows[0], select) / weights, 0.0)
    b[...] = rhs

    def step(z, carry):
        before = d0[z]
        res = s0[z] - before + own_neighbours(d0, g, z) + from_faces(z, zp2, cross2, yq2)
        after = A[0] * before + B[0] * res
        s[z] = res
        d[z] = after
        acc[z] = u[z] + before + after
        return carry

    lax.fori_loop(0, NZ, step, 0, unroll=8)

    for side, z in ((0, 0), (1, NZ - 1)):
        stage[side, 0:32, :] = d[z]
        stage[side, 32:64, :] = s[z] - d[z] + own_neighbours(d, g, z)
        stage[side, 64:80, :] = rhs
    put_out(stage, even, odd, "gz")


def partial_kernel(g, s1, d, s, yp2, xp2):
    def partial(z, carry):
        ylo, yhi = carry
        here = d[z]
        res = s1[z] - here + own_neighbours(d, g, z)
        s[z] = res
        for side, r in ((0, 0), (1, NX - 1)):
            xp2[side, pl.ds(z, 1), :] = here[r : r + 1]
            xp2[side, pl.ds(NZ + z, 1), :] = res[r : r + 1]
        for base, values in ((0, here), (32, res)):
            ylo = pack(ylo, values, z, 0, base)
            yhi = pack(yhi, values, z, NY - 1, base)
        return ylo, yhi

    zero = jnp.zeros((NX, NY), F32)
    ylo, yhi = lax.fori_loop(0, NZ, partial, (zero, zero), unroll=8)
    yp2[0] = ylo
    yp2[1] = yhi


def second_y_kernel(zeven, zodd, gzf, yp2, b, zh2, even, odd, b3, stage):
    take_in(zh2, zeven, zodd, "gz")
    lane16 = iota((16, NY), 1)
    wide = jnp.where(lane16 < 32, b[...], 0.0)
    for end in (0, 1):
        base = 32 * (end + 1)
        inside = (lane16 >= base) & (lane16 < base + 16)
        wide = jnp.where(inside, pltpu.roll(zh2[end, 64:80, :], base, 1), wide)
    b3[...] = wide
    for side in (0, 1):
        stage[side, 0:NX, :] = y_body(yp2, gzf, zh2, side)
        stage[side, NX:YM2, :] = wide
    put_out(stage, even, odd, "gy")


def second_x_kernel(yeven, yodd, gzf, yp, xp2, b3, zh2, yh2, even, odd, bw, stage):
    take_in(yh2, yeven, yodd, "gy")
    gy = y_couplings(yp)
    within = lax.rem(iota((16, NY), 1), 32)
    wide = jnp.where((within >= 3) & (within < 19), pltpu.roll(b3[...], 3, 1), 0.0)
    wide = jnp.where(within < 3, pltpu.roll(yh2[0, NX:YM2, :], NY - 13, 1), wide)
    wide = jnp.where((within >= 19) & (within < 22), pltpu.roll(yh2[1, NX:YM2, :], 19, 1), wide)
    bw[...] = wide
    for side in (0, 1):
        res, lines = x_rows(xp2, side, gzf, gy, zh2, yh2)
        stage[side, 0:32, :] = xp2[side, 0:32, :]
        stage[side, 32:64, :] = res
        stage[side, 64:72, :] = lines
        stage[side, 72:88, :] = wide
    put_out(stage, even, odd, "gx")


def coarse_solve(bw, xh2, ext, err, spread):
    ext[...] = jnp.zeros_like(ext)
    lane4 = iota((4, NY), 1)

    def blocks(values, z):
        if z < 3:
            at, shift = 4 * (z + 1), 32
        elif z < 7:
            at, shift = 4 * (z - 3), 0
        else:
            at, shift = 4 * (z - 7), 64
        rows = values[at : at + 4]
        rows = pltpu.roll(rows, NY - shift, 1) if shift else rows
        return jnp.where(lane4 < 22, rows, 0.0)

    mine, low, high = bw[...], xh2[0, 72:88, :], xh2[1, 72:88, :]
    for z in range(10):
        ext[z, 0:3, :] = blocks(low, z)[1:4]
        ext[z, 3:7, :] = blocks(mine, z)
        ext[z, 7:10, :] = blocks(high, z)[0:3]
    x, y = iota((16, NY), 0), iota((16, NY), 1)
    at_z, at_x, at_y = lax.axis_index("gz"), lax.axis_index("gx"), lax.axis_index("gy")
    last_z, last_x, last_y = lax.axis_size("gz") - 1, lax.axis_size("gx") - 1, lax.axis_size("gy") - 1
    inside = (x < 10) & (y < 22)
    inside &= ((x >= 3) | (at_x > 0)) & ((x < 7) | (at_x < last_x))
    inside &= ((y >= 3) | (at_y > 0)) & ((y < 19) | (at_y < last_y))
    keep = jnp.where(inside, 1.0, 0.0)
    keep_low = jnp.where(at_z > 0, keep, 0.0)
    keep_high = jnp.where(at_z < last_z, keep, 0.0)
    rhs = [ext[z] for z in range(10)]
    e = rhs
    for sweep in range(3):
        lo, hi = sweep + 1, 9 - sweep
        new = []
        for z in range(10):
            if z < lo or z >= hi:
                new.append(e[z])
                continue
            c = e[z]
            beside = e[z - 1] + e[z + 1] + pltpu.roll(c, 1, 0) + pltpu.roll(c, 15, 0) + pltpu.roll(c, 1, 1) + pltpu.roll(c, NY - 1, 1)
            v = (1.0 - OMEGA) * c + (OMEGA / 6.0) * beside + rhs[z]
            new.append(v * (keep_low if z < 3 else keep_high if z >= 7 else keep))
        e = new
    for z in range(4):
        err[4 * z : 4 * z + 4, :] = e[z + 3][3:7]
    select = jnp.where(iota((NY, NY), 0) == iota((NY, NY), 1) // 8 + 3, 1.0, 0.0)
    fine = exact_dot(err[...], select)
    for z in range(4):
        spread[z] = jnp.broadcast_to(fine[4 * z : 4 * z + 4][:, None, :], (4, 8, NY)).reshape(NX, NY)


def third_kernel(
    g, s2, d1, acc, gzf, yp, xp, zh, yh, xh, yp2, xp2, zh2, yh2, bw, xeven, xodd,
    out,
    xh2, s, d, cross, cross2, ext, err, spread,
):
    take_in(xh2, xeven, xodd, "gx")
    gy = y_couplings(yp)
    zp, yq, zp2, yq2 = [], [], [], []
    for side, z in ((0, 0), (1, NZ - 1)):
        zu, yu, xu = zh2[side, 0:32, :], yh2[side, 0:NX, :], xh2[side, 0:32, :]
        zp.append(gzf[side] * zu)
        yq.append(gy[side] * yu)
        gx = xp[side, 64:96, :]
        cross[side] = gx * xu
        dz = A[1] * zu + B[1] * z_halo_residual(side, zh2[side, 32:64, :], zh, xh2, 64, yh2, d1[z])
        dy = A[1] * yu + B[1] * y_halo_residual(side, shift_lanes(yu, 96), yh, xh2, 64, yp2[side])
        dx = A[1] * xu + B[1] * (xh2[side, 32:64, :] + xh[side, 64:96, :] * xp2[side, 0:32, :])
        zp2.append(gzf[side] * dz)
        yq2.append(gy[side] * dy)
        cross2[side] = gx * dx
    coarse_solve(bw, xh2, ext, err, spread)

    def step(z, carry):
        res = s2[z] + from_faces(z, zp, cross, yq)
        s[z] = res
        d[z] = A[1] * d1[z] + B[1] * res
        return carry

    lax.fori_loop(0, NZ, step, 0, unroll=8)

    def finish(z, carry):
        before = d[z]
        res = s[z] - before + own_neighbours(d, g, z) + from_faces(z, zp2, cross2, yq2)
        out[z] = acc[z] + before + (A[2] * before + B[2] * res) + spread[z // 8]
        return carry

    lax.fori_loop(0, NZ, finish, 0, unroll=8)


VM = pl.BlockSpec(memory_space=pltpu.VMEM)
HBM = pl.BlockSpec(memory_space=pltpu.HBM)


def call(kernel, name, n_in, outs, scratch, us=0.2, place=VM, more=()):
    return pl.pallas_call(
        kernel,
        out_shape=[jax.ShapeDtypeStruct(shape, F32) for shape in outs],
        in_specs=[place] * n_in,
        out_specs=[VM] * len(outs),
        scratch_shapes=[pltpu.VMEM(shape, F32) for shape in scratch] + list(more),
        compiler_params=pltpu.CompilerParams(vmem_limit_bytes=32 * 2**20),
        cost_estimate=pl.CostEstimate(flops=0, transcendentals=0, bytes_accessed=int(us * 3e6)),
        name=name,
    )


def swap(even, odd, axis):
    count = lax.axis_size(axis)
    results = []
    for first, values in ((1, odd), (0, even)):
        pairs = []
        for i in range(first, count - 1, 2):
            pairs += [(i, i + 1), (i + 1, i)]
        results.append(lax.ppermute(values, axis, pairs))
    return results[::-1]


def per_device(u, f, p, w):
    face = (2, 32, NY)
    far = [pltpu.with_memory_space_constraint(x, pltpu.HBM) for x in (u, f, p, w)]
    gzf, even, odd = call(
        face_kernel, "z_faces", 4, [face, (ZM1, NY), (ZM1, NY)], [(2, 4, NX, NY)], 1.0, HBM,
        [pltpu.VMEM((2, 3, NX, NY), jnp.bfloat16), pltpu.VMEM((2, ZM1, NY), F32), pltpu.SemaphoreType.DMA((2, 7))],
    )(*far)
    g, diag, s, perm_sum, yp, xp = call(
        first_kernel, "block", 4,
        [(6,) + FULL, FULL, FULL, (4, NX, NY), (2, YM1, NY), (2, XM1, NY)], [FULL, FULL, FULL], 3.0, HBM,
        [pltpu.VMEM((3,) + FULL, jnp.bfloat16), pltpu.SemaphoreType.DMA((4, 4))],
    )(*far)
    even, odd = swap(even, odd, "gz")
    zh, even, odd = call(
        first_y_kernel, "y_message", 4, [(2, ZM1, NY), (YM1, NY), (YM1, NY)], [(2, YM1, NY)]
    )(even, odd, gzf, yp)
    even, odd = swap(even, odd, "gy")
    yh, even, odd = call(
        first_x_kernel, "x_message", 6, [(2, YM1, NY), (XM1, NY), (XM1, NY)], [(2, XM1, NY)]
    )(even, odd, gzf, yp, xp, zh)
    even, odd = swap(even, odd, "gx")
    xh, s, d1, acc, b, even, odd = call(
        second_kernel, "two_steps", 12,
        [(2, XM1, NY), FULL, FULL, FULL, (16, NY), (ZM2, NY), (ZM2, NY)],
        [FULL, FULL, face, face, (4, NX, NY), (2, 16, NY), (2, ZM2, NY)], 3.0,
    )(u, g, diag, s, perm_sum, gzf, yp, xp, zh, yh, even, odd)
    s, yp2, xp2 = call(
        partial_kernel, "block_2", 3, [FULL, (2, NX, NY), (2, 64, NY)], [], 1.5
    )(g, s, d1)
    even, odd = swap(even, odd, "gz")
    zh2, even, odd, b3 = call(
        second_y_kernel, "y_message_2", 5, [(2, ZM2, NY), (YM2, NY), (YM2, NY), (16, NY)], [(2, YM2, NY)]
    )(even, odd, gzf, yp2, b)
    even, odd = swap(even, odd, "gy")
    yh2, even, odd, bw = call(
        second_x_kernel, "x_message_2", 7, [(2, YM2, NY), (XM2, NY), (XM2, NY), (16, NY)], [(2, XM2, NY)]
    )(even, odd, gzf, yp, xp2, b3, zh2)
    even, odd = swap(even, odd, "gx")
    (out,) = call(
        third_kernel, "last_steps", 17, [FULL],
        [(2, XM2, NY), FULL, FULL, face, face, (10, 16, NY), (16, NY), (4, NX, NY)], 3.0,
    )(g, s, d1, acc, gzf, yp, xp, zh, yh, xh, yp2, xp2, zh2, yh2, bw, even, odd)
    return out


def solution(mesh):
    placed = (
        P("gz", "gx", "gy"),
        P("gz", "gx", "gy"),
        P("gz", "gx", "gy"),
        P(None, "gz", "gx", "gy"),
    )
    return jax.shard_map(
        per_device, mesh=mesh, in_specs=placed, out_specs=P("gz", "gx", "gy"), check_vma=False
    )
```

```python
import jax
import jax.numpy as jnp
from jax import lax
from jax.experimental import pallas as pl
from jax.experimental.pallas import tpu as pltpu
from jax.sharding import PartitionSpec as P

THETA = 1.15
DELTA = 0.85
OMEGA = 0.8
F32 = jnp.float32

NZ, NX, NY = 32, 32, 128
FULL = (NZ, NX, NY)

SIGMA = THETA / DELTA
RHO0 = 1.0 / SIGMA
RHO1 = 1.0 / (2.0 * SIGMA - RHO0)
RHO2 = 1.0 / (2.0 * SIGMA - RHO1)
RHO3 = 1.0 / (2.0 * SIGMA - RHO2)
A = (RHO1 * RHO0, RHO2 * RHO1, RHO3 * RHO2)
B = (2.0 * RHO1 / DELTA, 2.0 * RHO2 / DELTA, 2.0 * RHO3 / DELTA)

ZM1 = 136
YM1 = 40
XM1 = 104
ZM2 = 80
YM2 = 48
XM2 = 88


def iota(shape, dim):
    return lax.broadcasted_iota(jnp.int32, shape, dim)


def plane():
    return iota((NX, NY), 0), iota((NX, NY), 1)


def parity(axis):
    return lax.rem(lax.axis_index(axis), 2)


def put_out(stage, even, odd, axis):
    odd_one = parity(axis)
    even[...] = stage[1 - odd_one]
    odd[...] = stage[odd_one]


def take_in(halo, even, odd, axis):
    odd_one = parity(axis)
    halo[1 - odd_one] = even[...]
    halo[odd_one] = odd[...]


def to_column(row_values):
    row, lane = plane()
    spread = jnp.where(lane == row, jnp.broadcast_to(row_values, (NX, NY)), 0.0)
    return jnp.sum(spread, axis=1, keepdims=True)


def shift_lanes(x, amount):
    return pltpu.roll(x, amount % NY if isinstance(amount, int) else amount, 1)


def own_neighbours(field, g, z):
    here = field[z]
    total = g[0, z] * field[jnp.maximum(z - 1, 0)] + g[1, z] * field[jnp.minimum(z + 1, NZ - 1)]
    total += g[2, z] * pltpu.roll(here, 1, 0) + g[3, z] * pltpu.roll(here, NX - 1, 0)
    total += g[4, z] * pltpu.roll(here, 1, 1) + g[5, z] * pltpu.roll(here, NY - 1, 1)
    return total


def from_faces(z, zp, xp, yp):
    row, lane = plane()
    total = jnp.where(lane == 0, pltpu.roll(yp[0], lax.rem(NY - z, NY), 1), 0.0)
    total = jnp.where(lane == NY - 1, pltpu.roll(yp[1], NY - 1 - z, 1), total)
    total += jnp.where(row == 0, xp[0, pl.ds(z, 1), :], 0.0)
    total += jnp.where(row == NX - 1, xp[1, pl.ds(z, 1), :], 0.0)
    total += jnp.where(z == 0, zp[0], 0.0) + jnp.where(z == NZ - 1, zp[1], 0.0)
    return total


def pack(into, values, z, source, base):
    _, lane = plane()
    return jnp.where(lane == base + z, pltpu.roll(values, lax.rem(base + z + NY - source, NY), 1), into)


def couplings(perm, speeds):
    total = 6.0 * perm + jnp.abs(speeds[0]) + jnp.abs(speeds[1]) + jnp.abs(speeds[2])
    inverse = 1.0 / total
    pairs = []
    for speed in speeds:
        pairs.append((perm + jnp.maximum(speed, 0.0)) * inverse)
        pairs.append((perm - jnp.minimum(speed, 0.0)) * inverse)
    return total, inverse, pairs


def face_kernel(u, f, p, w, gzf, even, odd, planes, speed_planes, stage, sems):
    row, lane = plane()
    row8 = iota((8, NY), 0)
    copies = []
    for side, z, inner in ((0, 0, 1), (1, NZ - 1, NZ - 2)):
        for k, source in enumerate((u.at[z], u.at[inner], f.at[z], p.at[z])):
            copies.append(pltpu.make_async_copy(source, planes.at[side, k], sems.at[side, k]))
        for k in range(3):
            copies.append(pltpu.make_async_copy(w.at[k, z], speed_planes.at[side, k], sems.at[side, 4 + k]))
    for copy in copies:
        copy.start()
    for copy in copies:
        copy.wait()
    for side in (0, 1):
        here, inner = planes[side, 0], planes[side, 1]
        _, inverse, c = couplings(planes[side, 3], [speed_planes[side, k].astype(F32) for k in range(3)])
        res = planes[side, 2] * inverse - here + c[1 - side] * inner
        res += jnp.where(row == 0, 0.0, c[2]) * pltpu.roll(here, 1, 0)
        res += jnp.where(row == NX - 1, 0.0, c[3]) * pltpu.roll(here, NX - 1, 0)
        res += jnp.where(lane == 0, 0.0, c[4]) * pltpu.roll(here, 1, 1)
        res += jnp.where(lane == NY - 1, 0.0, c[5]) * pltpu.roll(here, NY - 1, 1)
        gzf[side] = c[side]
        stage[side, 0:32, :] = here
        stage[side, 32:64, :] = res
        stage[side, 64:96, :] = c[side]
        stage[side, 96:128, :] = jnp.where(lane == 0, c[4], 0.0) + jnp.where(lane == 1, pltpu.roll(c[5], 2, 1), 0.0)
        stage[side, 128:136, :] = jnp.where(row8 == 0, c[2][0:1], 0.0) + jnp.where(row8 == 1, c[3][NX - 1 :], 0.0)
    put_out(stage, even, odd, "gz")


def first_kernel(u_far, f_far, p_far, w_far, g, diag, s, perm_sum, yp, xp, u, f, p, w, sems):
    row, lane = plane()
    row8, lane8 = iota((8, NY), 0), iota((8, NY), 1)
    copies = []
    for part in range(4):
        rows = pl.ds(8 * part, 8)
        copies.append([
            pltpu.make_async_copy(u_far.at[rows], u.at[rows], sems.at[part, 0]),
            pltpu.make_async_copy(f_far.at[rows], f.at[rows], sems.at[part, 1]),
            pltpu.make_async_copy(p_far.at[rows], p.at[rows], sems.at[part, 2]),
            pltpu.make_async_copy(w_far.at[:, rows], w.at[:, rows], sems.at[part, 3]),
        ])
    for part in range(4):
        copies[part][0].start()
    for part in range(4):
        for copy in copies[part][1:]:
            copy.start()
    perm_sum[...] = jnp.zeros_like(perm_sum)

    def layer(z, carry):
        ylo, yhi, elo0, elo1, ehi0, ehi1 = carry
        perm = p[z]
        total, inverse, c = couplings(perm, [w[k, z].astype(F32) for k in range(3)])
        g[0, z] = jnp.where(z == 0, 0.0, c[0])
        g[1, z] = jnp.where(z == NZ - 1, 0.0, c[1])
        g[2, z] = jnp.where(row == 0, 0.0, c[2])
        g[3, z] = jnp.where(row == NX - 1, 0.0, c[3])
        g[4, z] = jnp.where(lane == 0, 0.0, c[4])
        g[5, z] = jnp.where(lane == NY - 1, 0.0, c[5])
        diag[z] = total
        here = u[z]
        res = f[z] * inverse - here + own_neighbours(u, g, z)
        s[z] = res
        perm_sum[z // 8] += perm
        for side, r, coupling in ((0, 0, c[2]), (1, NX - 1, c[3])):
            xp[side, pl.ds(z, 1), :] = here[r : r + 1]
            xp[side, pl.ds(NZ + z, 1), :] = res[r : r + 1]
            xp[side, pl.ds(2 * NZ + z, 1), :] = coupling[r : r + 1]
        for base, values, coupling in ((0, here, None), (32, res, None), (64, None, c)):
            ylo = pack(ylo, coupling[4] if coupling else values, z, 0, base)
            yhi = pack(yhi, coupling[5] if coupling else values, z, NY - 1, base)
        to_lo, to_hi = z, lax.rem(z + 1, NY)
        pick = lane8 == z
        elo0 = jnp.where(pick, pltpu.roll(c[2][0:8], to_lo, 1), elo0)
        elo1 = jnp.where(pick, pltpu.roll(c[3][NX - 8 :], to_lo, 1), elo1)
        ehi0 = jnp.where(pick, pltpu.roll(c[2][0:8], to_hi, 1), ehi0)
        ehi1 = jnp.where(pick, pltpu.roll(c[3][NX - 8 :], to_hi, 1), ehi1)
        return ylo, yhi, elo0, elo1, ehi0, ehi1

    zero, zero8 = jnp.zeros((NX, NY), F32), jnp.zeros((8, NY), F32)
    start = (zero, zero, zero8, zero8, zero8, zero8)
    for part in range(4):
        copies[part][0].wait()
    for part in range(4):
        for copy in copies[part][1:]:
            copy.wait()
        start = lax.fori_loop(8 * part, 8 * part + 8, layer, start, unroll=4)
    ylo, yhi, elo0, elo1, ehi0, ehi1 = start
    for side, body, first, last in ((0, ylo, elo0, elo1), (1, yhi, ehi0, ehi1)):
        yp[side, 0:NX, :] = body
        yp[side, NX:YM1, :] = jnp.where(row8 == 0, first[0:1], 0.0) + jnp.where(row8 == 1, last[7:8], 0.0)
        xp[side, 3 * NZ : XM1, :] = zero8


def y_body(yp, gzf, zh, side):
    _, lane = plane()
    source = 0 if side == 0 else NY - 1
    body = yp[side, 0:NX, :]
    for end, at in ((0, 32), (1, 63)):
        halo = zh[end, 0:32, :]
        body += jnp.where(lane == at, shift_lanes(gzf[end] * halo, at - source), 0.0)
        body = jnp.where(lane == 96 + end, shift_lanes(halo, 96 + end - source), body)
    return body


def first_y_kernel(zeven, zodd, gzf, yp, zh, even, odd, stage):
    take_in(zh, zeven, zodd, "gz")
    for side in (0, 1):
        stage[side, 0:NX, :] = y_body(yp, gzf, zh, side)
        stage[side, NX:YM1, :] = yp[side, NX:YM1, :]
    put_out(stage, even, odd, "gy")


def x_rows(xp, side, gzf, gy, zh, yh):
    row, lane = plane()
    row8 = iota((8, NY), 0)
    x = 0 if side == 0 else NX - 1
    res = xp[side, 32:64, :]
    lines = jnp.zeros((8, NY), F32)
    for end, at in ((0, 0), (1, NZ - 1)):
        line = zh[end, x : x + 1, :]
        res += jnp.where(row == at, gzf[end, x : x + 1, :] * line, 0.0)
        lines = jnp.where(row8 == end, line, lines)
    for end, at in ((0, 0), (1, NY - 1)):
        line = yh[end, x : x + 1, :]
        res += jnp.where(lane == at, to_column(gy[end][x : x + 1] * line), 0.0)
        lines = jnp.where(row8 == 2 + end, line, lines)
    return res, lines


def y_couplings(yp):
    return [shift_lanes(yp[side, 0:NX, :], 64) for side in (0, 1)]


def first_x_kernel(yodd, yeven, gzf, yp, xp, zh, yh, even, odd, stage):
    take_in(yh, yeven, yodd, "gy")
    gy = y_couplings(yp)
    for side in (0, 1):
        res, lines = x_rows(xp, side, gzf, gy, zh, yh)
        stage[side, 0:32, :] = xp[side, 0:32, :]
        stage[side, 32:64, :] = res
        stage[side, 64:96, :] = xp[side, 64:96, :]
        stage[side, 96:104, :] = lines
    put_out(stage, even, odd, "gx")


def z_halo_residual(side, res, zh1, xh, lines, yh, mine):
    row, lane = plane()
    x_edges = zh1[side, 128:136, :]
    y_edges = zh1[side, 96:128, :]
    total = res + zh1[side, 64:96, :] * mine
    total += jnp.where(row == 0, x_edges[0:1] * xh[0, lines + side : lines + side + 1, :], 0.0)
    total += jnp.where(row == NX - 1, x_edges[1:2] * xh[1, lines + side : lines + side + 1, :], 0.0)
    low = y_edges[:, 0:1] * yh[0, 0:NX, 96 + side : 97 + side]
    high = y_edges[:, 1:2] * yh[1, 0:NX, 96 + side : 97 + side]
    return total + jnp.where(lane == 0, low, 0.0) + jnp.where(lane == NY - 1, high, 0.0)


def y_halo_residual(side, res, yh1, xh, lines, mine):
    row, _ = plane()
    total = res + shift_lanes(yh1[side, 0:NX, :], 64) * mine
    at = lines + 2 + side
    total += jnp.where(row == 0, yh1[side, NX : NX + 1, :] * xh[0, at : at + 1, :], 0.0)
    total += jnp.where(row == NX - 1, yh1[side, NX + 1 : NX + 2, :] * xh[1, at : at + 1, :], 0.0)
    return total


def group_sums(x):
    return jnp.sum(x.reshape(4, 8, NY), axis=1)


def exact_dot(a, b):
    return jnp.dot(a, b, precision=lax.Precision.HIGHEST, preferred_element_type=F32)


def second_kernel(
    u, g, diag, s1, perm_sum, gzf, yp, xp, zh, yh, xodd, xeven,
    xh, s, d, acc, b, even, odd,
    s0, d0, cross, cross2, rsum, rows, stage,
):
    row, lane = plane()
    take_in(xh, xeven, xodd, "gx")
    gy = y_couplings(yp)
    zp, yq, zp2, yq2 = [], [], [], []
    for side, z in ((0, 0), (1, NZ - 1)):
        zp.append(gzf[side] * zh[side, 0:32, :])
        yq.append(gy[side] * yh[side, 0:NX, :])
        gx = xp[side, 64:96, :]
        cross[side] = gx * xh[side, 0:32, :]
        dz = z_halo_residual(side, zh[side, 32:64, :], zh, xh, 96, yh, u[z]) * (1.0 / THETA)
        dy = y_halo_residual(side, shift_lanes(yh[side, 0:NX, :], 96), yh, xh, 96, yp[side, 0:NX, :]) * (1.0 / THETA)
        dx = (xh[side, 32:64, :] + xh[side, 64:96, :] * xp[side, 0:32, :]) * (1.0 / THETA)
        zp2.append(gzf[side] * dz)
        yq2.append(gy[side] * dy)
        cross2[side] = gx * dx
    rsum[...] = jnp.zeros_like(rsum)

    def start(z, carry):
        res = s1[z] + from_faces(z, zp, cross, yq)
        s0[z] = res
        d0[z] = res * (1.0 / THETA)
        rsum[z // 8] += res * diag[z]
        return carry

    lax.fori_loop(0, NZ, start, 0, unroll=8)
    for block in range(4):
        rows[0, 4 * block : 4 * block + 4, :] = group_sums(rsum[block])
        rows[1, 4 * block : 4 * block + 4, :] = group_sums(perm_sum[block])
    select = jnp.where(iota((NY, NY), 0) // 8 == iota((NY, NY), 1), 1.0, 0.0)
    lane16 = iota((16, NY), 1)
    weights = jnp.where(lane16 < 16, exact_dot(rows[1], select), 1.0)
    rhs = jnp.where(lane16 < 16, (OMEGA * 8.0 / 6.0) * exact_dot(rows[0], select) / weights, 0.0)
    b[...] = rhs

    def step(z, carry):
        before = d0[z]
        res = s0[z] - before + own_neighbours(d0, g, z) + from_faces(z, zp2, cross2, yq2)
        after = A[0] * before + B[0] * res
        s[z] = res
        d[z] = after
        acc[z] = u[z] + before + after
        return carry

    lax.fori_loop(0, NZ, step, 0, unroll=8)

    for side, z in ((0, 0), (1, NZ - 1)):
        stage[side, 0:32, :] = d[z]
        stage[side, 32:64, :] = s[z] - d[z] + own_neighbours(d, g, z)
        stage[side, 64:80, :] = rhs
    put_out(stage, even, odd, "gz")


def partial_kernel(g, s1, d, s, yp2, xp2):
    def partial(z, carry):
        ylo, yhi = carry
        here = d[z]
        res = s1[z] - here + own_neighbours(d, g, z)
        s[z] = res
        for side, r in ((0, 0), (1, NX - 1)):
            xp2[side, pl.ds(z, 1), :] = here[r : r + 1]
            xp2[side, pl.ds(NZ + z, 1), :] = res[r : r + 1]
        for base, values in ((0, here), (32, res)):
            ylo = pack(ylo, values, z, 0, base)
            yhi = pack(yhi, values, z, NY - 1, base)
        return ylo, yhi

    zero = jnp.zeros((NX, NY), F32)
    ylo, yhi = lax.fori_loop(0, NZ, partial, (zero, zero), unroll=8)
    yp2[0] = ylo
    yp2[1] = yhi


def second_y_kernel(zeven, zodd, gzf, yp2, b, zh2, even, odd, b3, stage):
    take_in(zh2, zeven, zodd, "gz")
    lane16 = iota((16, NY), 1)
    wide = jnp.where(lane16 < 32, b[...], 0.0)
    for end in (0, 1):
        base = 32 * (end + 1)
        inside = (lane16 >= base) & (lane16 < base + 16)
        wide = jnp.where(inside, pltpu.roll(zh2[end, 64:80, :], base, 1), wide)
    b3[...] = wide
    for side in (0, 1):
        stage[side, 0:NX, :] = y_body(yp2, gzf, zh2, side)
        stage[side, NX:YM2, :] = wide
    put_out(stage, even, odd, "gy")


def second_x_kernel(yodd, yeven, gzf, yp, xp2, b3, zh2, yh2, even, odd, bw, stage):
    take_in(yh2, yeven, yodd, "gy")
    gy = y_couplings(yp)
    within = lax.rem(iota((16, NY), 1), 32)
    wide = jnp.where((within >= 3) & (within < 19), pltpu.roll(b3[...], 3, 1), 0.0)
    wide = jnp.where(within < 3, pltpu.roll(yh2[0, NX:YM2, :], NY - 13, 1), wide)
    wide = jnp.where((within >= 19) & (within < 22), pltpu.roll(yh2[1, NX:YM2, :], 19, 1), wide)
    bw[...] = wide
    for side in (0, 1):
        res, lines = x_rows(xp2, side, gzf, gy, zh2, yh2)
        stage[side, 0:32, :] = xp2[side, 0:32, :]
        stage[side, 32:64, :] = res
        stage[side, 64:72, :] = lines
        stage[side, 72:88, :] = wide
    put_out(stage, even, odd, "gx")


def coarse_solve(bw, xh2, ext, err, spread):
    ext[...] = jnp.zeros_like(ext)
    lane4 = iota((4, NY), 1)

    def blocks(values, z):
        if z < 3:
            at, shift = 4 * (z + 1), 32
        elif z < 7:
            at, shift = 4 * (z - 3), 0
        else:
            at, shift = 4 * (z - 7), 64
        rows = values[at : at + 4]
        rows = pltpu.roll(rows, NY - shift, 1) if shift else rows
        return jnp.where(lane4 < 22, rows, 0.0)

    mine, low, high = bw[...], xh2[0, 72:88, :], xh2[1, 72:88, :]
    for z in range(10):
        ext[z, 0:3, :] = blocks(low, z)[1:4]
        ext[z, 3:7, :] = blocks(mine, z)
        ext[z, 7:10, :] = blocks(high, z)[0:3]
    x, y = iota((16, NY), 0), iota((16, NY), 1)
    at_z, at_x, at_y = lax.axis_index("gz"), lax.axis_index("gx"), lax.axis_index("gy")
    last_z, last_x, last_y = lax.axis_size("gz") - 1, lax.axis_size("gx") - 1, lax.axis_size("gy") - 1
    inside = (x < 10) & (y < 22)
    inside &= ((x >= 3) | (at_x > 0)) & ((x < 7) | (at_x < last_x))
    inside &= ((y >= 3) | (at_y > 0)) & ((y < 19) | (at_y < last_y))
    keep = jnp.where(inside, 1.0, 0.0)
    keep_low = jnp.where(at_z > 0, keep, 0.0)
    keep_high = jnp.where(at_z < last_z, keep, 0.0)
    rhs = [ext[z] for z in range(10)]
    e = rhs
    for sweep in range(3):
        lo, hi = sweep + 1, 9 - sweep
        new = []
        for z in range(10):
            if z < lo or z >= hi:
                new.append(e[z])
                continue
            c = e[z]
            beside = e[z - 1] + e[z + 1] + pltpu.roll(c, 1, 0) + pltpu.roll(c, 15, 0) + pltpu.roll(c, 1, 1) + pltpu.roll(c, NY - 1, 1)
            v = (1.0 - OMEGA) * c + (OMEGA / 6.0) * beside + rhs[z]
            new.append(v * (keep_low if z < 3 else keep_high if z >= 7 else keep))
        e = new
    for z in range(4):
        err[4 * z : 4 * z + 4, :] = e[z + 3][3:7]
    select = jnp.where(iota((NY, NY), 0) == iota((NY, NY), 1) // 8 + 3, 1.0, 0.0)
    fine = exact_dot(err[...], select)
    for z in range(4):
        spread[z] = jnp.broadcast_to(fine[4 * z : 4 * z + 4][:, None, :], (4, 8, NY)).reshape(NX, NY)


def third_kernel(
    g, s2, d1, acc, gzf, yp, xp, zh, yh, xh, yp2, xp2, zh2, yh2, bw, xodd, xeven,
    out,
    xh2, s, d, cross, cross2, ext, err, spread,
):
    take_in(xh2, xeven, xodd, "gx")
    gy = y_couplings(yp)
    zp, yq, zp2, yq2 = [], [], [], []
    for side, z in ((0, 0), (1, NZ - 1)):
        zu, yu, xu = zh2[side, 0:32, :], yh2[side, 0:NX, :], xh2[side, 0:32, :]
        zp.append(gzf[side] * zu)
        yq.append(gy[side] * yu)
        gx = xp[side, 64:96, :]
        cross[side] = gx * xu
        dz = A[1] * zu + B[1] * z_halo_residual(side, zh2[side, 32:64, :], zh, xh2, 64, yh2, d1[z])
        dy = A[1] * yu + B[1] * y_halo_residual(side, shift_lanes(yu, 96), yh, xh2, 64, yp2[side])
        dx = A[1] * xu + B[1] * (xh2[side, 32:64, :] + xh[side, 64:96, :] * xp2[side, 0:32, :])
        zp2.append(gzf[side] * dz)
        yq2.append(gy[side] * dy)
        cross2[side] = gx * dx
    coarse_solve(bw, xh2, ext, err, spread)

    def step(z, carry):
        res = s2[z] + from_faces(z, zp, cross, yq)
        s[z] = res
        d[z] = A[1] * d1[z] + B[1] * res
        return carry

    lax.fori_loop(0, NZ, step, 0, unroll=8)

    def finish(z, carry):
        before = d[z]
        res = s[z] - before + own_neighbours(d, g, z) + from_faces(z, zp2, cross2, yq2)
        out[z] = acc[z] + before + (A[2] * before + B[2] * res) + spread[z // 8]
        return carry

    lax.fori_loop(0, NZ, finish, 0, unroll=8)


VM = pl.BlockSpec(memory_space=pltpu.VMEM)
HBM = pl.BlockSpec(memory_space=pltpu.HBM)


def call(kernel, name, n_in, outs, scratch, us=0.2, place=VM, more=()):
    return pl.pallas_call(
        kernel,
        out_shape=[jax.ShapeDtypeStruct(shape, F32) for shape in outs],
        in_specs=[place] * n_in,
        out_specs=[VM] * len(outs),
        scratch_shapes=[pltpu.VMEM(shape, F32) for shape in scratch] + list(more),
        compiler_params=pltpu.CompilerParams(vmem_limit_bytes=32 * 2**20),
        cost_estimate=pl.CostEstimate(flops=0, transcendentals=0, bytes_accessed=int(us * 3e6)),
        name=name,
    )


def swap(even, odd, axis):
    count = lax.axis_size(axis)
    results = []
    for first, values in ((1, odd), (0, even)):
        pairs = []
        for i in range(first, count - 1, 2):
            pairs += [(i, i + 1), (i + 1, i)]
        results.append(lax.ppermute(values, axis, pairs))
    return results[::-1]


def per_device(u, f, p, w):
    face = (2, 32, NY)
    far = [pltpu.with_memory_space_constraint(x, pltpu.HBM) for x in (u, f, p, w)]
    gzf, even, odd = call(
        face_kernel, "z_faces", 4, [face, (ZM1, NY), (ZM1, NY)], [(2, 4, NX, NY)], 1.0, HBM,
        [pltpu.VMEM((2, 3, NX, NY), jnp.bfloat16), pltpu.VMEM((2, ZM1, NY), F32), pltpu.SemaphoreType.DMA((2, 7))],
    )(*far)
    g, diag, s, perm_sum, yp, xp = call(
        first_kernel, "block", 4,
        [(6,) + FULL, FULL, FULL, (4, NX, NY), (2, YM1, NY), (2, XM1, NY)], [FULL, FULL, FULL], 3.0, HBM,
        [pltpu.VMEM((3,) + FULL, jnp.bfloat16), pltpu.SemaphoreType.DMA((4, 4))],
    )(*far)
    even, odd = swap(even, odd, "gz")
    zh, even, odd = call(
        first_y_kernel, "y_message", 4, [(2, ZM1, NY), (YM1, NY), (YM1, NY)], [(2, YM1, NY)]
    )(even, odd, gzf, yp)
    even, odd = swap(even, odd, "gy")
    yh, even, odd = call(
        first_x_kernel, "x_message", 6, [(2, YM1, NY), (XM1, NY), (XM1, NY)], [(2, XM1, NY)]
    )(odd, even, gzf, yp, xp, zh)
    even, odd = swap(even, odd, "gx")
    xh, s, d1, acc, b, even, odd = call(
        second_kernel, "two_steps", 12,
        [(2, XM1, NY), FULL, FULL, FULL, (16, NY), (ZM2, NY), (ZM2, NY)],
        [FULL, FULL, face, face, (4, NX, NY), (2, 16, NY), (2, ZM2, NY)], 3.0,
    )(u, g, diag, s, perm_sum, gzf, yp, xp, zh, yh, odd, even)
    s, yp2, xp2 = call(
        partial_kernel, "block_2", 3, [FULL, (2, NX, NY), (2, 64, NY)], [], 1.5
    )(g, s, d1)
    even, odd = swap(even, odd, "gz")
    zh2, even, odd, b3 = call(
        second_y_kernel, "y_message_2", 5, [(2, ZM2, NY), (YM2, NY), (YM2, NY), (16, NY)], [(2, YM2, NY)]
    )(even, odd, gzf, yp2, b)
    even, odd = swap(even, odd, "gy")
    yh2, even, odd, bw = call(
        second_x_kernel, "x_message_2", 7, [(2, YM2, NY), (XM2, NY), (XM2, NY), (16, NY)], [(2, XM2, NY)]
    )(odd, even, gzf, yp, xp2, b3, zh2)
    even, odd = swap(even, odd, "gx")
    (out,) = call(
        third_kernel, "last_steps", 17, [FULL],
        [(2, XM2, NY), FULL, FULL, face, face, (10, 16, NY), (16, NY), (4, NX, NY)], 3.0,
    )(g, s, d1, acc, gzf, yp, xp, zh, yh, xh, yp2, xp2, zh2, yh2, bw, odd, even)
    return out


def solution(mesh):
    placed = (
        P("gz", "gx", "gy"),
        P("gz", "gx", "gy"),
        P("gz", "gx", "gy"),
        P(None, "gz", "gx", "gy"),
    )
    return jax.shard_map(
        per_device, mesh=mesh, in_specs=placed, out_specs=P("gz", "gx", "gy"), check_vma=False
    )
```

```python
import jax
import jax.numpy as jnp
from jax import lax
from jax.experimental import pallas as pl
from jax.experimental.pallas import tpu as pltpu
from jax.sharding import PartitionSpec as P

THETA = 1.15
DELTA = 0.85
OMEGA = 0.8
F32 = jnp.float32

NZ, NX, NY = 32, 32, 128
FULL = (NZ, NX, NY)

SIGMA = THETA / DELTA
RHO0 = 1.0 / SIGMA
RHO1 = 1.0 / (2.0 * SIGMA - RHO0)
RHO2 = 1.0 / (2.0 * SIGMA - RHO1)
RHO3 = 1.0 / (2.0 * SIGMA - RHO2)
A = (RHO1 * RHO0, RHO2 * RHO1, RHO3 * RHO2)
B = (2.0 * RHO1 / DELTA, 2.0 * RHO2 / DELTA, 2.0 * RHO3 / DELTA)

XM1 = 104
ZM1 = 136
YM1 = 40
XM2 = 80
ZM2 = 88
YM2 = 56


def iota(shape, dim):
    return lax.broadcasted_iota(jnp.int32, shape, dim)


def plane():
    return iota((NX, NY), 0), iota((NX, NY), 1)


def parity(axis):
    return lax.rem(lax.axis_index(axis), 2)


def put_out(stage, even, odd, axis):
    odd_one = parity(axis)
    even[...] = stage[1 - odd_one]
    odd[...] = stage[odd_one]


def take_in(halo, even, odd, axis):
    odd_one = parity(axis)
    halo[1 - odd_one] = even[...]
    halo[odd_one] = odd[...]


def fourths(shape=(NX, NY)):
    return lax.rem(iota(shape, 1), 4)


def layer_lanes(z, shape=(NX, NY)):
    lane = iota(shape, 1)
    return (lane == 4 * z) | (lane == lax.rem(4 * z + NY - 1, NY))


def ends(lane):
    return (lane == 0) | (lane == NY - 1)


def shift_lanes(x, amount):
    return pltpu.roll(x, amount % NY, 1)


def columns(row_values):
    row, lane = plane()
    wide = jnp.broadcast_to(row_values, (NX, NY))
    low = jnp.sum(jnp.where(lane == 4 * row, wide, 0.0), axis=1, keepdims=True)
    high = jnp.sum(jnp.where(lane == lax.rem(4 * row + NY - 1, NY), wide, 0.0), axis=1, keepdims=True)
    return jnp.where(lane == 0, low, 0.0) + jnp.where(lane == NY - 1, high, 0.0)


def combined_row(values):
    row, lane = plane()
    low = jnp.where(lane == 4 * row, jnp.broadcast_to(values[:, 0:1], (NX, NY)), 0.0)
    high = jnp.where(lane == lax.rem(4 * row + NY - 1, NY), jnp.broadcast_to(values[:, NY - 1 :], (NX, NY)), 0.0)
    return jnp.sum(low + high, axis=0, keepdims=True)


def combine(low, high, q):
    return jnp.where(fourths(low.shape) == 0, shift_lanes(low, -q), shift_lanes(high, -q - 1))


def own_neighbours(field, g, z):
    here = field[z]
    total = g[0, z] * field[jnp.maximum(z - 1, 0)] + g[1, z] * field[jnp.minimum(z + 1, NZ - 1)]
    total += g[2, z] * pltpu.roll(here, 1, 0) + g[3, z] * pltpu.roll(here, NX - 1, 0)
    total += g[4, z] * pltpu.roll(here, 1, 1) + g[5, z] * pltpu.roll(here, NY - 1, 1)
    return total


def from_faces(z, zp, xp, yp):
    row, lane = plane()
    total = jnp.where(ends(lane), pltpu.roll(yp, lax.rem(NY - 4 * z, NY), 1), 0.0)
    total += jnp.where(row == 0, xp[0, pl.ds(z, 1), :], 0.0)
    total += jnp.where(row == NX - 1, xp[1, pl.ds(z, 1), :], 0.0)
    total += jnp.where(z == 0, zp[0], 0.0) + jnp.where(z == NZ - 1, zp[1], 0.0)
    return total


def couplings(perm, speeds):
    total = 6.0 * perm + jnp.abs(speeds[0]) + jnp.abs(speeds[1]) + jnp.abs(speeds[2])
    inverse = 1.0 / total
    pairs = []
    for speed in speeds:
        pairs.append((perm + jnp.maximum(speed, 0.0)) * inverse)
        pairs.append((perm - jnp.minimum(speed, 0.0)) * inverse)
    return total, inverse, pairs


def face_rows(side):
    return (slice(0, 8), 0) if side == 0 else (slice(NX - 8, NX), 7)


def inner_neighbours(field, c, z, side):
    rows, _ = face_rows(side)
    lane = iota((8, NY), 1)
    here = field[z, rows, :]
    total = jnp.where(z == 0, 0.0, c[0]) * field[jnp.maximum(z - 1, 0), rows, :]
    total += jnp.where(z == NZ - 1, 0.0, c[1]) * field[jnp.minimum(z + 1, NZ - 1), rows, :]
    total += c[3 - side] * pltpu.roll(here, 7 if side == 0 else 1, 0)
    total += jnp.where(lane == 0, 0.0, c[4]) * pltpu.roll(here, 1, 1)
    total += jnp.where(lane == NY - 1, 0.0, c[5]) * pltpu.roll(here, NY - 1, 1)
    return total


def face_kernel(u_far, f_far, p_far, w_far, u, f, p, w, xp, even, odd, sems):
    lane8 = iota((8, NY), 1)
    copies = []
    for part in range(4):
        rows = pl.ds(8 * part, 8)
        copies.append([
            pltpu.make_async_copy(u_far.at[rows], u.at[rows], sems.at[part, 0]),
            pltpu.make_async_copy(f_far.at[rows], f.at[rows], sems.at[part, 1]),
            pltpu.make_async_copy(p_far.at[rows], p.at[rows], sems.at[part, 2]),
            pltpu.make_async_copy(w_far.at[:, rows], w.at[:, rows], sems.at[part, 3]),
        ])
    for part in range(4):
        copies[part][0].start()
    for part in range(4):
        for copy in copies[part][1:]:
            copy.start()

    def face(z, side):
        rows, _ = face_rows(side)
        half = slice(0, 16) if side == 0 else slice(NX - 16, NX)
        speeds = [w[k, z, half, :].astype(F32)[8 * side : 8 * side + 8] for k in range(3)]
        return couplings(p[z, rows, :], speeds)

    def layer(z, carry):
        edges = []
        for side in (0, 1):
            rows, r = face_rows(side)
            _, inverse, c = face(z, side)
            here = u[z, rows, :]
            res = f[z, rows, :] * inverse - here + inner_neighbours(u, c, z, side)
            for base, values in ((0, here), (NZ, res), (2 * NZ, c[2 + side])):
                xp[side, pl.ds(base + z, 1), :] = values[r : r + 1]
            merged = pltpu.roll(jnp.where(lane8 == 0, c[4], c[5]), 4 * z, 1)
            edges.append(jnp.where(layer_lanes(z, (8, NY)), merged, carry[side]))
        return tuple(edges)

    edges = (jnp.zeros((8, NY), F32),) * 2
    for part in range(4):
        copies[part][0].wait()
    for part in range(4):
        for copy in copies[part][1:]:
            copy.wait()
        edges = lax.fori_loop(8 * part, 8 * part + 8, layer, edges, unroll=4)
    for side in (0, 1):
        _, r = face_rows(side)
        xp[side, 96:104, :] = jnp.zeros((8, NY), F32)
        for end, z in ((0, 0), (1, NZ - 1)):
            _, _, c = face(z, side)
            xp[side, 96 + end : 97 + end, :] = c[end][r : r + 1]
        xp[side, 98:99, :] = edges[side][r : r + 1]
    put_out(xp, even, odd, "gx")


def block_kernel(u, f, p, w, g, diag, s, perm_sum, zp, yp):
    row, lane = plane()
    perm_sum[...] = jnp.zeros_like(perm_sum)

    def layer(z, carry):
        pu, ps, pg = carry
        perm = p[z]
        total, inverse, c = couplings(perm, [w[k, z].astype(F32) for k in range(3)])
        g[0, z] = jnp.where(z == 0, 0.0, c[0])
        g[1, z] = jnp.where(z == NZ - 1, 0.0, c[1])
        g[2, z] = jnp.where(row == 0, 0.0, c[2])
        g[3, z] = jnp.where(row == NX - 1, 0.0, c[3])
        g[4, z] = jnp.where(lane == 0, 0.0, c[4])
        g[5, z] = jnp.where(lane == NY - 1, 0.0, c[5])
        diag[z] = total
        here = u[z]
        res = f[z] * inverse - here + own_neighbours(u, g, z)
        s[z] = res
        perm_sum[z // 8] += perm
        mine = layer_lanes(z)
        pu = jnp.where(mine, pltpu.roll(here, 4 * z, 1), pu)
        ps = jnp.where(mine, pltpu.roll(res, 4 * z, 1), ps)
        pg = jnp.where(mine, pltpu.roll(jnp.where(lane == 0, c[4], c[5]), 4 * z, 1), pg)
        return pu, ps, pg

    zero = jnp.zeros((NX, NY), F32)
    pu, ps, pg = lax.fori_loop(0, NZ, layer, (zero, zero, zero), unroll=4)
    yp[0:32, :] = pu
    yp[32:64, :] = ps
    yp[64:96, :] = pg
    for side, z in ((0, 0), (1, NZ - 1)):
        _, _, c = couplings(p[z], [w[k, z].astype(F32) for k in range(3)])
        zp[side, 0:32, :] = u[z]
        zp[side, 32:64, :] = s[z]
        zp[side, 64:96, :] = c[side]
        zp[side, 96:128, :] = jnp.where(lane == 0, c[4], 0.0) + jnp.where(lane == NY - 1, c[5], 0.0)


def z_part(stage, faces, xp, xh):
    row, _ = plane()
    row8 = iota((8, NY), 0)
    all_lines = []
    for side, z in ((0, 0), (1, NZ - 1)):
        res = faces[side, 32:64, :]
        lines = jnp.zeros((8, NY), F32)
        for end, at in ((0, 0), (1, NX - 1)):
            line = xh[end, z : z + 1, :]
            res += jnp.where(row == at, xp[end, 64 + z : 65 + z, :] * line, 0.0)
            lines = jnp.where(row8 == end, line, lines)
        stage[side, 0:32, :] = faces[side, 0:32, :]
        stage[side, 32:64, :] = res
        all_lines.append(lines)
    return all_lines


def first_z_kernel(xodd, xeven, xp, zp, xh, even, odd, stage):
    take_in(xh, xeven, xodd, "gx")
    lines = z_part(stage, zp, xp, xh)
    for side in (0, 1):
        stage[side, 64:128, :] = zp[side, 64:128, :]
        stage[side, 128:136, :] = lines[side]
    put_out(stage, even, odd, "gz")


def y_part(field, res, coupling, zp, zh, xp, xh):
    row, lane = plane()
    row8 = iota((8, NY), 0)
    z_lines = [zh[end, 0:32, :] for end in (0, 1)]
    res += jnp.where(ends(lane), zp[0, 64:96, :] * z_lines[0], 0.0)
    last = 4 * (NZ - 1)
    res += jnp.where(layer_lanes(NZ - 1), pltpu.roll(zp[1, 64:96, :] * z_lines[1], last, 1), 0.0)
    x_lines = jnp.zeros((8, NY), F32)
    for end, at in ((0, 0), (1, NX - 1)):
        line = xh[end, 0:32, :]
        res += jnp.where(row == at, combined_row(xp[end, 64:96, :] * line), 0.0)
        x_lines = jnp.where(row8 == end, combined_row(line), x_lines)
    messages = []
    q = fourths()
    for side in (0, 1):
        body = jnp.where(q == 0, shift_lanes(field, side), shift_lanes(res, 1 + side))
        if coupling is not None:
            body = jnp.where(q == 2, shift_lanes(coupling, 2 + side), body)
        for end in (0, 1):
            at = 3 + 4 * end
            body = jnp.where(lane == at, shift_lanes(z_lines[end], at + side), body)
        messages.append((body, shift_lanes(x_lines, side)))
    return messages


def first_y_kernel(zeven, zodd, xp, zp, yp, xh, zh, even, odd, stage):
    take_in(zh, zeven, zodd, "gz")
    messages = y_part(yp[0:32, :], yp[32:64, :], yp[64:96, :], zp, zh, xp, xh)
    for side in (0, 1):
        stage[side, 0:32, :], stage[side, 32:40, :] = messages[side]
    put_out(stage, even, odd, "gy")


def z_halo_residual(side, res, zh1, yh, mine):
    _, lane = plane()
    at = 3 + 4 * side
    low, high = yh[0, 0:32, at : at + 1], yh[1, 0:32, at : at + 1]
    corner = jnp.where(lane == 0, low, 0.0) + jnp.where(lane == NY - 1, high, 0.0)
    return res + zh1[side, 64:96, :] * mine + zh1[side, 96:128, :] * corner


def x_halo_residual(side, res, xh1, zh, lines, yh, mine):
    row, _ = plane()
    total = res + xh1[side, 64:96, :] * mine
    for end, at in ((0, 0), (1, NZ - 1)):
        total += jnp.where(row == at, xh1[side, 96 + end : 97 + end, :] * zh[end, lines + side : lines + side + 1, :], 0.0)
    corner = combine(yh[0, 32 + side : 33 + side, :], yh[1, 32 + side : 33 + side, :], 0)
    return total + columns(xh1[side, 98:99, :] * corner)


def group_sums(x):
    return jnp.sum(x.reshape(4, 8, NY), axis=1)


def exact_dot(a, b):
    return jnp.dot(a, b, precision=lax.Precision.HIGHEST, preferred_element_type=F32)


def second_kernel(
    u, g, diag, s1, perm_sum, zp, yp, xp, xh, zh, yodd, yeven,
    yh, s, d, acc, b, xp2, even, odd,
    s0, d0, cross, cross2, rsum, rows, stage,
):
    take_in(yh, yeven, yodd, "gy")
    scale = 1.0 / THETA
    low, high = yh[0, 0:32, :], yh[1, 0:32, :]
    own_y = yp[64:96, :]
    yq = own_y * combine(low, high, 0)
    yq2 = own_y * (scale * (combine(low, high, 1) + combine(low, high, 2) * yp[0:32, :]))
    zq, zq2 = [], []
    for side, z in ((0, 0), (1, NZ - 1)):
        zq.append(zp[side, 64:96, :] * zh[side, 0:32, :])
        zq2.append(zp[side, 64:96, :] * (scale * z_halo_residual(side, zh[side, 32:64, :], zh, yh, u[z])))
        gx = xp[side, 64:96, :]
        cross[side] = gx * xh[side, 0:32, :]
        cross2[side] = gx * (scale * x_halo_residual(side, xh[side, 32:64, :], xh, zh, 128, yh, xp[side, 0:32, :]))
    rsum[...] = jnp.zeros_like(rsum)

    def start(z, carry):
        res = s1[z] + from_faces(z, zq, cross, yq)
        s0[z] = res
        d0[z] = res * scale
        rsum[z // 8] += res * diag[z]
        return carry

    lax.fori_loop(0, NZ, start, 0, unroll=8)
    for block in range(4):
        rows[0, 4 * block : 4 * block + 4, :] = group_sums(rsum[block])
        rows[1, 4 * block : 4 * block + 4, :] = group_sums(perm_sum[block])
    select = jnp.where(iota((NY, NY), 0) // 8 == iota((NY, NY), 1), 1.0, 0.0)
    lane16 = iota((16, NY), 1)
    weights = jnp.where(lane16 < 16, exact_dot(rows[1], select), 1.0)
    rhs = jnp.where(lane16 < 16, (OMEGA * 8.0 / 6.0) * exact_dot(rows[0], select) / weights, 0.0)
    b[...] = rhs

    def step(z, carry):
        before = d0[z]
        res = s0[z] - before + own_neighbours(d0, g, z) + from_faces(z, zq2, cross2, yq2)
        after = A[0] * before + B[0] * res
        s[z] = res
        d[z] = after
        acc[z] = u[z] + before + after
        return carry

    lax.fori_loop(0, NZ, step, 0, unroll=8)

    def face(z, carry):
        for side in (0, 1):
            at, r = face_rows(side)
            here = d[z, at, :]
            res = s[z, at, :] - here + inner_neighbours(d, [g[k, z, at, :] for k in range(6)], z, side)
            xp2[side, pl.ds(z, 1), :] = here[r : r + 1]
            xp2[side, pl.ds(NZ + z, 1), :] = res[r : r + 1]
        return carry

    lax.fori_loop(0, NZ, face, 0, unroll=8)
    for side in (0, 1):
        stage[side, 0:64, :] = xp2[side]
        for z in range(4):
            stage[side, 64 + 3 * z : 67 + 3 * z, :] = rhs[4 * z + side : 4 * z + side + 3]
        stage[side, 76:80, :] = jnp.zeros((4, NY), F32)
    put_out(stage, even, odd, "gx")


def second_block_kernel(g, s1, d, s, zp2, yp2):
    def partial(z, carry):
        pu, ps = carry
        here = d[z]
        res = s1[z] - here + own_neighbours(d, g, z)
        s[z] = res
        mine = layer_lanes(z)
        return jnp.where(mine, pltpu.roll(here, 4 * z, 1), pu), jnp.where(mine, pltpu.roll(res, 4 * z, 1), ps)

    zero = jnp.zeros((NX, NY), F32)
    pu, ps = lax.fori_loop(0, NZ, partial, (zero, zero), unroll=8)
    yp2[0:32, :] = pu
    yp2[32:64, :] = ps
    for side, z in ((0, 0), (1, NZ - 1)):
        zp2[side, 0:32, :] = d[z]
        zp2[side, 32:64, :] = s[z]


def second_z_kernel(xodd, xeven, xp, zp2, b, xh2, even, odd, b3, stage, rows):
    take_in(xh2, xeven, xodd, "gx")
    lines = z_part(stage, zp2, xp, xh2)
    lane16 = iota((16, NY), 1)
    wide = b[...]
    for end in (0, 1):
        first = 1 - end
        rows[...] = jnp.zeros_like(rows)
        for z in range(4):
            rows[4 * z + first : 4 * z + first + 3, :] = xh2[end, 64 + 3 * z : 67 + 3 * z, :]
        base = 32 * (end + 1)
        wide = jnp.where((lane16 >= base) & (lane16 < base + 16), pltpu.roll(rows[...], base, 1), wide)
    b3[...] = wide
    for side in (0, 1):
        stage[side, 64:72, :] = lines[side]
        stage[side, 72:88, :] = wide
    put_out(stage, even, odd, "gz")


def second_y_kernel(zeven, zodd, xp, zp, yp2, xh2, b3, zh2, even, odd, stage):
    take_in(zh2, zeven, zodd, "gz")
    messages = y_part(yp2[0:32, :], yp2[32:64, :], None, zp, zh2, xp, xh2)
    within = lax.rem(iota((16, NY), 1), 32)
    parts = (b3[...], zh2[0, 72:88, :], zh2[1, 72:88, :])
    for side in (0, 1):
        stage[side, 0:32, :], stage[side, 32:40, :] = messages[side]
        coarse = jnp.zeros((16, NY), F32)
        for k in range(3):
            at = 4 * k
            moved = shift_lanes(parts[k], at - 13 * side)
            coarse = jnp.where((within >= at) & (within < at + 3), moved, coarse)
        stage[side, 40:56, :] = coarse
    put_out(stage, even, odd, "gy")


def coarse_solve(b3, zh2, yh2, ext, err, spread):
    ext[...] = jnp.zeros_like(ext)
    lane4 = iota((4, NY), 1)
    within = lax.rem(iota((16, NY), 1), 32)
    wide = []
    for k, part in enumerate((b3[...], zh2[0, 72:88, :], zh2[1, 72:88, :])):
        full = jnp.where((within >= 3) & (within < 19), shift_lanes(part, 3), 0.0)
        full = jnp.where(within < 3, shift_lanes(yh2[0, 40:56, :], -4 * k), full)
        wide.append(jnp.where((within >= 19) & (within < 22), shift_lanes(yh2[1, 40:56, :], 19 - 4 * k), full))

    for z in range(10):
        values, at = (wide[1], 4 * (z + 1)) if z < 3 else (wide[0], 4 * (z - 3)) if z < 7 else (wide[2], 4 * (z - 7))
        four = values[at : at + 4]
        own, low, high = [jnp.where(lane4 < 22, shift_lanes(four, -32 * k), 0.0) for k in range(3)]
        ext[z, 0:3, :] = low[1:4]
        ext[z, 3:7, :] = own
        ext[z, 7:10, :] = high[0:3]
    x, y = iota((16, NY), 0), iota((16, NY), 1)
    at_z, at_x, at_y = lax.axis_index("gz"), lax.axis_index("gx"), lax.axis_index("gy")
    last_z, last_x, last_y = lax.axis_size("gz") - 1, lax.axis_size("gx") - 1, lax.axis_size("gy") - 1
    inside = (x < 10) & (y < 22)
    inside &= ((x >= 3) | (at_x > 0)) & ((x < 7) | (at_x < last_x))
    inside &= ((y >= 3) | (at_y > 0)) & ((y < 19) | (at_y < last_y))
    keep = jnp.where(inside, 1.0, 0.0)
    keep_low = jnp.where(at_z > 0, keep, 0.0)
    keep_high = jnp.where(at_z < last_z, keep, 0.0)
    rhs = [ext[z] for z in range(10)]
    e = rhs
    for sweep in range(3):
        lo, hi = sweep + 1, 9 - sweep
        new = []
        for z in range(10):
            if z < lo or z >= hi:
                new.append(e[z])
                continue
            c = e[z]
            beside = e[z - 1] + e[z + 1] + pltpu.roll(c, 1, 0) + pltpu.roll(c, 15, 0) + pltpu.roll(c, 1, 1) + pltpu.roll(c, NY - 1, 1)
            v = (1.0 - OMEGA) * c + (OMEGA / 6.0) * beside + rhs[z]
            new.append(v * (keep_low if z < 3 else keep_high if z >= 7 else keep))
        e = new
    for z in range(4):
        err[4 * z : 4 * z + 4, :] = e[z + 3][3:7]
    select = jnp.where(iota((NY, NY), 0) == iota((NY, NY), 1) // 8 + 3, 1.0, 0.0)
    fine = exact_dot(err[...], select)
    for z in range(4):
        spread[z] = jnp.broadcast_to(fine[4 * z : 4 * z + 4][:, None, :], (4, 8, NY)).reshape(NX, NY)


def third_kernel(
    g, s2, d1, acc, zp, yp, xp, xh, zh, yh, xp2, zp2, yp2, xh2, zh2, b3, yodd, yeven,
    out,
    yh2, s, d, cross, cross2, ext, err, spread,
):
    take_in(yh2, yeven, yodd, "gy")
    low, high = yh2[0, 0:32, :], yh2[1, 0:32, :]
    own_y = yp[64:96, :]
    yu = combine(low, high, 0)
    yq = own_y * yu
    yq2 = own_y * (A[1] * yu + B[1] * (combine(low, high, 1) + combine(yh[0, 0:32, :], yh[1, 0:32, :], 2) * yp2[0:32, :]))
    zq, zq2 = [], []
    for side, z in ((0, 0), (1, NZ - 1)):
        zu, xu = zh2[side, 0:32, :], xh2[side, 0:32, :]
        zq.append(zp[side, 64:96, :] * zu)
        dz = A[1] * zu + B[1] * z_halo_residual(side, zh2[side, 32:64, :], zh, yh2, zp2[side, 0:32, :])
        zq2.append(zp[side, 64:96, :] * dz)
        gx = xp[side, 64:96, :]
        cross[side] = gx * xu
        dx = A[1] * xu + B[1] * x_halo_residual(side, xh2[side, 32:64, :], xh, zh2, 64, yh2, xp2[side, 0:32, :])
        cross2[side] = gx * dx
    coarse_solve(b3, zh2, yh2, ext, err, spread)

    def step(z, carry):
        res = s2[z] + from_faces(z, zq, cross, yq)
        s[z] = res
        d[z] = A[1] * d1[z] + B[1] * res
        return carry

    lax.fori_loop(0, NZ, step, 0, unroll=8)

    def finish(z, carry):
        before = d[z]
        res = s[z] - before + own_neighbours(d, g, z) + from_faces(z, zq2, cross2, yq2)
        out[z] = acc[z] + before + (A[2] * before + B[2] * res) + spread[z // 8]
        return carry

    lax.fori_loop(0, NZ, finish, 0, unroll=8)


VM = pl.BlockSpec(memory_space=pltpu.VMEM)
HBM = pl.BlockSpec(memory_space=pltpu.HBM)
BF16_FIELD = jax.ShapeDtypeStruct((3,) + FULL, jnp.bfloat16)


def call(kernel, name, n_in, outs, scratch=(), us=0.2, place=VM, more=()):
    return pl.pallas_call(
        kernel,
        out_shape=[x if isinstance(x, jax.ShapeDtypeStruct) else jax.ShapeDtypeStruct(x, F32) for x in outs],
        in_specs=[place] * n_in,
        out_specs=[VM] * len(outs),
        scratch_shapes=[pltpu.VMEM(shape, F32) for shape in scratch] + list(more),
        compiler_params=pltpu.CompilerParams(vmem_limit_bytes=32 * 2**20),
        cost_estimate=pl.CostEstimate(flops=0, transcendentals=0, bytes_accessed=int(us * 3e6)),
        name=name,
    )


def swap(even, odd, axis):
    count = lax.axis_size(axis)
    results = []
    for first, values in ((1, odd), (0, even)):
        pairs = []
        for i in range(first, count - 1, 2):
            pairs += [(i, i + 1), (i + 1, i)]
        results.append(lax.ppermute(values, axis, pairs))
    return results[::-1]


def per_device(u, f, p, w):
    face = (2, 32, NY)
    far = [pltpu.with_memory_space_constraint(x, pltpu.HBM) for x in (u, f, p, w)]
    u, f, p, w, xp, even, odd = call(
        face_kernel, "x_faces", 4, [FULL, FULL, FULL, BF16_FIELD, (2, XM1, NY), (XM1, NY), (XM1, NY)], (), 2.0, HBM,
        [pltpu.SemaphoreType.DMA((4, 4))],
    )(*far)
    g, diag, s, perm_sum, zp, yp = call(
        block_kernel, "block", 4, [(6,) + FULL, FULL, FULL, (4, NX, NY), (2, 128, NY), (96, NY)], (), 2.5
    )(u, f, p, w)
    even, odd = swap(even, odd, "gx")
    xh, even, odd = call(first_z_kernel, "z_message", 4, [(2, XM1, NY), (ZM1, NY), (ZM1, NY)], [(2, ZM1, NY)])(odd, even, xp, zp)
    even, odd = swap(even, odd, "gz")
    zh, even, odd = call(
        first_y_kernel, "y_message", 6, [(2, ZM1, NY), (YM1, NY), (YM1, NY)], [(2, YM1, NY)]
    )(even, odd, xp, zp, yp, xh)
    even, odd = swap(even, odd, "gy")
    yh, s, d1, acc, b, xp2, even, odd = call(
        second_kernel, "two_steps", 12,
        [(2, YM1, NY), FULL, FULL, FULL, (16, NY), (2, 64, NY), (XM2, NY), (XM2, NY)],
        [FULL, FULL, face, face, (4, NX, NY), (2, 16, NY), (2, XM2, NY)], 2.0,
    )(u, g, diag, s, perm_sum, zp, yp, xp, xh, zh, odd, even)
    s, zp2, yp2 = call(
        second_block_kernel, "block_2", 3, [FULL, (2, 64, NY), (64, NY)], (), 1.5
    )(g, s, d1)
    even, odd = swap(even, odd, "gx")
    xh2, even, odd, b3 = call(
        second_z_kernel, "z_message_2", 5, [(2, XM2, NY), (ZM2, NY), (ZM2, NY), (16, NY)], [(2, ZM2, NY), (16, NY)]
    )(odd, even, xp, zp2, b)
    even, odd = swap(even, odd, "gz")
    zh2, even, odd = call(
        second_y_kernel, "y_message_2", 7, [(2, ZM2, NY), (YM2, NY), (YM2, NY)], [(2, YM2, NY)]
    )(even, odd, xp, zp, yp2, xh2, b3)
    even, odd = swap(even, odd, "gy")
    (out,) = call(
        third_kernel, "last_steps", 18, [FULL],
        [(2, YM2, NY), FULL, FULL, face, face, (10, 16, NY), (16, NY), (4, NX, NY)], 2.5,
    )(g, s, d1, acc, zp, yp, xp, xh, zh, yh, xp2, zp2, yp2, xh2, zh2, b3, odd, even)
    return out


def solution(mesh):
    placed = (
        P("gz", "gx", "gy"),
        P("gz", "gx", "gy"),
        P("gz", "gx", "gy"),
        P(None, "gz", "gx", "gy"),
    )
    return jax.shard_map(
        per_device, mesh=mesh, in_specs=placed, out_specs=P("gz", "gx", "gy"), check_vma=False
    )
```

```python
import jax
import jax.numpy as jnp
from jax import lax
from jax.experimental import pallas as pl
from jax.experimental.pallas import tpu as pltpu
from jax.sharding import PartitionSpec as P

THETA = 1.15
DELTA = 0.85
OMEGA = 0.8
F32 = jnp.float32

NZ, NX, NY = 32, 32, 128
FULL = (NZ, NX, NY)

SIGMA = THETA / DELTA
RHO0 = 1.0 / SIGMA
RHO1 = 1.0 / (2.0 * SIGMA - RHO0)
RHO2 = 1.0 / (2.0 * SIGMA - RHO1)
RHO3 = 1.0 / (2.0 * SIGMA - RHO2)
A = (RHO1 * RHO0, RHO2 * RHO1, RHO3 * RHO2)
B = (2.0 * RHO1 / DELTA, 2.0 * RHO2 / DELTA, 2.0 * RHO3 / DELTA)

XM1 = 104
ZM1 = 104
ZH1 = 136
YM1 = 40
XM2 = 80
ZM2 = 88
YM2 = 56


def iota(shape, dim):
    return lax.broadcasted_iota(jnp.int32, shape, dim)


def plane():
    return iota((NX, NY), 0), iota((NX, NY), 1)


def parity(axis):
    return lax.rem(lax.axis_index(axis), 2)


def put_out(stage, even, odd, axis):
    odd_one = parity(axis)
    even[...] = stage[1 - odd_one]
    odd[...] = stage[odd_one]


def take_in(halo, even, odd, axis):
    odd_one = parity(axis)
    halo[1 - odd_one] = even[...]
    halo[odd_one] = odd[...]


def fourths(shape=(NX, NY)):
    return lax.rem(iota(shape, 1), 4)


def layer_lanes(z, shape=(NX, NY)):
    lane = iota(shape, 1)
    return (lane == 4 * z) | (lane == lax.rem(4 * z + NY - 1, NY))


def ends(lane):
    return (lane == 0) | (lane == NY - 1)


def shift_lanes(x, amount):
    return pltpu.roll(x, amount % NY, 1)


def columns(row_values):
    row, lane = plane()
    wide = jnp.broadcast_to(row_values, (NX, NY))
    low = jnp.sum(jnp.where(lane == 4 * row, wide, 0.0), axis=1, keepdims=True)
    high = jnp.sum(jnp.where(lane == lax.rem(4 * row + NY - 1, NY), wide, 0.0), axis=1, keepdims=True)
    return jnp.where(lane == 0, low, 0.0) + jnp.where(lane == NY - 1, high, 0.0)


def combined_row(values):
    row, lane = plane()
    low = jnp.where(lane == 4 * row, jnp.broadcast_to(values[:, 0:1], (NX, NY)), 0.0)
    high = jnp.where(lane == lax.rem(4 * row + NY - 1, NY), jnp.broadcast_to(values[:, NY - 1 :], (NX, NY)), 0.0)
    return jnp.sum(low + high, axis=0, keepdims=True)


def combine(low, high, q):
    return jnp.where(fourths(low.shape) == 0, shift_lanes(low, -q), shift_lanes(high, -q - 1))


def own_neighbours(field, g, z):
    here = field[z]
    total = g[0, z] * field[jnp.maximum(z - 1, 0)] + g[1, z] * field[jnp.minimum(z + 1, NZ - 1)]
    total += g[2, z] * pltpu.roll(here, 1, 0) + g[3, z] * pltpu.roll(here, NX - 1, 0)
    total += g[4, z] * pltpu.roll(here, 1, 1) + g[5, z] * pltpu.roll(here, NY - 1, 1)
    return total


def from_faces(z, zp, xp, yp):
    row, lane = plane()
    total = jnp.where(ends(lane), pltpu.roll(yp, lax.rem(NY - 4 * z, NY), 1), 0.0)
    total += jnp.where(row == 0, xp[0, pl.ds(z, 1), :], 0.0)
    total += jnp.where(row == NX - 1, xp[1, pl.ds(z, 1), :], 0.0)
    total += jnp.where(z == 0, zp[0], 0.0) + jnp.where(z == NZ - 1, zp[1], 0.0)
    return total


def couplings(perm, speeds):
    total = 6.0 * perm + jnp.abs(speeds[0]) + jnp.abs(speeds[1]) + jnp.abs(speeds[2])
    inverse = 1.0 / total
    pairs = []
    for speed in speeds:
        pairs.append((perm + jnp.maximum(speed, 0.0)) * inverse)
        pairs.append((perm - jnp.minimum(speed, 0.0)) * inverse)
    return total, inverse, pairs


def face_rows(side):
    return (slice(0, 8), 0) if side == 0 else (slice(NX - 8, NX), 7)


def inner_neighbours(field, c, z, side):
    rows, _ = face_rows(side)
    lane = iota((8, NY), 1)
    here = field[z, rows, :]
    total = jnp.where(z == 0, 0.0, c[0]) * field[jnp.maximum(z - 1, 0), rows, :]
    total += jnp.where(z == NZ - 1, 0.0, c[1]) * field[jnp.minimum(z + 1, NZ - 1), rows, :]
    total += c[3 - side] * pltpu.roll(here, 7 if side == 0 else 1, 0)
    total += jnp.where(lane == 0, 0.0, c[4]) * pltpu.roll(here, 1, 1)
    total += jnp.where(lane == NY - 1, 0.0, c[5]) * pltpu.roll(here, NY - 1, 1)
    return total


def face_kernel(u_far, f_far, p_far, w_far, u, f, p, w, xp, even, odd, zeven, zodd, sems):
    lane8 = iota((8, NY), 1)
    copies = []
    for part in range(4):
        rows = pl.ds(8 * part, 8)
        copies.append([
            pltpu.make_async_copy(u_far.at[rows], u.at[rows], sems.at[part, 0]),
            pltpu.make_async_copy(f_far.at[rows], f.at[rows], sems.at[part, 1]),
            pltpu.make_async_copy(p_far.at[rows], p.at[rows], sems.at[part, 2]),
            pltpu.make_async_copy(w_far.at[:, rows], w.at[:, rows], sems.at[part, 3]),
        ])
    for part in range(4):
        copies[part][0].start()
    for part in range(4):
        for copy in copies[part][1:]:
            copy.start()

    def face(z, side):
        rows, _ = face_rows(side)
        half = slice(0, 16) if side == 0 else slice(NX - 16, NX)
        speeds = [w[k, z, half, :].astype(F32)[8 * side : 8 * side + 8] for k in range(3)]
        return couplings(p[z, rows, :], speeds)

    def layer(z, carry):
        edges = []
        for side in (0, 1):
            rows, r = face_rows(side)
            _, inverse, c = face(z, side)
            here = u[z, rows, :]
            res = f[z, rows, :] * inverse - here + inner_neighbours(u, c, z, side)
            for base, values in ((0, here), (NZ, res), (2 * NZ, c[2 + side])):
                xp[side, pl.ds(base + z, 1), :] = values[r : r + 1]
            merged = pltpu.roll(jnp.where(lane8 == 0, c[4], c[5]), 4 * z, 1)
            edges.append(jnp.where(layer_lanes(z, (8, NY)), merged, carry[side]))
        return tuple(edges)

    edges = (jnp.zeros((8, NY), F32),) * 2
    for part in range(4):
        copies[part][0].wait()
    for part in range(4):
        for copy in copies[part][1:]:
            copy.wait()
        edges = lax.fori_loop(8 * part, 8 * part + 8, layer, edges, unroll=4)
    for side in (0, 1):
        _, r = face_rows(side)
        xp[side, 96:104, :] = jnp.zeros((8, NY), F32)
        for end, z in ((0, 0), (1, NZ - 1)):
            _, _, c = face(z, side)
            xp[side, 96 + end : 97 + end, :] = c[end][r : r + 1]
        xp[side, 98:99, :] = edges[side][r : r + 1]
    put_out(xp, even, odd, "gx")
    odd_one = parity("gz")
    zeven[...] = u[(1 - odd_one) * (NZ - 1)]
    zodd[...] = u[odd_one * (NZ - 1)]


def block_kernel(u, f, p, w, g, diag, s, perm_sum, zp, yp):
    row, lane = plane()
    perm_sum[...] = jnp.zeros_like(perm_sum)

    def layer(z, carry):
        pu, ps, pg = carry
        perm = p[z]
        total, inverse, c = couplings(perm, [w[k, z].astype(F32) for k in range(3)])
        g[0, z] = jnp.where(z == 0, 0.0, c[0])
        g[1, z] = jnp.where(z == NZ - 1, 0.0, c[1])
        g[2, z] = jnp.where(row == 0, 0.0, c[2])
        g[3, z] = jnp.where(row == NX - 1, 0.0, c[3])
        g[4, z] = jnp.where(lane == 0, 0.0, c[4])
        g[5, z] = jnp.where(lane == NY - 1, 0.0, c[5])
        diag[z] = total
        here = u[z]
        res = f[z] * inverse - here + own_neighbours(u, g, z)
        s[z] = res
        perm_sum[z // 8] += perm
        mine = layer_lanes(z)
        pu = jnp.where(mine, pltpu.roll(here, 4 * z, 1), pu)
        ps = jnp.where(mine, pltpu.roll(res, 4 * z, 1), ps)
        pg = jnp.where(mine, pltpu.roll(jnp.where(lane == 0, c[4], c[5]), 4 * z, 1), pg)
        return pu, ps, pg

    zero = jnp.zeros((NX, NY), F32)
    pu, ps, pg = lax.fori_loop(0, NZ, layer, (zero, zero, zero), unroll=4)
    yp[0:32, :] = pu
    yp[32:64, :] = ps
    yp[64:96, :] = pg
    for side, z in ((0, 0), (1, NZ - 1)):
        _, _, c = couplings(p[z], [w[k, z].astype(F32) for k in range(3)])
        zp[side, 0:32, :] = u[z]
        zp[side, 32:64, :] = s[z]
        zp[side, 64:96, :] = c[side]
        zp[side, 96:128, :] = jnp.where(lane == 0, c[4], 0.0) + jnp.where(lane == NY - 1, c[5], 0.0)


def z_part(stage, faces, xp, xh):
    row, _ = plane()
    row8 = iota((8, NY), 0)
    all_lines = []
    for side, z in ((0, 0), (1, NZ - 1)):
        res = faces[side, 32:64, :]
        lines = jnp.zeros((8, NY), F32)
        for end, at in ((0, 0), (1, NX - 1)):
            line = xh[end, z : z + 1, :]
            res += jnp.where(row == at, xp[end, 64 + z : 65 + z, :] * line, 0.0)
            lines = jnp.where(row8 == end, line, lines)
        stage[side, 0:32, :] = faces[side, 0:32, :]
        stage[side, 32:64, :] = res
        all_lines.append(lines)
    return all_lines


def y_part(field, res, coupling, zp, zh, xp, xh):
    row, lane = plane()
    row8 = iota((8, NY), 0)
    z_lines = [zh[end, 0:32, :] for end in (0, 1)]
    res += jnp.where(ends(lane), zp[0, 64:96, :] * z_lines[0], 0.0)
    last = 4 * (NZ - 1)
    res += jnp.where(layer_lanes(NZ - 1), pltpu.roll(zp[1, 64:96, :] * z_lines[1], last, 1), 0.0)
    x_lines = jnp.zeros((8, NY), F32)
    for end, at in ((0, 0), (1, NX - 1)):
        line = xh[end, 0:32, :]
        res += jnp.where(row == at, combined_row(xp[end, 64:96, :] * line), 0.0)
        x_lines = jnp.where(row8 == end, combined_row(line), x_lines)
    messages = []
    q = fourths()
    for side in (0, 1):
        body = jnp.where(q == 0, shift_lanes(field, side), shift_lanes(res, 1 + side))
        if coupling is not None:
            body = jnp.where(q == 2, shift_lanes(coupling, 2 + side), body)
        for end in (0, 1):
            at = 3 + 4 * end
            body = jnp.where(lane == at, shift_lanes(z_lines[end], at + side), body)
        messages.append((body, shift_lanes(x_lines, side)))
    return messages


def first_message_kernel(
    xodd, xeven, zeven, zodd, xp, zp, yp,
    xh, zu, z_to_even, z_to_odd, y_to_even, y_to_odd,
    z_stage, z_rows, y_stage,
):
    take_in(xh, xeven, xodd, "gx")
    take_in(zu, zeven, zodd, "gz")
    lines = z_part(z_stage, zp, xp, xh)
    for side in (0, 1):
        z_rows[side, 0:32, :] = z_stage[side, 32:64, :]
        z_rows[side, 32:96, :] = zp[side, 64:128, :]
        z_rows[side, 96:104, :] = lines[side]
    put_out(z_rows, z_to_even, z_to_odd, "gz")
    messages = y_part(yp[0:32, :], yp[32:64, :], yp[64:96, :], zp, zu, xp, xh)
    for side in (0, 1):
        y_stage[side, 0:32, :], y_stage[side, 32:40, :] = messages[side]
    put_out(y_stage, y_to_even, y_to_odd, "gy")


def z_halo_residual(side, res, zh1, yh, mine):
    _, lane = plane()
    at = 3 + 4 * side
    low, high = yh[0, 0:32, at : at + 1], yh[1, 0:32, at : at + 1]
    corner = jnp.where(lane == 0, low, 0.0) + jnp.where(lane == NY - 1, high, 0.0)
    return res + zh1[side, 64:96, :] * mine + zh1[side, 96:128, :] * corner


def x_halo_residual(side, res, xh1, zh, lines, yh, mine):
    row, _ = plane()
    total = res + xh1[side, 64:96, :] * mine
    for end, at in ((0, 0), (1, NZ - 1)):
        total += jnp.where(row == at, xh1[side, 96 + end : 97 + end, :] * zh[end, lines + side : lines + side + 1, :], 0.0)
    corner = combine(yh[0, 32 + side : 33 + side, :], yh[1, 32 + side : 33 + side, :], 0)
    return total + columns(xh1[side, 98:99, :] * corner)


def group_sums(x):
    return jnp.sum(x.reshape(4, 8, NY), axis=1)


def exact_dot(a, b):
    return jnp.dot(a, b, precision=lax.Precision.HIGHEST, preferred_element_type=F32)


def second_kernel(
    u, g, diag, s1, perm_sum, zp, yp, xp, xh, zu, yodd, zeven, zodd, yeven,
    zh, yh, s, d, acc, b, xp2, even, odd,
    zin, s0, d0, cross, cross2, rsum, rows, stage,
):
    take_in(yh, yeven, yodd, "gy")
    take_in(zin, zeven, zodd, "gz")
    for side in (0, 1):
        zh[side, 0:32, :] = zu[side]
        zh[side, 32:ZH1, :] = zin[side]
    scale = 1.0 / THETA
    low, high = yh[0, 0:32, :], yh[1, 0:32, :]
    own_y = yp[64:96, :]
    yq = own_y * combine(low, high, 0)
    yq2 = own_y * (scale * (combine(low, high, 1) + combine(low, high, 2) * yp[0:32, :]))
    zq, zq2 = [], []
    for side, z in ((0, 0), (1, NZ - 1)):
        zq.append(zp[side, 64:96, :] * zh[side, 0:32, :])
        zq2.append(zp[side, 64:96, :] * (scale * z_halo_residual(side, zh[side, 32:64, :], zh, yh, u[z])))
        gx = xp[side, 64:96, :]
        cross[side] = gx * xh[side, 0:32, :]
        cross2[side] = gx * (scale * x_halo_residual(side, xh[side, 32:64, :], xh, zh, 128, yh, xp[side, 0:32, :]))
    rsum[...] = jnp.zeros_like(rsum)

    def start(z, carry):
        res = s1[z] + from_faces(z, zq, cross, yq)
        s0[z] = res
        d0[z] = res * scale
        rsum[z // 8] += res * diag[z]
        return carry

    lax.fori_loop(0, NZ, start, 0, unroll=8)
    for block in range(4):
        rows[0, 4 * block : 4 * block + 4, :] = group_sums(rsum[block])
        rows[1, 4 * block : 4 * block + 4, :] = group_sums(perm_sum[block])
    select = jnp.where(iota((NY, NY), 0) // 8 == iota((NY, NY), 1), 1.0, 0.0)
    lane16 = iota((16, NY), 1)
    weights = jnp.where(lane16 < 16, exact_dot(rows[1], select), 1.0)
    rhs = jnp.where(lane16 < 16, (OMEGA * 8.0 / 6.0) * exact_dot(rows[0], select) / weights, 0.0)
    b[...] = rhs

    def step(z, carry):
        before = d0[z]
        res = s0[z] - before + own_neighbours(d0, g, z) + from_faces(z, zq2, cross2, yq2)
        after = A[0] * before + B[0] * res
        s[z] = res
        d[z] = after
        acc[z] = u[z] + before + after
        return carry

    lax.fori_loop(0, NZ, step, 0, unroll=8)

    def face(z, carry):
        for side in (0, 1):
            at, r = face_rows(side)
            here = d[z, at, :]
            res = s[z, at, :] - here + inner_neighbours(d, [g[k, z, at, :] for k in range(6)], z, side)
            xp2[side, pl.ds(z, 1), :] = here[r : r + 1]
            xp2[side, pl.ds(NZ + z, 1), :] = res[r : r + 1]
        return carry

    lax.fori_loop(0, NZ, face, 0, unroll=8)
    for side in (0, 1):
        stage[side, 0:64, :] = xp2[side]
        for z in range(4):
            stage[side, 64 + 3 * z : 67 + 3 * z, :] = rhs[4 * z + side : 4 * z + side + 3]
        stage[side, 76:80, :] = jnp.zeros((4, NY), F32)
    put_out(stage, even, odd, "gx")


def second_block_kernel(g, s1, d, s, zp2, yp2):
    def partial(z, carry):
        pu, ps = carry
        here = d[z]
        res = s1[z] - here + own_neighbours(d, g, z)
        s[z] = res
        mine = layer_lanes(z)
        return jnp.where(mine, pltpu.roll(here, 4 * z, 1), pu), jnp.where(mine, pltpu.roll(res, 4 * z, 1), ps)

    zero = jnp.zeros((NX, NY), F32)
    pu, ps = lax.fori_loop(0, NZ, partial, (zero, zero), unroll=8)
    yp2[0:32, :] = pu
    yp2[32:64, :] = ps
    for side, z in ((0, 0), (1, NZ - 1)):
        zp2[side, 0:32, :] = d[z]
        zp2[side, 32:64, :] = s[z]


def second_z_kernel(xodd, xeven, xp, zp2, b, xh2, even, odd, b3, stage, rows):
    take_in(xh2, xeven, xodd, "gx")
    lines = z_part(stage, zp2, xp, xh2)
    lane16 = iota((16, NY), 1)
    wide = b[...]
    for end in (0, 1):
        first = 1 - end
        rows[...] = jnp.zeros_like(rows)
        for z in range(4):
            rows[4 * z + first : 4 * z + first + 3, :] = xh2[end, 64 + 3 * z : 67 + 3 * z, :]
        base = 32 * (end + 1)
        wide = jnp.where((lane16 >= base) & (lane16 < base + 16), pltpu.roll(rows[...], base, 1), wide)
    b3[...] = wide
    for side in (0, 1):
        stage[side, 64:72, :] = lines[side]
        stage[side, 72:88, :] = wide
    put_out(stage, even, odd, "gz")


def second_y_kernel(zeven, zodd, xp, zp, yp2, xh2, b3, zh2, even, odd, stage):
    take_in(zh2, zeven, zodd, "gz")
    messages = y_part(yp2[0:32, :], yp2[32:64, :], None, zp, zh2, xp, xh2)
    within = lax.rem(iota((16, NY), 1), 32)
    parts = (b3[...], zh2[0, 72:88, :], zh2[1, 72:88, :])
    for side in (0, 1):
        stage[side, 0:32, :], stage[side, 32:40, :] = messages[side]
        coarse = jnp.zeros((16, NY), F32)
        for k in range(3):
            at = 4 * k
            moved = shift_lanes(parts[k], at - 13 * side)
            coarse = jnp.where((within >= at) & (within < at + 3), moved, coarse)
        stage[side, 40:56, :] = coarse
    put_out(stage, even, odd, "gy")


def coarse_solve(b3, zh2, yh2, ext, err, spread):
    ext[...] = jnp.zeros_like(ext)
    lane4 = iota((4, NY), 1)
    within = lax.rem(iota((16, NY), 1), 32)
    wide = []
    for k, part in enumerate((b3[...], zh2[0, 72:88, :], zh2[1, 72:88, :])):
        full = jnp.where((within >= 3) & (within < 19), shift_lanes(part, 3), 0.0)
        full = jnp.where(within < 3, shift_lanes(yh2[0, 40:56, :], -4 * k), full)
        wide.append(jnp.where((within >= 19) & (within < 22), shift_lanes(yh2[1, 40:56, :], 19 - 4 * k), full))

    for z in range(10):
        values, at = (wide[1], 4 * (z + 1)) if z < 3 else (wide[0], 4 * (z - 3)) if z < 7 else (wide[2], 4 * (z - 7))
        four = values[at : at + 4]
        own, low, high = [jnp.where(lane4 < 22, shift_lanes(four, -32 * k), 0.0) for k in range(3)]
        ext[z, 0:3, :] = low[1:4]
        ext[z, 3:7, :] = own
        ext[z, 7:10, :] = high[0:3]
    x, y = iota((16, NY), 0), iota((16, NY), 1)
    at_z, at_x, at_y = lax.axis_index("gz"), lax.axis_index("gx"), lax.axis_index("gy")
    last_z, last_x, last_y = lax.axis_size("gz") - 1, lax.axis_size("gx") - 1, lax.axis_size("gy") - 1
    inside = (x < 10) & (y < 22)
    inside &= ((x >= 3) | (at_x > 0)) & ((x < 7) | (at_x < last_x))
    inside &= ((y >= 3) | (at_y > 0)) & ((y < 19) | (at_y < last_y))
    keep = jnp.where(inside, 1.0, 0.0)
    keep_low = jnp.where(at_z > 0, keep, 0.0)
    keep_high = jnp.where(at_z < last_z, keep, 0.0)
    rhs = [ext[z] for z in range(10)]
    e = rhs
    for sweep in range(3):
        lo, hi = sweep + 1, 9 - sweep
        new = []
        for z in range(10):
            if z < lo or z >= hi:
                new.append(e[z])
                continue
            c = e[z]
            beside = e[z - 1] + e[z + 1] + pltpu.roll(c, 1, 0) + pltpu.roll(c, 15, 0) + pltpu.roll(c, 1, 1) + pltpu.roll(c, NY - 1, 1)
            v = (1.0 - OMEGA) * c + (OMEGA / 6.0) * beside + rhs[z]
            new.append(v * (keep_low if z < 3 else keep_high if z >= 7 else keep))
        e = new
    for z in range(4):
        err[4 * z : 4 * z + 4, :] = e[z + 3][3:7]
    select = jnp.where(iota((NY, NY), 0) == iota((NY, NY), 1) // 8 + 3, 1.0, 0.0)
    fine = exact_dot(err[...], select)
    for z in range(4):
        spread[z] = jnp.broadcast_to(fine[4 * z : 4 * z + 4][:, None, :], (4, 8, NY)).reshape(NX, NY)


def third_kernel(
    g, s2, d1, acc, zp, yp, xp, xh, zh, yh, xp2, zp2, yp2, xh2, zh2, b3, yodd, yeven,
    out,
    yh2, s, d, cross, cross2, ext, err, spread,
):
    take_in(yh2, yeven, yodd, "gy")
    low, high = yh2[0, 0:32, :], yh2[1, 0:32, :]
    own_y = yp[64:96, :]
    yu = combine(low, high, 0)
    yq = own_y * yu
    yq2 = own_y * (A[1] * yu + B[1] * (combine(low, high, 1) + combine(yh[0, 0:32, :], yh[1, 0:32, :], 2) * yp2[0:32, :]))
    zq, zq2 = [], []
    for side, z in ((0, 0), (1, NZ - 1)):
        zu, xu = zh2[side, 0:32, :], xh2[side, 0:32, :]
        zq.append(zp[side, 64:96, :] * zu)
        dz = A[1] * zu + B[1] * z_halo_residual(side, zh2[side, 32:64, :], zh, yh2, zp2[side, 0:32, :])
        zq2.append(zp[side, 64:96, :] * dz)
        gx = xp[side, 64:96, :]
        cross[side] = gx * xu
        dx = A[1] * xu + B[1] * x_halo_residual(side, xh2[side, 32:64, :], xh, zh2, 64, yh2, xp2[side, 0:32, :])
        cross2[side] = gx * dx
    coarse_solve(b3, zh2, yh2, ext, err, spread)

    def step(z, carry):
        res = s2[z] + from_faces(z, zq, cross, yq)
        s[z] = res
        d[z] = A[1] * d1[z] + B[1] * res
        return carry

    lax.fori_loop(0, NZ, step, 0, unroll=8)

    def finish(z, carry):
        before = d[z]
        res = s[z] - before + own_neighbours(d, g, z) + from_faces(z, zq2, cross2, yq2)
        out[z] = acc[z] + before + (A[2] * before + B[2] * res) + spread[z // 8]
        return carry

    lax.fori_loop(0, NZ, finish, 0, unroll=8)


VM = pl.BlockSpec(memory_space=pltpu.VMEM)
HBM = pl.BlockSpec(memory_space=pltpu.HBM)
BF16_FIELD = jax.ShapeDtypeStruct((3,) + FULL, jnp.bfloat16)


def call(kernel, name, n_in, outs, scratch=(), us=0.2, place=VM, more=()):
    return pl.pallas_call(
        kernel,
        out_shape=[x if isinstance(x, jax.ShapeDtypeStruct) else jax.ShapeDtypeStruct(x, F32) for x in outs],
        in_specs=[place] * n_in,
        out_specs=[VM] * len(outs),
        scratch_shapes=[pltpu.VMEM(shape, F32) for shape in scratch] + list(more),
        compiler_params=pltpu.CompilerParams(vmem_limit_bytes=32 * 2**20),
        cost_estimate=pl.CostEstimate(flops=0, transcendentals=0, bytes_accessed=int(us * 3e6)),
        name=name,
    )


def swap(even, odd, axis):
    count = lax.axis_size(axis)
    results = []
    for first, values in ((1, odd), (0, even)):
        pairs = []
        for i in range(first, count - 1, 2):
            pairs += [(i, i + 1), (i + 1, i)]
        results.append(lax.ppermute(values, axis, pairs))
    return results[::-1]


def per_device(u, f, p, w):
    face = (2, 32, NY)
    far = [pltpu.with_memory_space_constraint(x, pltpu.HBM) for x in (u, f, p, w)]
    u, f, p, w, xp, even, odd, zeven, zodd = call(
        face_kernel, "x_faces", 4,
        [FULL, FULL, FULL, BF16_FIELD, (2, XM1, NY), (XM1, NY), (XM1, NY), (NX, NY), (NX, NY)], (), 2.0, HBM,
        [pltpu.SemaphoreType.DMA((4, 4))],
    )(*far)
    g, diag, s, perm_sum, zp, yp = call(
        block_kernel, "block", 4, [(6,) + FULL, FULL, FULL, (4, NX, NY), (2, 128, NY), (96, NY)], (), 2.5
    )(u, f, p, w)
    even, odd = swap(even, odd, "gx")
    zeven, zodd = swap(zeven, zodd, "gz")
    xh, zu, zeven, zodd, yeven, yodd = call(
        first_message_kernel, "zy_message", 7,
        [(2, XM1, NY), (2, NX, NY), (ZM1, NY), (ZM1, NY), (YM1, NY), (YM1, NY)],
        [(2, 64, NY), (2, ZM1, NY), (2, YM1, NY)],
    )(odd, even, zeven, zodd, xp, zp, yp)
    zeven, zodd = swap(zeven, zodd, "gz")
    yeven, yodd = swap(yeven, yodd, "gy")
    zh, yh, s, d1, acc, b, xp2, even, odd = call(
        second_kernel, "two_steps", 14,
        [(2, ZH1, NY), (2, YM1, NY), FULL, FULL, FULL, (16, NY), (2, 64, NY), (XM2, NY), (XM2, NY)],
        [(2, ZM1, NY), FULL, FULL, face, face, (4, NX, NY), (2, 16, NY), (2, XM2, NY)], 2.0,
    )(u, g, diag, s, perm_sum, zp, yp, xp, xh, zu, yodd, zeven, zodd, yeven)
    s, zp2, yp2 = call(
        second_block_kernel, "block_2", 3, [FULL, (2, 64, NY), (64, NY)], (), 1.5
    )(g, s, d1)
    even, odd = swap(even, odd, "gx")
    xh2, even, odd, b3 = call(
        second_z_kernel, "z_message_2", 5, [(2, XM2, NY), (ZM2, NY), (ZM2, NY), (16, NY)], [(2, ZM2, NY), (16, NY)]
    )(odd, even, xp, zp2, b)
    even, odd = swap(even, odd, "gz")
    zh2, even, odd = call(
        second_y_kernel, "y_message_2", 7, [(2, ZM2, NY), (YM2, NY), (YM2, NY)], [(2, YM2, NY)]
    )(even, odd, xp, zp, yp2, xh2, b3)
    even, odd = swap(even, odd, "gy")
    (out,) = call(
        third_kernel, "last_steps", 18, [FULL],
        [(2, YM2, NY), FULL, FULL, face, face, (10, 16, NY), (16, NY), (4, NX, NY)], 2.5,
    )(g, s, d1, acc, zp, yp, xp, xh, zh, yh, xp2, zp2, yp2, xh2, zh2, b3, odd, even)
    return out


def solution(mesh):
    placed = (
        P("gz", "gx", "gy"),
        P("gz", "gx", "gy"),
        P("gz", "gx", "gy"),
        P(None, "gz", "gx", "gy"),
    )
    return jax.shard_map(
        per_device, mesh=mesh, in_specs=placed, out_specs=P("gz", "gx", "gy"), check_vma=False
    )
```

```python
import jax
import jax.numpy as jnp
from jax import lax
from jax.experimental import pallas as pl
from jax.experimental.pallas import tpu as pltpu
from jax.sharding import PartitionSpec as P

THETA = 1.15
DELTA = 0.85
OMEGA = 0.8
F32 = jnp.float32

NZ, NX, NY = 32, 32, 128
FULL = (NZ, NX, NY)

SIGMA = THETA / DELTA
RHO0 = 1.0 / SIGMA
RHO1 = 1.0 / (2.0 * SIGMA - RHO0)
RHO2 = 1.0 / (2.0 * SIGMA - RHO1)
RHO3 = 1.0 / (2.0 * SIGMA - RHO2)
A = (RHO1 * RHO0, RHO2 * RHO1, RHO3 * RHO2)
B = (2.0 * RHO1 / DELTA, 2.0 * RHO2 / DELTA, 2.0 * RHO3 / DELTA)

XM1 = 104
ZM1 = 104
ZH1 = 136
YM1 = 40
XM2 = 80
ZM2 = 88
YM2 = 56


def iota(shape, dim):
    return lax.broadcasted_iota(jnp.int32, shape, dim)


def plane():
    return iota((NX, NY), 0), iota((NX, NY), 1)


def parity(axis):
    return lax.rem(lax.axis_index(axis), 2)


def put_out(stage, even, odd, axis):
    odd_one = parity(axis)
    even[...] = stage[1 - odd_one]
    odd[...] = stage[odd_one]


def take_in(halo, even, odd, axis):
    odd_one = parity(axis)
    halo[1 - odd_one] = even[...]
    halo[odd_one] = odd[...]


def fourths(shape=(NX, NY)):
    return lax.rem(iota(shape, 1), 4)


def layer_lanes(z, shape=(NX, NY)):
    lane = iota(shape, 1)
    return (lane == 4 * z) | (lane == lax.rem(4 * z + NY - 1, NY))


def ends(lane):
    return (lane == 0) | (lane == NY - 1)


def shift_lanes(x, amount):
    return pltpu.roll(x, amount % NY, 1)


def columns(row_values):
    row, lane = plane()
    wide = jnp.broadcast_to(row_values, (NX, NY))
    low = jnp.sum(jnp.where(lane == 4 * row, wide, 0.0), axis=1, keepdims=True)
    high = jnp.sum(jnp.where(lane == lax.rem(4 * row + NY - 1, NY), wide, 0.0), axis=1, keepdims=True)
    return jnp.where(lane == 0, low, 0.0) + jnp.where(lane == NY - 1, high, 0.0)


def combined_row(values):
    row, lane = plane()
    low = jnp.where(lane == 4 * row, jnp.broadcast_to(values[:, 0:1], (NX, NY)), 0.0)
    high = jnp.where(lane == lax.rem(4 * row + NY - 1, NY), jnp.broadcast_to(values[:, NY - 1 :], (NX, NY)), 0.0)
    return jnp.sum(low + high, axis=0, keepdims=True)


def combine(low, high, q):
    return jnp.where(fourths(low.shape) == 0, shift_lanes(low, -q), shift_lanes(high, -q - 1))


def own_neighbours(field, g, z):
    here = field[z]
    total = g[0, z] * field[jnp.maximum(z - 1, 0)] + g[1, z] * field[jnp.minimum(z + 1, NZ - 1)]
    total += g[2, z] * pltpu.roll(here, 1, 0) + g[3, z] * pltpu.roll(here, NX - 1, 0)
    total += g[4, z] * pltpu.roll(here, 1, 1) + g[5, z] * pltpu.roll(here, NY - 1, 1)
    return total


def from_faces(z, xp, yp):
    row8 = iota((8, NY), 0)
    total = jnp.where(ends(iota((NX, NY), 1)), pltpu.roll(yp, lax.rem(NY - 4 * z, NY), 1), 0.0)
    first = total[0:8] + jnp.where(row8 == 0, xp[0, pl.ds(z, 1), :], 0.0)
    last = total[NX - 8 :] + jnp.where(row8 == 7, xp[1, pl.ds(z, 1), :], 0.0)
    return jnp.concatenate([first, total[8 : NX - 8], last], axis=0)


def from_faces_rows(z, xp, yp, side):
    rows, r = face_rows(side)
    total = jnp.where(ends(iota((8, NY), 1)), pltpu.roll(yp[rows], lax.rem(NY - 4 * z, NY), 1), 0.0)
    return total + jnp.where(iota((8, NY), 0) == r, xp[side, pl.ds(z, 1), :], 0.0)


def couplings(perm, speeds):
    total = 6.0 * perm + jnp.abs(speeds[0]) + jnp.abs(speeds[1]) + jnp.abs(speeds[2])
    inverse = 1.0 / total
    pairs = []
    for speed in speeds:
        pairs.append((perm + jnp.maximum(speed, 0.0)) * inverse)
        pairs.append((perm - jnp.minimum(speed, 0.0)) * inverse)
    return total, inverse, pairs


def face_rows(side):
    return (slice(0, 8), 0) if side == 0 else (slice(NX - 8, NX), 7)


def inner_neighbours(field, c, z, side):
    rows, _ = face_rows(side)
    lane = iota((8, NY), 1)
    here = field[z, rows, :]
    total = jnp.where(z == 0, 0.0, c[0]) * field[jnp.maximum(z - 1, 0), rows, :]
    total += jnp.where(z == NZ - 1, 0.0, c[1]) * field[jnp.minimum(z + 1, NZ - 1), rows, :]
    total += c[3 - side] * pltpu.roll(here, 7 if side == 0 else 1, 0)
    total += jnp.where(lane == 0, 0.0, c[4]) * pltpu.roll(here, 1, 1)
    total += jnp.where(lane == NY - 1, 0.0, c[5]) * pltpu.roll(here, NY - 1, 1)
    return total


def face_kernel(u_far, f_far, p_far, w_far, u, f, p, w, xp, even, odd, zeven, zodd, sems):
    lane8 = iota((8, NY), 1)
    copies = []
    for part in range(4):
        rows = pl.ds(8 * part, 8)
        copies.append([
            pltpu.make_async_copy(u_far.at[rows], u.at[rows], sems.at[part, 0]),
            pltpu.make_async_copy(f_far.at[rows], f.at[rows], sems.at[part, 1]),
            pltpu.make_async_copy(p_far.at[rows], p.at[rows], sems.at[part, 2]),
            pltpu.make_async_copy(w_far.at[:, rows], w.at[:, rows], sems.at[part, 3]),
        ])
    for part in range(4):
        copies[part][0].start()
    for part in range(4):
        for copy in copies[part][1:]:
            copy.start()

    def face(z, side):
        rows, _ = face_rows(side)
        half = slice(0, 16) if side == 0 else slice(NX - 16, NX)
        speeds = [w[k, z, half, :].astype(F32)[8 * side : 8 * side + 8] for k in range(3)]
        return couplings(p[z, rows, :], speeds)

    def layer(z, carry):
        edges = []
        for side in (0, 1):
            rows, r = face_rows(side)
            _, inverse, c = face(z, side)
            here = u[z, rows, :]
            res = f[z, rows, :] * inverse - here + inner_neighbours(u, c, z, side)
            for base, values in ((0, here), (NZ, res), (2 * NZ, c[2 + side])):
                xp[side, pl.ds(base + z, 1), :] = values[r : r + 1]
            merged = pltpu.roll(jnp.where(lane8 == 0, c[4], c[5]), 4 * z, 1)
            edges.append(jnp.where(layer_lanes(z, (8, NY)), merged, carry[side]))
        return tuple(edges)

    edges = (jnp.zeros((8, NY), F32),) * 2
    for part in range(4):
        copies[part][0].wait()
    for part in range(4):
        for copy in copies[part][1:]:
            copy.wait()
        edges = lax.fori_loop(8 * part, 8 * part + 8, layer, edges, unroll=8)
    for side in (0, 1):
        _, r = face_rows(side)
        xp[side, 96:104, :] = jnp.zeros((8, NY), F32)
        for end, z in ((0, 0), (1, NZ - 1)):
            _, _, c = face(z, side)
            xp[side, 96 + end : 97 + end, :] = c[end][r : r + 1]
        xp[side, 98:99, :] = edges[side][r : r + 1]
    put_out(xp, even, odd, "gx")
    odd_one = parity("gz")
    zeven[...] = u[(1 - odd_one) * (NZ - 1)]
    zodd[...] = u[odd_one * (NZ - 1)]


def block_kernel(u, f, p, w, g, diag, s, perm_sum, zp, yp):
    row, lane = plane()
    perm_sum[...] = jnp.zeros_like(perm_sum)

    def layer(z, carry):
        pu, ps, pg = carry
        perm = p[z]
        total, inverse, c = couplings(perm, [w[k, z].astype(F32) for k in range(3)])
        g[0, z] = jnp.where(z == 0, 0.0, c[0])
        g[1, z] = jnp.where(z == NZ - 1, 0.0, c[1])
        g[2, z] = jnp.where(row == 0, 0.0, c[2])
        g[3, z] = jnp.where(row == NX - 1, 0.0, c[3])
        g[4, z] = jnp.where(lane == 0, 0.0, c[4])
        g[5, z] = jnp.where(lane == NY - 1, 0.0, c[5])
        diag[z] = total
        here = u[z]
        res = f[z] * inverse - here + own_neighbours(u, g, z)
        s[z] = res
        perm_sum[z // 8] += perm
        mine = layer_lanes(z)
        pu = jnp.where(mine, pltpu.roll(here, 4 * z, 1), pu)
        ps = jnp.where(mine, pltpu.roll(res, 4 * z, 1), ps)
        pg = jnp.where(mine, pltpu.roll(jnp.where(lane == 0, c[4], c[5]), 4 * z, 1), pg)
        return pu, ps, pg

    zero = jnp.zeros((NX, NY), F32)
    pu, ps, pg = lax.fori_loop(0, NZ, layer, (zero, zero, zero), unroll=8)
    yp[0:32, :] = pu
    yp[32:64, :] = ps
    yp[64:96, :] = pg
    for side, z in ((0, 0), (1, NZ - 1)):
        _, _, c = couplings(p[z], [w[k, z].astype(F32) for k in range(3)])
        zp[side, 0:32, :] = u[z]
        zp[side, 32:64, :] = s[z]
        zp[side, 64:96, :] = c[side]
        zp[side, 96:128, :] = jnp.where(lane == 0, c[4], 0.0) + jnp.where(lane == NY - 1, c[5], 0.0)


def z_part(stage, faces, xp, xh):
    row, _ = plane()
    row8 = iota((8, NY), 0)
    all_lines = []
    for side, z in ((0, 0), (1, NZ - 1)):
        res = faces[side, 32:64, :]
        lines = jnp.zeros((8, NY), F32)
        for end, at in ((0, 0), (1, NX - 1)):
            line = xh[end, z : z + 1, :]
            res += jnp.where(row == at, xp[end, 64 + z : 65 + z, :] * line, 0.0)
            lines = jnp.where(row8 == end, line, lines)
        stage[side, 0:32, :] = faces[side, 0:32, :]
        stage[side, 32:64, :] = res
        all_lines.append(lines)
    return all_lines


def y_part(field, res, coupling, zp, zh, xp, xh):
    row, lane = plane()
    row8 = iota((8, NY), 0)
    z_lines = [zh[end, 0:32, :] for end in (0, 1)]
    res += jnp.where(ends(lane), zp[0, 64:96, :] * z_lines[0], 0.0)
    last = 4 * (NZ - 1)
    res += jnp.where(layer_lanes(NZ - 1), pltpu.roll(zp[1, 64:96, :] * z_lines[1], last, 1), 0.0)
    x_lines = jnp.zeros((8, NY), F32)
    for end, at in ((0, 0), (1, NX - 1)):
        line = xh[end, 0:32, :]
        res += jnp.where(row == at, combined_row(xp[end, 64:96, :] * line), 0.0)
        x_lines = jnp.where(row8 == end, combined_row(line), x_lines)
    messages = []
    q = fourths()
    for side in (0, 1):
        body = jnp.where(q == 0, shift_lanes(field, side), shift_lanes(res, 1 + side))
        if coupling is not None:
            body = jnp.where(q == 2, shift_lanes(coupling, 2 + side), body)
        for end in (0, 1):
            at = 3 + 4 * end
            body = jnp.where(lane == at, shift_lanes(z_lines[end], at + side), body)
        messages.append((body, shift_lanes(x_lines, side)))
    return messages


def first_message_kernel(
    xodd, xeven, zeven, zodd, xp, zp, yp,
    xh, zu, z_to_even, z_to_odd, y_to_even, y_to_odd,
    z_stage, z_rows, y_stage,
):
    take_in(xh, xeven, xodd, "gx")
    take_in(zu, zeven, zodd, "gz")
    lines = z_part(z_stage, zp, xp, xh)
    for side in (0, 1):
        z_rows[side, 0:32, :] = z_stage[side, 32:64, :]
        z_rows[side, 32:96, :] = zp[side, 64:128, :]
        z_rows[side, 96:104, :] = lines[side]
    put_out(z_rows, z_to_even, z_to_odd, "gz")
    messages = y_part(yp[0:32, :], yp[32:64, :], yp[64:96, :], zp, zu, xp, xh)
    for side in (0, 1):
        y_stage[side, 0:32, :], y_stage[side, 32:40, :] = messages[side]
    put_out(y_stage, y_to_even, y_to_odd, "gy")


def z_halo_residual(side, res, zh1, yh, mine):
    _, lane = plane()
    at = 3 + 4 * side
    low, high = yh[0, 0:32, at : at + 1], yh[1, 0:32, at : at + 1]
    corner = jnp.where(lane == 0, low, 0.0) + jnp.where(lane == NY - 1, high, 0.0)
    return res + zh1[side, 64:96, :] * mine + zh1[side, 96:128, :] * corner


def x_halo_residual(side, res, xh1, zh, lines, yh, mine):
    row, _ = plane()
    total = res + xh1[side, 64:96, :] * mine
    for end, at in ((0, 0), (1, NZ - 1)):
        total += jnp.where(row == at, xh1[side, 96 + end : 97 + end, :] * zh[end, lines + side : lines + side + 1, :], 0.0)
    corner = combine(yh[0, 32 + side : 33 + side, :], yh[1, 32 + side : 33 + side, :], 0)
    return total + columns(xh1[side, 98:99, :] * corner)


def group_sums(x):
    return jnp.sum(x.reshape(4, 8, NY), axis=1)


def exact_dot(a, b):
    return jnp.dot(a, b, precision=lax.Precision.HIGHEST, preferred_element_type=F32)


def second_kernel(
    u, g, diag, s1, perm_sum, zp, yp, xp, xh, zu, yodd, zeven, zodd, yeven,
    zh, yh, s0, d0, b, xp2, cross2, zy2, even, odd,
    zin, cross, rsum, rows, edge_s, edge_d, stage,
):
    take_in(yh, yeven, yodd, "gy")
    take_in(zin, zeven, zodd, "gz")
    for side in (0, 1):
        zh[side, 0:32, :] = zu[side]
        zh[side, 32:ZH1, :] = zin[side]
    scale = 1.0 / THETA
    low, high = yh[0, 0:32, :], yh[1, 0:32, :]
    own_y = yp[64:96, :]
    yq = own_y * combine(low, high, 0)
    yq2 = own_y * (scale * (combine(low, high, 1) + combine(low, high, 2) * yp[0:32, :]))
    zy2[2] = yq2
    zq = []
    for side, z in ((0, 0), (1, NZ - 1)):
        zq.append(zp[side, 64:96, :] * zh[side, 0:32, :])
        zy2[side] = zp[side, 64:96, :] * (scale * z_halo_residual(side, zh[side, 32:64, :], zh, yh, u[z]))
        gx = xp[side, 64:96, :]
        cross[side] = gx * xh[side, 0:32, :]
        cross2[side] = gx * (scale * x_halo_residual(side, xh[side, 32:64, :], xh, zh, 128, yh, xp[side, 0:32, :]))
    rsum[...] = jnp.zeros_like(rsum)

    def start(z, carry):
        res = s1[z] + from_faces(z, cross, yq)
        s0[z] = res
        d0[z] = res * scale
        rsum[z // 8] += res * diag[z]
        return carry

    lax.fori_loop(0, NZ, start, 0, unroll=32)
    for side, z in ((0, 0), (1, NZ - 1)):
        s0[z] += zq[side]
        d0[z] += zq[side] * scale
        rsum[z // 8] += zq[side] * diag[z]
    for block in range(4):
        rows[0, 4 * block : 4 * block + 4, :] = group_sums(rsum[block])
        rows[1, 4 * block : 4 * block + 4, :] = group_sums(perm_sum[block])
    select = jnp.where(iota((NY, NY), 0) // 8 == iota((NY, NY), 1), 1.0, 0.0)
    lane16 = iota((16, NY), 1)
    weights = jnp.where(lane16 < 16, exact_dot(rows[1], select), 1.0)
    rhs = jnp.where(lane16 < 16, (OMEGA * 8.0 / 6.0) * exact_dot(rows[0], select) / weights, 0.0)
    b[...] = rhs

    def edge(z, carry):
        for side in (0, 1):
            at, _ = face_rows(side)
            before = d0[z, at, :]
            near = edge_neighbours(lambda k: d0[k, at, :], [g[k, z, at, :] for k in range(6)], z)
            res = s0[z, at, :] - before + near + from_faces_rows(z, cross2, yq2, side)
            edge_s[side, z] = res
            edge_d[side, z] = A[0] * before + B[0] * res
        return carry

    lax.fori_loop(0, NZ, edge, 0, unroll=32)
    for side in (0, 1):
        at, _ = face_rows(side)
        for end, z in ((0, 0), (1, NZ - 1)):
            edge_s[side, z] += zy2[end, at, :]
            edge_d[side, z] += B[0] * zy2[end, at, :]

    def face(z, carry):
        for side in (0, 1):
            at, r = face_rows(side)
            here = edge_d[side, z]
            near = edge_neighbours(lambda k: edge_d[side, k], [g[k, z, at, :] for k in range(6)], z)
            res = edge_s[side, z] - here + near
            xp2[side, pl.ds(z, 1), :] = here[r : r + 1]
            xp2[side, pl.ds(NZ + z, 1), :] = res[r : r + 1]
        return carry

    lax.fori_loop(0, NZ, face, 0, unroll=32)
    for side in (0, 1):
        stage[side, 0:64, :] = xp2[side]
        for z in range(4):
            stage[side, 64 + 3 * z : 67 + 3 * z, :] = rhs[4 * z + side : 4 * z + side + 3]
        stage[side, 76:80, :] = jnp.zeros((4, NY), F32)
    put_out(stage, even, odd, "gx")


def edge_neighbours(rows_of, g, z):
    here = rows_of(z)
    total = g[0] * rows_of(jnp.maximum(z - 1, 0)) + g[1] * rows_of(jnp.minimum(z + 1, NZ - 1))
    total += g[2] * pltpu.roll(here, 1, 0) + g[3] * pltpu.roll(here, 7, 0)
    return total + g[4] * pltpu.roll(here, 1, 1) + g[5] * pltpu.roll(here, NY - 1, 1)


def second_block_kernel(u, g, s0, d0, cross2, zy2, s, d, acc, zp2, yp2, s1):
    yq2 = zy2[2]

    def step(z, carry):
        before = d0[z]
        res = s0[z] - before + own_neighbours(d0, g, z) + from_faces(z, cross2, yq2)
        after = A[0] * before + B[0] * res
        s1[z] = res
        d[z] = after
        acc[z] = u[z] + before + after
        return carry

    lax.fori_loop(0, NZ, step, 0, unroll=32)
    for side, z in ((0, 0), (1, NZ - 1)):
        s1[z] += zy2[side]
        d[z] += B[0] * zy2[side]
        acc[z] += B[0] * zy2[side]

    def partial(z, carry):
        pu, ps = carry
        here = d[z]
        res = s1[z] - here + own_neighbours(d, g, z)
        s[z] = res
        mine = layer_lanes(z)
        return jnp.where(mine, pltpu.roll(here, 4 * z, 1), pu), jnp.where(mine, pltpu.roll(res, 4 * z, 1), ps)

    zero = jnp.zeros((NX, NY), F32)
    pu, ps = lax.fori_loop(0, NZ, partial, (zero, zero), unroll=8)
    yp2[0:32, :] = pu
    yp2[32:64, :] = ps
    for side, z in ((0, 0), (1, NZ - 1)):
        zp2[side, 0:32, :] = d[z]
        zp2[side, 32:64, :] = s[z]


def second_z_kernel(xodd, xeven, xp, zp2, b, xh2, even, odd, b3, stage, rows):
    take_in(xh2, xeven, xodd, "gx")
    lines = z_part(stage, zp2, xp, xh2)
    lane16 = iota((16, NY), 1)
    wide = b[...]
    for end in (0, 1):
        first = 1 - end
        rows[...] = jnp.zeros_like(rows)
        for z in range(4):
            rows[4 * z + first : 4 * z + first + 3, :] = xh2[end, 64 + 3 * z : 67 + 3 * z, :]
        base = 32 * (end + 1)
        wide = jnp.where((lane16 >= base) & (lane16 < base + 16), pltpu.roll(rows[...], base, 1), wide)
    b3[...] = wide
    for side in (0, 1):
        stage[side, 64:72, :] = lines[side]
        stage[side, 72:88, :] = wide
    put_out(stage, even, odd, "gz")


def second_y_kernel(zeven, zodd, xp, zp, yp2, xh2, b3, zh2, even, odd, stage):
    take_in(zh2, zeven, zodd, "gz")
    messages = y_part(yp2[0:32, :], yp2[32:64, :], None, zp, zh2, xp, xh2)
    within = lax.rem(iota((16, NY), 1), 32)
    parts = (b3[...], zh2[0, 72:88, :], zh2[1, 72:88, :])
    for side in (0, 1):
        stage[side, 0:32, :], stage[side, 32:40, :] = messages[side]
        coarse = jnp.zeros((16, NY), F32)
        for k in range(3):
            at = 4 * k
            moved = shift_lanes(parts[k], at - 13 * side)
            coarse = jnp.where((within >= at) & (within < at + 3), moved, coarse)
        stage[side, 40:56, :] = coarse
    put_out(stage, even, odd, "gy")


def coarse_solve(b3, zh2, yh2, ext, err, spread):
    ext[...] = jnp.zeros_like(ext)
    lane4 = iota((4, NY), 1)
    within = lax.rem(iota((16, NY), 1), 32)
    wide = []
    for k, part in enumerate((b3[...], zh2[0, 72:88, :], zh2[1, 72:88, :])):
        full = jnp.where((within >= 3) & (within < 19), shift_lanes(part, 3), 0.0)
        full = jnp.where(within < 3, shift_lanes(yh2[0, 40:56, :], -4 * k), full)
        wide.append(jnp.where((within >= 19) & (within < 22), shift_lanes(yh2[1, 40:56, :], 19 - 4 * k), full))

    for z in range(10):
        values, at = (wide[1], 4 * (z + 1)) if z < 3 else (wide[0], 4 * (z - 3)) if z < 7 else (wide[2], 4 * (z - 7))
        four = values[at : at + 4]
        own, low, high = [jnp.where(lane4 < 22, shift_lanes(four, -32 * k), 0.0) for k in range(3)]
        ext[z, 0:3, :] = low[1:4]
        ext[z, 3:7, :] = own
        ext[z, 7:10, :] = high[0:3]
    x, y = iota((16, NY), 0), iota((16, NY), 1)
    at_z, at_x, at_y = lax.axis_index("gz"), lax.axis_index("gx"), lax.axis_index("gy")
    last_z, last_x, last_y = lax.axis_size("gz") - 1, lax.axis_size("gx") - 1, lax.axis_size("gy") - 1
    inside = (x < 10) & (y < 22)
    inside &= ((x >= 3) | (at_x > 0)) & ((x < 7) | (at_x < last_x))
    inside &= ((y >= 3) | (at_y > 0)) & ((y < 19) | (at_y < last_y))
    keep = jnp.where(inside, 1.0, 0.0)
    keep_low = jnp.where(at_z > 0, keep, 0.0)
    keep_high = jnp.where(at_z < last_z, keep, 0.0)
    rhs = [ext[z] for z in range(10)]
    e = rhs
    for sweep in range(3):
        lo, hi = sweep + 1, 9 - sweep
        new = []
        for z in range(10):
            if z < lo or z >= hi:
                new.append(e[z])
                continue
            c = e[z]
            beside = e[z - 1] + e[z + 1] + pltpu.roll(c, 1, 0) + pltpu.roll(c, 15, 0) + pltpu.roll(c, 1, 1) + pltpu.roll(c, NY - 1, 1)
            v = (1.0 - OMEGA) * c + (OMEGA / 6.0) * beside + rhs[z]
            new.append(v * (keep_low if z < 3 else keep_high if z >= 7 else keep))
        e = new
    for z in range(4):
        err[4 * z : 4 * z + 4, :] = e[z + 3][3:7]
    select = jnp.where(iota((NY, NY), 0) == iota((NY, NY), 1) // 8 + 3, 1.0, 0.0)
    fine = exact_dot(err[...], select)
    for z in range(4):
        spread[z] = jnp.broadcast_to(fine[4 * z : 4 * z + 4][:, None, :], (4, 8, NY)).reshape(NX, NY)


def third_kernel(
    g, s2, d1, acc, zp, yp, xp, xh, zh, yh, xp2, zp2, yp2, xh2, zh2, b3, yodd, yeven,
    far_out,
    yh2, s, d, cross, cross2, ext, err, spread, out, sems,
):
    take_in(yh2, yeven, yodd, "gy")
    low, high = yh2[0, 0:32, :], yh2[1, 0:32, :]
    own_y = yp[64:96, :]
    yu = combine(low, high, 0)
    yq = own_y * yu
    yq2 = own_y * (A[1] * yu + B[1] * (combine(low, high, 1) + combine(yh[0, 0:32, :], yh[1, 0:32, :], 2) * yp2[0:32, :]))
    zq, zq2 = [], []
    for side, z in ((0, 0), (1, NZ - 1)):
        zu, xu = zh2[side, 0:32, :], xh2[side, 0:32, :]
        zq.append(zp[side, 64:96, :] * zu)
        dz = A[1] * zu + B[1] * z_halo_residual(side, zh2[side, 32:64, :], zh, yh2, zp2[side, 0:32, :])
        zq2.append(zp[side, 64:96, :] * dz)
        gx = xp[side, 64:96, :]
        cross[side] = gx * xu
        dx = A[1] * xu + B[1] * x_halo_residual(side, xh2[side, 32:64, :], xh, zh2, 64, yh2, xp2[side, 0:32, :])
        cross2[side] = gx * dx
    coarse_solve(b3, zh2, yh2, ext, err, spread)

    def step(z, carry):
        res = s2[z] + from_faces(z, cross, yq)
        s[z] = res
        d[z] = A[1] * d1[z] + B[1] * res
        return carry

    lax.fori_loop(0, NZ, step, 0, unroll=32)
    for side, z in ((0, 0), (1, NZ - 1)):
        s[z] += zq[side]
        d[z] += B[1] * zq[side]

    def finish(z, carry):
        before = d[z]
        res = s[z] - before + own_neighbours(d, g, z) + from_faces(z, cross2, yq2)
        out[z] = acc[z] + before + (A[2] * before + B[2] * res) + spread[z // 8]
        return carry

    copies = []
    for part in range(4):
        lax.fori_loop(8 * part, 8 * part + 8, finish, 0, unroll=8)
        if part == 0:
            out[0] += B[2] * zq2[0]
        if part == 3:
            out[NZ - 1] += B[2] * zq2[1]
        rows = pl.ds(8 * part, 8)
        copies.append(pltpu.make_async_copy(out.at[rows], far_out.at[rows], sems.at[part]))
        copies[part].start()
    for copy in copies:
        copy.wait()


VM = pl.BlockSpec(memory_space=pltpu.VMEM)
HBM = pl.BlockSpec(memory_space=pltpu.HBM)
BF16_FIELD = jax.ShapeDtypeStruct((3,) + FULL, jnp.bfloat16)


def call(kernel, name, n_in, outs, scratch=(), us=0.2, place=VM, more=(), results=VM):
    return pl.pallas_call(
        kernel,
        out_shape=[x if isinstance(x, jax.ShapeDtypeStruct) else jax.ShapeDtypeStruct(x, F32) for x in outs],
        in_specs=[place] * n_in,
        out_specs=[results] * len(outs),
        scratch_shapes=[pltpu.VMEM(shape, F32) for shape in scratch] + list(more),
        compiler_params=pltpu.CompilerParams(vmem_limit_bytes=32 * 2**20),
        cost_estimate=pl.CostEstimate(flops=0, transcendentals=0, bytes_accessed=int(us * 3e6)),
        name=name,
    )


def swap(even, odd, axis):
    count = lax.axis_size(axis)
    results = []
    for first, values in ((1, odd), (0, even)):
        pairs = []
        for i in range(first, count - 1, 2):
            pairs += [(i, i + 1), (i + 1, i)]
        results.append(lax.ppermute(values, axis, pairs))
    return results[::-1]


def per_device(u, f, p, w):
    face = (2, 32, NY)
    far = [pltpu.with_memory_space_constraint(x, pltpu.HBM) for x in (u, f, p, w)]
    u, f, p, w, xp, even, odd, zeven, zodd = call(
        face_kernel, "x_faces", 4,
        [FULL, FULL, FULL, BF16_FIELD, (2, XM1, NY), (XM1, NY), (XM1, NY), (NX, NY), (NX, NY)], (), 2.0, HBM,
        [pltpu.SemaphoreType.DMA((4, 4))],
    )(*far)
    g, diag, s, perm_sum, zp, yp = call(
        block_kernel, "block", 4, [(6,) + FULL, FULL, FULL, (4, NX, NY), (2, 128, NY), (96, NY)], (), 2.5
    )(u, f, p, w)
    even, odd = swap(even, odd, "gx")
    zeven, zodd = swap(zeven, zodd, "gz")
    xh, zu, zeven, zodd, yeven, yodd = call(
        first_message_kernel, "zy_message", 7,
        [(2, XM1, NY), (2, NX, NY), (ZM1, NY), (ZM1, NY), (YM1, NY), (YM1, NY)],
        [(2, 64, NY), (2, ZM1, NY), (2, YM1, NY)],
    )(odd, even, zeven, zodd, xp, zp, yp)
    zeven, zodd = swap(zeven, zodd, "gz")
    yeven, yodd = swap(yeven, yodd, "gy")
    zh, yh, s, d, b, xp2, cross2, zy2, even, odd = call(
        second_kernel, "two_steps", 14,
        [(2, ZH1, NY), (2, YM1, NY), FULL, FULL, (16, NY), (2, 64, NY), face, (3, NX, NY), (XM2, NY), (XM2, NY)],
        [(2, ZM1, NY), face, (4, NX, NY), (2, 16, NY), (2, NZ, 8, NY), (2, NZ, 8, NY), (2, XM2, NY)], 1.5,
    )(u, g, diag, s, perm_sum, zp, yp, xp, xh, zu, yodd, zeven, zodd, yeven)
    s, d1, acc, zp2, yp2 = call(
        second_block_kernel, "block_2", 6, [FULL, FULL, FULL, (2, 64, NY), (64, NY)], [FULL], 2.0
    )(u, g, s, d, cross2, zy2)
    even, odd = swap(even, odd, "gx")
    xh2, even, odd, b3 = call(
        second_z_kernel, "z_message_2", 5, [(2, XM2, NY), (ZM2, NY), (ZM2, NY), (16, NY)], [(2, ZM2, NY), (16, NY)]
    )(odd, even, xp, zp2, b)
    even, odd = swap(even, odd, "gz")
    zh2, even, odd = call(
        second_y_kernel, "y_message_2", 7, [(2, ZM2, NY), (YM2, NY), (YM2, NY)], [(2, YM2, NY)]
    )(even, odd, xp, zp, yp2, xh2, b3)
    even, odd = swap(even, odd, "gy")
    (out,) = call(
        third_kernel, "last_steps", 18, [FULL],
        [(2, YM2, NY), FULL, FULL, face, face, (10, 16, NY), (16, NY), (4, NX, NY), FULL], 2.5, VM,
        [pltpu.SemaphoreType.DMA((4,))], HBM,
    )(g, s, d1, acc, zp, yp, xp, xh, zh, yh, xp2, zp2, yp2, xh2, zh2, b3, odd, even)
    return out


def solution(mesh):
    placed = (
        P("gz", "gx", "gy"),
        P("gz", "gx", "gy"),
        P("gz", "gx", "gy"),
        P(None, "gz", "gx", "gy"),
    )
    return jax.shard_map(
        per_device, mesh=mesh, in_specs=placed, out_specs=P("gz", "gx", "gy"), check_vma=False
    )
```

```python
import jax
import jax.numpy as jnp
from jax import lax
from jax.experimental import pallas as pl
from jax.experimental.pallas import tpu as pltpu
from jax.sharding import PartitionSpec as P

THETA = 1.15
DELTA = 0.85
OMEGA = 0.8
F32 = jnp.float32

NZ, NX, NY = 32, 32, 128
FULL = (NZ, NX, NY)

SIGMA = THETA / DELTA
RHO0 = 1.0 / SIGMA
RHO1 = 1.0 / (2.0 * SIGMA - RHO0)
RHO2 = 1.0 / (2.0 * SIGMA - RHO1)
RHO3 = 1.0 / (2.0 * SIGMA - RHO2)
A = (RHO1 * RHO0, RHO2 * RHO1, RHO3 * RHO2)
B = (2.0 * RHO1 / DELTA, 2.0 * RHO2 / DELTA, 2.0 * RHO3 / DELTA)

XM1 = 104
ZM1 = 99
YM1 = 40
XM2 = 80
ZM2 = 88
YM2 = 56


def iota(shape, dim):
    return lax.broadcasted_iota(jnp.int32, shape, dim)


def plane():
    return iota((NX, NY), 0), iota((NX, NY), 1)


def parity(axis):
    return lax.rem(lax.axis_index(axis), 2)


def put_out(stage, even, odd, axis):
    odd_one = parity(axis)
    even[...] = stage[1 - odd_one]
    odd[...] = stage[odd_one]


def take_in(halo, even, odd, axis):
    odd_one = parity(axis)
    halo[1 - odd_one] = even[...]
    halo[odd_one] = odd[...]


def fourths(shape=(NX, NY)):
    return lax.rem(iota(shape, 1), 4)


def layer_lanes(z, shape=(NX, NY)):
    lane = iota(shape, 1)
    return (lane == 4 * z) | (lane == lax.rem(4 * z + NY - 1, NY))


def ends(lane):
    return (lane == 0) | (lane == NY - 1)


def shift_lanes(x, amount):
    return pltpu.roll(x, amount % NY, 1)


def columns(row_values):
    row, lane = plane()
    wide = jnp.broadcast_to(row_values, (NX, NY))
    low = jnp.sum(jnp.where(lane == 4 * row, wide, 0.0), axis=1, keepdims=True)
    high = jnp.sum(jnp.where(lane == lax.rem(4 * row + NY - 1, NY), wide, 0.0), axis=1, keepdims=True)
    return jnp.where(lane == 0, low, 0.0) + jnp.where(lane == NY - 1, high, 0.0)


def combined_row(values):
    row, lane = plane()
    low = jnp.where(lane == 4 * row, jnp.broadcast_to(values[:, 0:1], (NX, NY)), 0.0)
    high = jnp.where(lane == lax.rem(4 * row + NY - 1, NY), jnp.broadcast_to(values[:, NY - 1 :], (NX, NY)), 0.0)
    return jnp.sum(low + high, axis=0, keepdims=True)


def combine(low, high, q):
    return jnp.where(fourths(low.shape) == 0, shift_lanes(low, -q), shift_lanes(high, -q - 1))


def own_neighbours(field, g, z):
    here = field[z]
    total = g[0, z] * field[jnp.maximum(z - 1, 0)] + g[1, z] * field[jnp.minimum(z + 1, NZ - 1)]
    total += g[2, z] * pltpu.roll(here, 1, 0) + g[3, z] * pltpu.roll(here, NX - 1, 0)
    total += g[4, z] * pltpu.roll(here, 1, 1) + g[5, z] * pltpu.roll(here, NY - 1, 1)
    return total


def from_faces(z, xp, yp):
    row8 = iota((8, NY), 0)
    total = jnp.where(ends(iota((NX, NY), 1)), pltpu.roll(yp, lax.rem(NY - 4 * z, NY), 1), 0.0)
    first = total[0:8] + jnp.where(row8 == 0, xp[0, pl.ds(z, 1), :], 0.0)
    last = total[NX - 8 :] + jnp.where(row8 == 7, xp[1, pl.ds(z, 1), :], 0.0)
    return jnp.concatenate([first, total[8 : NX - 8], last], axis=0)


def from_faces_rows(z, xp, yp, side):
    rows, r = face_rows(side)
    total = jnp.where(ends(iota((8, NY), 1)), pltpu.roll(yp[rows], lax.rem(NY - 4 * z, NY), 1), 0.0)
    return total + jnp.where(iota((8, NY), 0) == r, xp[side, pl.ds(z, 1), :], 0.0)


def couplings(perm, speeds):
    total = 6.0 * perm + jnp.abs(speeds[0]) + jnp.abs(speeds[1]) + jnp.abs(speeds[2])
    inverse = 1.0 / total
    pairs = []
    for speed in speeds:
        pairs.append((perm + jnp.maximum(speed, 0.0)) * inverse)
        pairs.append((perm - jnp.minimum(speed, 0.0)) * inverse)
    return total, inverse, pairs


def face_rows(side):
    return (slice(0, 8), 0) if side == 0 else (slice(NX - 8, NX), 7)


def inner_neighbours(field, c, z, side):
    rows, _ = face_rows(side)
    lane = iota((8, NY), 1)
    here = field[z, rows, :]
    total = jnp.where(z == 0, 0.0, c[0]) * field[jnp.maximum(z - 1, 0), rows, :]
    total += jnp.where(z == NZ - 1, 0.0, c[1]) * field[jnp.minimum(z + 1, NZ - 1), rows, :]
    total += c[3 - side] * pltpu.roll(here, 7 if side == 0 else 1, 0)
    total += jnp.where(lane == 0, 0.0, c[4]) * pltpu.roll(here, 1, 1)
    total += jnp.where(lane == NY - 1, 0.0, c[5]) * pltpu.roll(here, NY - 1, 1)
    return total


def face_kernel(u_far, f_far, p_far, w_far, u, f, p, w, xp, zp, last_coupling, even, odd, z_even, z_odd, sems):
    lane8 = iota((8, NY), 1)
    copies = []
    for part in range(4):
        rows = pl.ds(8 * part, 8)
        copies.append([
            pltpu.make_async_copy(u_far.at[rows], u.at[rows], sems.at[part, 0]),
            pltpu.make_async_copy(f_far.at[rows], f.at[rows], sems.at[part, 1]),
            pltpu.make_async_copy(p_far.at[rows], p.at[rows], sems.at[part, 2]),
            pltpu.make_async_copy(w_far.at[:, rows], w.at[:, rows], sems.at[part, 3]),
        ])
    for part in range(4):
        copies[part][0].start()
    for part in range(4):
        for copy in copies[part][1:]:
            copy.start()

    def face(z, side):
        rows, _ = face_rows(side)
        half = slice(0, 16) if side == 0 else slice(NX - 16, NX)
        speeds = [w[k, z, half, :].astype(F32)[8 * side : 8 * side + 8] for k in range(3)]
        return couplings(p[z, rows, :], speeds)

    def layer(z, carry):
        edges = []
        for side in (0, 1):
            rows, r = face_rows(side)
            _, inverse, c = face(z, side)
            here = u[z, rows, :]
            res = f[z, rows, :] * inverse - here + inner_neighbours(u, c, z, side)
            for base, values in ((0, here), (NZ, res), (2 * NZ, c[2 + side])):
                xp[side, pl.ds(base + z, 1), :] = values[r : r + 1]
            merged = pltpu.roll(jnp.where(lane8 == 0, c[4], c[5]), 4 * z, 1)
            edges.append(jnp.where(layer_lanes(z, (8, NY)), merged, carry[side]))
        return tuple(edges)

    edges = (jnp.zeros((8, NY), F32),) * 2
    for part in range(4):
        copies[part][0].wait()
    for part in range(4):
        for copy in copies[part][1:]:
            copy.wait()
        edges = lax.fori_loop(8 * part, 8 * part + 8, layer, edges, unroll=8)
    for side in (0, 1):
        _, r = face_rows(side)
        for end, z in ((0, 0), (1, NZ - 1)):
            _, _, c = face(z, side)
            xp[side, 96 + end : 97 + end, :] = c[end][r : r + 1]
            xp[side, 99 + 2 * end : 100 + 2 * end, :] = jnp.where(lane8 == 0, 0.0, c[4])[r : r + 1]
            xp[side, 100 + 2 * end : 101 + 2 * end, :] = jnp.where(lane8 == NY - 1, 0.0, c[5])[r : r + 1]
        xp[side, 98:99, :] = edges[side][r : r + 1]
        _, _, c = face(1, side)
        xp[side, 103:104, :] = c[0][r : r + 1]
        _, _, c = face(NZ - 2, side)
        last_coupling[side] = jnp.broadcast_to(c[1][r : r + 1], (8, NY))
    put_out(xp, even, odd, "gx")
    row, lane = plane()
    for side, z, inner in ((0, 0, 1), (1, NZ - 1, NZ - 2)):
        here = u[z]
        _, inverse, c = couplings(p[z], [w[k, z].astype(F32) for k in range(3)])
        res = f[z] * inverse - here + c[1 - side] * u[inner]
        res += jnp.where(row == 0, 0.0, c[2]) * pltpu.roll(here, 1, 0)
        res += jnp.where(row == NX - 1, 0.0, c[3]) * pltpu.roll(here, NX - 1, 0)
        res += jnp.where(lane == 0, 0.0, c[4]) * pltpu.roll(here, 1, 1)
        res += jnp.where(lane == NY - 1, 0.0, c[5]) * pltpu.roll(here, NY - 1, 1)
        zp[side, 0:32, :] = here
        zp[side, 32:64, :] = res
        zp[side, 64:96, :] = c[side]
        zp[side, 96:97, :] = combined_row(jnp.where(lane == 0, c[4], c[5]))
        zp[side, 97:98, :] = c[2][0:1]
        zp[side, 98:99, :] = c[3][NX - 1 :]
    put_out(zp, z_even, z_odd, "gz")


def block_kernel(u, f, p, w, g, diag, s, perm_sum, yp):
    row, lane = plane()
    perm_sum[...] = jnp.zeros_like(perm_sum)

    def layer(z, carry):
        pu, ps, pg = carry
        perm = p[z]
        total, inverse, c = couplings(perm, [w[k, z].astype(F32) for k in range(3)])
        g[0, z] = jnp.where(z == 0, 0.0, c[0])
        g[1, z] = jnp.where(z == NZ - 1, 0.0, c[1])
        g[2, z] = jnp.where(row == 0, 0.0, c[2])
        g[3, z] = jnp.where(row == NX - 1, 0.0, c[3])
        g[4, z] = jnp.where(lane == 0, 0.0, c[4])
        g[5, z] = jnp.where(lane == NY - 1, 0.0, c[5])
        diag[z] = total
        here = u[z]
        res = f[z] * inverse - here + own_neighbours(u, g, z)
        s[z] = res
        perm_sum[z // 8] += perm
        mine = layer_lanes(z)
        pu = jnp.where(mine, pltpu.roll(here, 4 * z, 1), pu)
        ps = jnp.where(mine, pltpu.roll(res, 4 * z, 1), ps)
        pg = jnp.where(mine, pltpu.roll(jnp.where(lane == 0, c[4], c[5]), 4 * z, 1), pg)
        return pu, ps, pg

    zero = jnp.zeros((NX, NY), F32)
    pu, ps, pg = lax.fori_loop(0, NZ, layer, (zero, zero, zero), unroll=8)
    yp[0:32, :] = pu
    yp[32:64, :] = ps
    yp[64:96, :] = pg


def z_part(stage, faces, xp, xh):
    row, _ = plane()
    row8 = iota((8, NY), 0)
    all_lines = []
    for side, z in ((0, 0), (1, NZ - 1)):
        res = faces[side, 32:64, :]
        lines = jnp.zeros((8, NY), F32)
        for end, at in ((0, 0), (1, NX - 1)):
            line = xh[end, z : z + 1, :]
            res += jnp.where(row == at, xp[end, 64 + z : 65 + z, :] * line, 0.0)
            lines = jnp.where(row8 == end, line, lines)
        stage[side, 0:32, :] = faces[side, 0:32, :]
        stage[side, 32:64, :] = res
        all_lines.append(lines)
    return all_lines


def y_part(field, res, coupling, zp, zh, xp, xh):
    row, lane = plane()
    row8 = iota((8, NY), 0)
    z_lines = [zh[end, 0:32, :] for end in (0, 1)]
    res += jnp.where(ends(lane), zp[0, 64:96, :] * z_lines[0], 0.0)
    last = 4 * (NZ - 1)
    res += jnp.where(layer_lanes(NZ - 1), pltpu.roll(zp[1, 64:96, :] * z_lines[1], last, 1), 0.0)
    x_lines = jnp.zeros((8, NY), F32)
    for end, at in ((0, 0), (1, NX - 1)):
        line = xh[end, 0:32, :]
        res += jnp.where(row == at, combined_row(xp[end, 64:96, :] * line), 0.0)
        x_lines = jnp.where(row8 == end, combined_row(line), x_lines)
    messages = []
    q = fourths()
    for side in (0, 1):
        body = jnp.where(q == 0, shift_lanes(field, side), shift_lanes(res, 1 + side))
        if coupling is not None:
            body = jnp.where(q == 2, shift_lanes(coupling, 2 + side), body)
        for end in (0, 1):
            at = 3 + 4 * end
            body = jnp.where(lane == at, shift_lanes(z_lines[end], at + side), body)
        messages.append((body, shift_lanes(x_lines, side)))
    return messages


def first_y_kernel(
    xodd, xeven, zeven, zodd, xp, zp, yp,
    xh, zh, even, odd, line_even, line_odd,
    stage, lines,
):
    take_in(xh, xeven, xodd, "gx")
    take_in(zh, zeven, zodd, "gz")
    messages = y_part(yp[0:32, :], yp[32:64, :], yp[64:96, :], zp, zh, xp, xh)
    for side in (0, 1):
        stage[side, 0:32, :], stage[side, 32:40, :] = messages[side]
    put_out(stage, even, odd, "gy")
    for side, z in ((0, 0), (1, NZ - 1)):
        for end in (0, 1):
            lines[side, end : end + 1, :] = xh[end, z : z + 1, :]
            lines[side, 2 + end : 3 + end, :] = xh[end, 64 + z : 65 + z, :]
        lines[side, 4:8, :] = jnp.zeros((4, NY), F32)
    put_out(lines, line_even, line_odd, "gz")


def z_halo_residual(side, res, zh1, yh, mine):
    _, lane = plane()
    at = 3 + 4 * side
    low, high = yh[0, 0:32, at : at + 1], yh[1, 0:32, at : at + 1]
    corner = jnp.where(lane == 0, low, 0.0) + jnp.where(lane == NY - 1, high, 0.0)
    return res + zh1[side, 64:96, :] * mine + columns(zh1[side, 96:97, :]) * corner


def x_halo_residual(side, res, xh1, zh, lines, yh, mine):
    row, _ = plane()
    total = res + xh1[side, 64:96, :] * mine
    if zh is not None:
        for end, at in ((0, 0), (1, NZ - 1)):
            total += jnp.where(row == at, xh1[side, 96 + end : 97 + end, :] * zh[end, lines + side : lines + side + 1, :], 0.0)
    corner = combine(yh[0, 32 + side : 33 + side, :], yh[1, 32 + side : 33 + side, :], 0)
    return total + columns(xh1[side, 98:99, :] * corner)


def group_sums(x):
    return jnp.sum(x.reshape(4, 8, NY), axis=1)


def exact_dot(a, b):
    return jnp.dot(a, b, precision=lax.Precision.HIGHEST, preferred_element_type=F32)


def second_kernel(
    u, g, diag, s1, perm_sum, zp, yp, xp, last_coupling, xh, zh, yodd, yeven,
    yh, s0, d0, b, xp2, cross2, zy2, even, odd,
    cross, rsum, rows, edge_s, edge_d, stage,
):
    take_in(yh, yeven, yodd, "gy")
    scale = 1.0 / THETA
    low, high = yh[0, 0:32, :], yh[1, 0:32, :]
    own_y = yp[64:96, :]
    yq = own_y * combine(low, high, 0)
    yq2 = own_y * (scale * (combine(low, high, 1) + combine(low, high, 2) * yp[0:32, :]))
    zy2[2] = yq2
    zq = []
    for side, z in ((0, 0), (1, NZ - 1)):
        zq.append(zp[side, 64:96, :] * zh[side, 0:32, :])
        zy2[side] = zp[side, 64:96, :] * (scale * z_halo_residual(side, zh[side, 32:64, :], zh, yh, u[z]))
        gx = xp[side, 64:96, :]
        cross[side] = gx * xh[side, 0:32, :]
        cross2[side] = gx * (scale * x_halo_residual(side, xh[side, 32:64, :], xh, None, 0, yh, xp[side, 0:32, :]))
    rsum[...] = jnp.zeros_like(rsum)

    def start(z, carry):
        res = s1[z] + from_faces(z, cross, yq)
        s0[z] = res
        d0[z] = res * scale
        rsum[z // 8] += res * diag[z]
        return carry

    lax.fori_loop(0, NZ, start, 0, unroll=32)
    for side, z in ((0, 0), (1, NZ - 1)):
        s0[z] += zq[side]
        d0[z] += zq[side] * scale
        rsum[z // 8] += zq[side] * diag[z]
    for block in range(4):
        rows[0, 4 * block : 4 * block + 4, :] = group_sums(rsum[block])
        rows[1, 4 * block : 4 * block + 4, :] = group_sums(perm_sum[block])
    select = jnp.where(iota((NY, NY), 0) // 8 == iota((NY, NY), 1), 1.0, 0.0)
    lane16 = iota((16, NY), 1)
    weights = jnp.where(lane16 < 16, exact_dot(rows[1], select), 1.0)
    rhs = jnp.where(lane16 < 16, (OMEGA * 8.0 / 6.0) * exact_dot(rows[0], select) / weights, 0.0)
    b[...] = rhs

    def edge(z, carry):
        for side in (0, 1):
            at, _ = face_rows(side)
            before = d0[z, at, :]
            near = edge_neighbours(lambda k: d0[k, at, :], [g[k, z, at, :] for k in range(6)], z)
            res = s0[z, at, :] - before + near + from_faces_rows(z, cross2, yq2, side)
            edge_s[side, z] = res
            edge_d[side, z] = A[0] * before + B[0] * res
        return carry

    lax.fori_loop(0, NZ, edge, 0, unroll=32)
    for side in (0, 1):
        at, _ = face_rows(side)
        for end, z in ((0, 0), (1, NZ - 1)):
            edge_s[side, z] += zy2[end, at, :]
            edge_d[side, z] += B[0] * zy2[end, at, :]

    def face(z, carry):
        for side in (0, 1):
            at, r = face_rows(side)
            here = edge_d[side, z]
            near = edge_neighbours(lambda k: edge_d[side, k], [g[k, z, at, :] for k in range(6)], z)
            res = edge_s[side, z] - here + near
            xp2[side, pl.ds(z, 1), :] = here[r : r + 1]
            xp2[side, pl.ds(NZ + z, 1), :] = res[r : r + 1]
        return carry

    lax.fori_loop(0, NZ, face, 0, unroll=32)
    for side in (0, 1):
        stage[side, 0:64, :] = xp2[side]
        for z in range(4):
            stage[side, 64 + 3 * z : 67 + 3 * z, :] = rhs[4 * z + side : 4 * z + side + 3]
        stage[side, 76:80, :] = last_coupling[side, 0:4, :]
    put_out(stage, even, odd, "gx")


def edge_neighbours(rows_of, g, z):
    here = rows_of(z)
    total = g[0] * rows_of(jnp.maximum(z - 1, 0)) + g[1] * rows_of(jnp.minimum(z + 1, NZ - 1))
    total += g[2] * pltpu.roll(here, 1, 0) + g[3] * pltpu.roll(here, 7, 0)
    return total + g[4] * pltpu.roll(here, 1, 1) + g[5] * pltpu.roll(here, NY - 1, 1)


def edge_change(coupling_x, edge_z, coupling_z, edge_x, corner):
    return (coupling_x * edge_z + coupling_z * edge_x) * corner * (1.0 / THETA)


def second_block_kernel(
    u, g, s0, d0, cross2, zy2, xp, xp2, zp, xh, zh, line_even, line_odd,
    s, d, acc, zp2, yp2, xm, lh,
    s1,
):
    yq2 = zy2[2]

    def step(z, carry):
        before = d0[z]
        res = s0[z] - before + own_neighbours(d0, g, z) + from_faces(z, cross2, yq2)
        after = A[0] * before + B[0] * res
        s1[z] = res
        d[z] = after
        acc[z] = u[z] + before + after
        return carry

    lax.fori_loop(0, NZ, step, 0, unroll=32)
    for side, z in ((0, 0), (1, NZ - 1)):
        s1[z] += zy2[side]
        d[z] += B[0] * zy2[side]
        acc[z] += B[0] * zy2[side]
    take_in(lh, line_even, line_odd, "gz")
    xm[...] = xp2[:, 0:32, :]
    for end, z in ((0, 0), (1, NZ - 1)):
        for side, x in ((0, 0), (1, NX - 1)):
            change = edge_change(
                xp[side, 64 + z : 65 + z, :], xh[side, 96 + end : 97 + end, :],
                zp[end, 64 + x : 65 + x, :], zh[end, 97 + side : 98 + side, :],
                lh[end, side : side + 1, :],
            )
            s1[z, x : x + 1, :] += change
            d[z, x : x + 1, :] += B[0] * change
            acc[z, x : x + 1, :] += B[0] * change
            xm[side, z : z + 1, :] += B[0] * change

    def partial(z, carry):
        pu, ps = carry
        here = d[z]
        res = s1[z] - here + own_neighbours(d, g, z)
        s[z] = res
        mine = layer_lanes(z)
        return jnp.where(mine, pltpu.roll(here, 4 * z, 1), pu), jnp.where(mine, pltpu.roll(res, 4 * z, 1), ps)

    zero = jnp.zeros((NX, NY), F32)
    pu, ps = lax.fori_loop(0, NZ, partial, (zero, zero), unroll=8)
    yp2[0:32, :] = pu
    yp2[32:64, :] = ps
    for side, z in ((0, 0), (1, NZ - 1)):
        zp2[side, 0:32, :] = d[z]
        zp2[side, 32:64, :] = s[z]


def second_z_kernel(xodd, xeven, xp, zp, zp2, b, xh, zh, lh, xh2, even, odd, b3, stage, rows):
    take_in(xh2, xeven, xodd, "gx")
    for side, x in ((0, 0), (1, NX - 1)):
        for end, z, inner in ((0, 0, 1), (1, NZ - 1, NZ - 2)):
            change = edge_change(
                xh[side, 64 + z : 65 + z, :], zp[end, 64 + x : 65 + x, :],
                xh[side, 96 + end : 97 + end, :], lh[end, 2 + side : 3 + side, :],
                zh[end, x : x + 1, :],
            )
            turn = B[0] * change
            at = 99 + 2 * end
            beside = xh[side, at : at + 1, :] * pltpu.roll(turn, 1, 1) + xh[side, at + 1 : at + 2, :] * pltpu.roll(turn, NY - 1, 1)
            inward = xh[side, 103:104, :] if end == 0 else xh2[side, 76:77, :]
            xh2[side, z : z + 1, :] += turn
            xh2[side, 32 + z : 33 + z, :] += change - turn + beside
            xh2[side, 32 + inner : 33 + inner, :] += inward * turn
    lines = z_part(stage, zp2, xp, xh2)
    lane16 = iota((16, NY), 1)
    wide = b[...]
    for end in (0, 1):
        first = 1 - end
        rows[...] = jnp.zeros_like(rows)
        for z in range(4):
            rows[4 * z + first : 4 * z + first + 3, :] = xh2[end, 64 + 3 * z : 67 + 3 * z, :]
        base = 32 * (end + 1)
        wide = jnp.where((lane16 >= base) & (lane16 < base + 16), pltpu.roll(rows[...], base, 1), wide)
    b3[...] = wide
    for side in (0, 1):
        stage[side, 64:72, :] = lines[side]
        stage[side, 72:88, :] = wide
    put_out(stage, even, odd, "gz")


def second_y_kernel(zeven, zodd, xp, zp, yp2, xh2, b3, zh2, even, odd, stage):
    take_in(zh2, zeven, zodd, "gz")
    messages = y_part(yp2[0:32, :], yp2[32:64, :], None, zp, zh2, xp, xh2)
    within = lax.rem(iota((16, NY), 1), 32)
    parts = (b3[...], zh2[0, 72:88, :], zh2[1, 72:88, :])
    for side in (0, 1):
        stage[side, 0:32, :], stage[side, 32:40, :] = messages[side]
        coarse = jnp.zeros((16, NY), F32)
        for k in range(3):
            at = 4 * k
            moved = shift_lanes(parts[k], at - 13 * side)
            coarse = jnp.where((within >= at) & (within < at + 3), moved, coarse)
        stage[side, 40:56, :] = coarse
    put_out(stage, even, odd, "gy")


def coarse_solve(b3, zh2, yh2, ext, err, spread):
    ext[...] = jnp.zeros_like(ext)
    lane4 = iota((4, NY), 1)
    within = lax.rem(iota((16, NY), 1), 32)
    wide = []
    for k, part in enumerate((b3[...], zh2[0, 72:88, :], zh2[1, 72:88, :])):
        full = jnp.where((within >= 3) & (within < 19), shift_lanes(part, 3), 0.0)
        full = jnp.where(within < 3, shift_lanes(yh2[0, 40:56, :], -4 * k), full)
        wide.append(jnp.where((within >= 19) & (within < 22), shift_lanes(yh2[1, 40:56, :], 19 - 4 * k), full))

    for z in range(10):
        values, at = (wide[1], 4 * (z + 1)) if z < 3 else (wide[0], 4 * (z - 3)) if z < 7 else (wide[2], 4 * (z - 7))
        four = values[at : at + 4]
        own, low, high = [jnp.where(lane4 < 22, shift_lanes(four, -32 * k), 0.0) for k in range(3)]
        ext[z, 0:3, :] = low[1:4]
        ext[z, 3:7, :] = own
        ext[z, 7:10, :] = high[0:3]
    x, y = iota((16, NY), 0), iota((16, NY), 1)
    at_z, at_x, at_y = lax.axis_index("gz"), lax.axis_index("gx"), lax.axis_index("gy")
    last_z, last_x, last_y = lax.axis_size("gz") - 1, lax.axis_size("gx") - 1, lax.axis_size("gy") - 1
    inside = (x < 10) & (y < 22)
    inside &= ((x >= 3) | (at_x > 0)) & ((x < 7) | (at_x < last_x))
    inside &= ((y >= 3) | (at_y > 0)) & ((y < 19) | (at_y < last_y))
    keep = jnp.where(inside, 1.0, 0.0)
    keep_low = jnp.where(at_z > 0, keep, 0.0)
    keep_high = jnp.where(at_z < last_z, keep, 0.0)
    rhs = [ext[z] for z in range(10)]
    e = rhs
    for sweep in range(3):
        lo, hi = sweep + 1, 9 - sweep
        new = []
        for z in range(10):
            if z < lo or z >= hi:
                new.append(e[z])
                continue
            c = e[z]
            beside = e[z - 1] + e[z + 1] + pltpu.roll(c, 1, 0) + pltpu.roll(c, 15, 0) + pltpu.roll(c, 1, 1) + pltpu.roll(c, NY - 1, 1)
            v = (1.0 - OMEGA) * c + (OMEGA / 6.0) * beside + rhs[z]
            new.append(v * (keep_low if z < 3 else keep_high if z >= 7 else keep))
        e = new
    for z in range(4):
        err[4 * z : 4 * z + 4, :] = e[z + 3][3:7]
    select = jnp.where(iota((NY, NY), 0) == iota((NY, NY), 1) // 8 + 3, 1.0, 0.0)
    fine = exact_dot(err[...], select)
    for z in range(4):
        spread[z] = jnp.broadcast_to(fine[4 * z : 4 * z + 4][:, None, :], (4, 8, NY)).reshape(NX, NY)


def third_kernel(
    g, s2, d1, acc, zp, yp, xp, xh, zh, yh, xm, zp2, yp2, xh2, zh2, b3, yodd, yeven,
    far_out,
    yh2, s, d, cross, cross2, ext, err, spread, out, sems,
):
    take_in(yh2, yeven, yodd, "gy")
    low, high = yh2[0, 0:32, :], yh2[1, 0:32, :]
    own_y = yp[64:96, :]
    yu = combine(low, high, 0)
    yq = own_y * yu
    yq2 = own_y * (A[1] * yu + B[1] * (combine(low, high, 1) + combine(yh[0, 0:32, :], yh[1, 0:32, :], 2) * yp2[0:32, :]))
    zq, zq2 = [], []
    for side, z in ((0, 0), (1, NZ - 1)):
        zu, xu = zh2[side, 0:32, :], xh2[side, 0:32, :]
        zq.append(zp[side, 64:96, :] * zu)
        dz = A[1] * zu + B[1] * z_halo_residual(side, zh2[side, 32:64, :], zh, yh2, zp2[side, 0:32, :])
        zq2.append(zp[side, 64:96, :] * dz)
        gx = xp[side, 64:96, :]
        cross[side] = gx * xu
        dx = A[1] * xu + B[1] * x_halo_residual(side, xh2[side, 32:64, :], xh, zh2, 64, yh2, xm[side])
        cross2[side] = gx * dx
    coarse_solve(b3, zh2, yh2, ext, err, spread)

    def step(z, carry):
        res = s2[z] + from_faces(z, cross, yq)
        s[z] = res
        d[z] = A[1] * d1[z] + B[1] * res
        return carry

    lax.fori_loop(0, NZ, step, 0, unroll=32)
    for side, z in ((0, 0), (1, NZ - 1)):
        s[z] += zq[side]
        d[z] += B[1] * zq[side]

    def finish(z, carry):
        before = d[z]
        res = s[z] - before + own_neighbours(d, g, z) + from_faces(z, cross2, yq2)
        out[z] = acc[z] + before + (A[2] * before + B[2] * res) + spread[z // 8]
        return carry

    copies = []
    for part in range(4):
        lax.fori_loop(8 * part, 8 * part + 8, finish, 0, unroll=8)
        if part == 0:
            out[0] += B[2] * zq2[0]
        if part == 3:
            out[NZ - 1] += B[2] * zq2[1]
        rows = pl.ds(8 * part, 8)
        copies.append(pltpu.make_async_copy(out.at[rows], far_out.at[rows], sems.at[part]))
        copies[part].start()
    for copy in copies:
        copy.wait()


VM = pl.BlockSpec(memory_space=pltpu.VMEM)
HBM = pl.BlockSpec(memory_space=pltpu.HBM)
BF16_FIELD = jax.ShapeDtypeStruct((3,) + FULL, jnp.bfloat16)


def call(kernel, name, n_in, outs, scratch=(), us=0.2, place=VM, more=(), results=VM):
    return pl.pallas_call(
        kernel,
        out_shape=[x if isinstance(x, jax.ShapeDtypeStruct) else jax.ShapeDtypeStruct(x, F32) for x in outs],
        in_specs=[place] * n_in,
        out_specs=[results] * len(outs),
        scratch_shapes=[pltpu.VMEM(shape, F32) for shape in scratch] + list(more),
        compiler_params=pltpu.CompilerParams(vmem_limit_bytes=32 * 2**20),
        cost_estimate=pl.CostEstimate(flops=0, transcendentals=0, bytes_accessed=int(us * 3e6)),
        name=name,
    )


def swap(even, odd, axis):
    count = lax.axis_size(axis)
    results = []
    for first, values in ((1, odd), (0, even)):
        pairs = []
        for i in range(first, count - 1, 2):
            pairs += [(i, i + 1), (i + 1, i)]
        results.append(lax.ppermute(values, axis, pairs))
    return results[::-1]


def per_device(u, f, p, w):
    face = (2, 32, NY)
    far = [pltpu.with_memory_space_constraint(x, pltpu.HBM) for x in (u, f, p, w)]
    u, f, p, w, xp, zp, last_coupling, even, odd, zeven, zodd = call(
        face_kernel, "faces", 4,
        [FULL, FULL, FULL, BF16_FIELD, (2, XM1, NY), (2, ZM1, NY), (2, 8, NY), (XM1, NY), (XM1, NY), (ZM1, NY), (ZM1, NY)],
        (), 2.0, HBM, [pltpu.SemaphoreType.DMA((4, 4))],
    )(*far)
    g, diag, s, perm_sum, yp = call(
        block_kernel, "block", 4, [(6,) + FULL, FULL, FULL, (4, NX, NY), (96, NY)], (), 2.5
    )(u, f, p, w)
    even, odd = swap(even, odd, "gx")
    zeven, zodd = swap(zeven, zodd, "gz")
    xh, zh, yeven, yodd, line_even, line_odd = call(
        first_y_kernel, "y_message", 7,
        [(2, XM1, NY), (2, ZM1, NY), (YM1, NY), (YM1, NY), (8, NY), (8, NY)],
        [(2, YM1, NY), (2, 8, NY)],
    )(odd, even, zeven, zodd, xp, zp, yp)
    yeven, yodd = swap(yeven, yodd, "gy")
    yh, s, d, b, xp2, cross2, zy2, even, odd = call(
        second_kernel, "two_steps", 13,
        [(2, YM1, NY), FULL, FULL, (16, NY), (2, 64, NY), face, (3, NX, NY), (XM2, NY), (XM2, NY)],
        [face, (4, NX, NY), (2, 16, NY), (2, NZ, 8, NY), (2, NZ, 8, NY), (2, XM2, NY)], 1.5,
    )(u, g, diag, s, perm_sum, zp, yp, xp, last_coupling, xh, zh, yodd, yeven)
    even, odd = swap(even, odd, "gx")
    line_even, line_odd = swap(line_even, line_odd, "gz")
    s, d1, acc, zp2, yp2, xm, lh = call(
        second_block_kernel, "block_2", 13, [FULL, FULL, FULL, (2, 64, NY), (64, NY), face, (2, 8, NY)], [FULL], 2.0
    )(u, g, s, d, cross2, zy2, xp, xp2, zp, xh, zh, line_even, line_odd)
    xh2, even, odd, b3 = call(
        second_z_kernel, "z_message_2", 9, [(2, XM2, NY), (ZM2, NY), (ZM2, NY), (16, NY)], [(2, ZM2, NY), (16, NY)]
    )(odd, even, xp, zp, zp2, b, xh, zh, lh)
    even, odd = swap(even, odd, "gz")
    zh2, even, odd = call(
        second_y_kernel, "y_message_2", 7, [(2, ZM2, NY), (YM2, NY), (YM2, NY)], [(2, YM2, NY)]
    )(even, odd, xp, zp, yp2, xh2, b3)
    even, odd = swap(even, odd, "gy")
    (out,) = call(
        third_kernel, "last_steps", 18, [FULL],
        [(2, YM2, NY), FULL, FULL, face, face, (10, 16, NY), (16, NY), (4, NX, NY), FULL], 2.5, VM,
        [pltpu.SemaphoreType.DMA((4,))], HBM,
    )(g, s, d1, acc, zp, yp, xp, xh, zh, yh, xm, zp2, yp2, xh2, zh2, b3, odd, even)
    return out


def solution(mesh):
    placed = (
        P("gz", "gx", "gy"),
        P("gz", "gx", "gy"),
        P("gz", "gx", "gy"),
        P(None, "gz", "gx", "gy"),
    )
    return jax.shard_map(
        per_device, mesh=mesh, in_specs=placed, out_specs=P("gz", "gx", "gy"), check_vma=False
    )
```

```python
import jax
import jax.numpy as jnp
from jax import lax
from jax.experimental import pallas as pl
from jax.experimental.pallas import tpu as pltpu
from jax.sharding import PartitionSpec as P

THETA = 1.15
DELTA = 0.85
OMEGA = 0.8
F32 = jnp.float32

NZ, NX, NY = 32, 32, 128
FULL = (NZ, NX, NY)

SIGMA = THETA / DELTA
RHO0 = 1.0 / SIGMA
RHO1 = 1.0 / (2.0 * SIGMA - RHO0)
RHO2 = 1.0 / (2.0 * SIGMA - RHO1)
RHO3 = 1.0 / (2.0 * SIGMA - RHO2)
A = (RHO1 * RHO0, RHO2 * RHO1, RHO3 * RHO2)
B = (2.0 * RHO1 / DELTA, 2.0 * RHO2 / DELTA, 2.0 * RHO3 / DELTA)

XM1 = 104
ZM1 = 104
YM1 = 40
XM2 = 80
XE2 = 77
LINES = 78
ZM2 = 88
YM2 = 56


def iota(shape, dim):
    return lax.broadcasted_iota(jnp.int32, shape, dim)


def plane():
    return iota((NX, NY), 0), iota((NX, NY), 1)


def parity(axis):
    return lax.rem(lax.axis_index(axis), 2)


def put_out(stage, even, odd, axis):
    odd_one = parity(axis)
    even[...] = stage[1 - odd_one, 0 : even.shape[0], :]
    odd[...] = stage[odd_one]


def take_in(halo, even, odd, axis):
    odd_one = parity(axis)
    halo[1 - odd_one, 0 : even.shape[0], :] = even[...]
    halo[odd_one] = odd[...]


def fourths(shape=(NX, NY)):
    return lax.rem(iota(shape, 1), 4)


def layer_lanes(z, shape=(NX, NY)):
    lane = iota(shape, 1)
    return (lane == 4 * z) | (lane == lax.rem(4 * z + NY - 1, NY))


def ends(lane):
    return (lane == 0) | (lane == NY - 1)


def shift_lanes(x, amount):
    return pltpu.roll(x, amount % NY, 1)


def columns(row_values):
    row, lane = plane()
    wide = jnp.broadcast_to(row_values, (NX, NY))
    low = jnp.sum(jnp.where(lane == 4 * row, wide, 0.0), axis=1, keepdims=True)
    high = jnp.sum(jnp.where(lane == lax.rem(4 * row + NY - 1, NY), wide, 0.0), axis=1, keepdims=True)
    return jnp.where(lane == 0, low, 0.0) + jnp.where(lane == NY - 1, high, 0.0)


def combined_row(values):
    row, lane = plane()
    low = jnp.where(lane == 4 * row, jnp.broadcast_to(values[:, 0:1], (NX, NY)), 0.0)
    high = jnp.where(lane == lax.rem(4 * row + NY - 1, NY), jnp.broadcast_to(values[:, NY - 1 :], (NX, NY)), 0.0)
    return jnp.sum(low + high, axis=0, keepdims=True)


def combine(low, high, q):
    return jnp.where(fourths(low.shape) == 0, shift_lanes(low, -q), shift_lanes(high, -q - 1))


def own_neighbours(field, g, z):
    here = field[z]
    total = g[0, z] * field[jnp.maximum(z - 1, 0)] + g[1, z] * field[jnp.minimum(z + 1, NZ - 1)]
    total += g[2, z] * pltpu.roll(here, 1, 0) + g[3, z] * pltpu.roll(here, NX - 1, 0)
    total += g[4, z] * pltpu.roll(here, 1, 1) + g[5, z] * pltpu.roll(here, NY - 1, 1)
    return total


def from_faces(z, xp, yp):
    row8 = iota((8, NY), 0)
    total = jnp.where(ends(iota((NX, NY), 1)), pltpu.roll(yp, lax.rem(NY - 4 * z, NY), 1), 0.0)
    first = total[0:8] + jnp.where(row8 == 0, xp[0, pl.ds(z, 1), :], 0.0)
    last = total[NX - 8 :] + jnp.where(row8 == 7, xp[1, pl.ds(z, 1), :], 0.0)
    return jnp.concatenate([first, total[8 : NX - 8], last], axis=0)


def from_faces_rows(z, xp, yp, side):
    rows, r = face_rows(side)
    total = jnp.where(ends(iota((8, NY), 1)), pltpu.roll(yp[rows], lax.rem(NY - 4 * z, NY), 1), 0.0)
    return total + jnp.where(iota((8, NY), 0) == r, xp[side, pl.ds(z, 1), :], 0.0)


def couplings(perm, speeds):
    total = 6.0 * perm + jnp.abs(speeds[0]) + jnp.abs(speeds[1]) + jnp.abs(speeds[2])
    inverse = 1.0 / total
    pairs = []
    for speed in speeds:
        pairs.append((perm + jnp.maximum(speed, 0.0)) * inverse)
        pairs.append((perm - jnp.minimum(speed, 0.0)) * inverse)
    return total, inverse, pairs


def face_rows(side):
    return (slice(0, 8), 0) if side == 0 else (slice(NX - 8, NX), 7)


def inner_neighbours(field, c, z, side):
    rows, _ = face_rows(side)
    lane = iota((8, NY), 1)
    here = field[z, rows, :]
    total = jnp.where(z == 0, 0.0, c[0]) * field[jnp.maximum(z - 1, 0), rows, :]
    total += jnp.where(z == NZ - 1, 0.0, c[1]) * field[jnp.minimum(z + 1, NZ - 1), rows, :]
    total += c[3 - side] * pltpu.roll(here, 7 if side == 0 else 1, 0)
    total += jnp.where(lane == 0, 0.0, c[4]) * pltpu.roll(here, 1, 1)
    total += jnp.where(lane == NY - 1, 0.0, c[5]) * pltpu.roll(here, NY - 1, 1)
    return total


def face_kernel(u_far, f_far, p_far, w_far, u, f, p, w, xp, zp, last_coupling, even, odd, z_even, z_odd, sems):
    lane8 = iota((8, NY), 1)
    copies = []
    for part in range(4):
        rows = pl.ds(8 * part, 8)
        copies.append([
            pltpu.make_async_copy(u_far.at[rows], u.at[rows], sems.at[part, 0]),
            pltpu.make_async_copy(f_far.at[rows], f.at[rows], sems.at[part, 1]),
            pltpu.make_async_copy(p_far.at[rows], p.at[rows], sems.at[part, 2]),
            pltpu.make_async_copy(w_far.at[:, rows], w.at[:, rows], sems.at[part, 3]),
        ])
    for part in range(4):
        copies[part][0].start()
    for part in range(4):
        for copy in copies[part][1:]:
            copy.start()

    def face(z, side):
        rows, _ = face_rows(side)
        half = slice(0, 16) if side == 0 else slice(NX - 16, NX)
        speeds = [w[k, z, half, :].astype(F32)[8 * side : 8 * side + 8] for k in range(3)]
        return couplings(p[z, rows, :], speeds)

    def layer(z, carry):
        edges = []
        for side in (0, 1):
            rows, r = face_rows(side)
            _, inverse, c = face(z, side)
            here = u[z, rows, :]
            res = f[z, rows, :] * inverse - here + inner_neighbours(u, c, z, side)
            for base, values in ((0, here), (NZ, res), (2 * NZ, c[2 + side])):
                xp[side, pl.ds(base + z, 1), :] = values[r : r + 1]
            merged = pltpu.roll(jnp.where(lane8 == 0, c[4], c[5]), 4 * z, 1)
            edges.append(jnp.where(layer_lanes(z, (8, NY)), merged, carry[side]))
        return tuple(edges)

    edges = (jnp.zeros((8, NY), F32),) * 2
    for part in range(4):
        copies[part][0].wait()
    for part in range(4):
        for copy in copies[part][1:]:
            copy.wait()
        edges = lax.fori_loop(8 * part, 8 * part + 8, layer, edges, unroll=8)
    for side in (0, 1):
        _, r = face_rows(side)
        for end, z in ((0, 0), (1, NZ - 1)):
            _, _, c = face(z, side)
            xp[side, 96 + end : 97 + end, :] = c[end][r : r + 1]
            xp[side, 99 + 2 * end : 100 + 2 * end, :] = jnp.where(lane8 == 0, 0.0, c[4])[r : r + 1]
            xp[side, 100 + 2 * end : 101 + 2 * end, :] = jnp.where(lane8 == NY - 1, 0.0, c[5])[r : r + 1]
        xp[side, 98:99, :] = edges[side][r : r + 1]
        _, _, c = face(1, side)
        xp[side, 103:104, :] = c[0][r : r + 1]
        _, _, c = face(NZ - 2, side)
        last_coupling[side] = jnp.broadcast_to(c[1][r : r + 1], (8, NY))
    put_out(xp, even, odd, "gx")
    row, lane = plane()
    for side, z, inner in ((0, 0, 1), (1, NZ - 1, NZ - 2)):
        here = u[z]
        _, inverse, c = couplings(p[z], [w[k, z].astype(F32) for k in range(3)])
        res = f[z] * inverse - here + c[1 - side] * u[inner]
        res += jnp.where(row == 0, 0.0, c[2]) * pltpu.roll(here, 1, 0)
        res += jnp.where(row == NX - 1, 0.0, c[3]) * pltpu.roll(here, NX - 1, 0)
        res += jnp.where(lane == 0, 0.0, c[4]) * pltpu.roll(here, 1, 1)
        res += jnp.where(lane == NY - 1, 0.0, c[5]) * pltpu.roll(here, NY - 1, 1)
        zp[side, 0:32, :] = here
        zp[side, 32:64, :] = res
        zp[side, 64:96, :] = c[side]
        zp[side, 96:97, :] = combined_row(jnp.where(lane == 0, c[4], c[5]))
        zp[side, 97:98, :] = c[2][0:1]
        zp[side, 98:99, :] = c[3][NX - 1 :]
        zp[side, 99:ZM1, :] = jnp.zeros((ZM1 - 99, NY), F32)
    put_out(zp, z_even, z_odd, "gz")


def block_kernel(u, f, p, w, g, diag, s, perm_sum, yp):
    row, lane = plane()
    perm_sum[...] = jnp.zeros_like(perm_sum)

    def layer(z, carry):
        pu, ps, pg = carry
        perm = p[z]
        total, inverse, c = couplings(perm, [w[k, z].astype(F32) for k in range(3)])
        g[0, z] = jnp.where(z == 0, 0.0, c[0])
        g[1, z] = jnp.where(z == NZ - 1, 0.0, c[1])
        g[2, z] = jnp.where(row == 0, 0.0, c[2])
        g[3, z] = jnp.where(row == NX - 1, 0.0, c[3])
        g[4, z] = jnp.where(lane == 0, 0.0, c[4])
        g[5, z] = jnp.where(lane == NY - 1, 0.0, c[5])
        diag[z] = total
        here = u[z]
        res = f[z] * inverse - here + own_neighbours(u, g, z)
        s[z] = res
        perm_sum[z // 8] += perm
        mine = layer_lanes(z)
        pu = jnp.where(mine, pltpu.roll(here, 4 * z, 1), pu)
        ps = jnp.where(mine, pltpu.roll(res, 4 * z, 1), ps)
        pg = jnp.where(mine, pltpu.roll(jnp.where(lane == 0, c[4], c[5]), 4 * z, 1), pg)
        return pu, ps, pg

    zero = jnp.zeros((NX, NY), F32)
    pu, ps, pg = lax.fori_loop(0, NZ, layer, (zero, zero, zero), unroll=8)
    yp[0:32, :] = pu
    yp[32:64, :] = ps
    yp[64:96, :] = pg


def z_part(stage, faces, xp, xh):
    row, _ = plane()
    row8 = iota((8, NY), 0)
    all_lines = []
    for side, z in ((0, 0), (1, NZ - 1)):
        res = faces[side, 32:64, :]
        lines = jnp.zeros((8, NY), F32)
        for end, at in ((0, 0), (1, NX - 1)):
            line = xh[end, z : z + 1, :]
            res += jnp.where(row == at, xp[end, 64 + z : 65 + z, :] * line, 0.0)
            lines = jnp.where(row8 == end, line, lines)
        stage[side, 0:32, :] = faces[side, 0:32, :]
        stage[side, 32:64, :] = res
        all_lines.append(lines)
    return all_lines


def y_part(field, res, coupling, zp, zh, xp, xh):
    row, lane = plane()
    row8 = iota((8, NY), 0)
    z_lines = [zh[end, 0:32, :] for end in (0, 1)]
    res += jnp.where(ends(lane), zp[0, 64:96, :] * z_lines[0], 0.0)
    last = 4 * (NZ - 1)
    res += jnp.where(layer_lanes(NZ - 1), pltpu.roll(zp[1, 64:96, :] * z_lines[1], last, 1), 0.0)
    x_lines = jnp.zeros((8, NY), F32)
    for end, at in ((0, 0), (1, NX - 1)):
        line = xh[end, 0:32, :]
        res += jnp.where(row == at, combined_row(xp[end, 64:96, :] * line), 0.0)
        x_lines = jnp.where(row8 == end, combined_row(line), x_lines)
    messages = []
    q = fourths()
    for side in (0, 1):
        body = jnp.where(q == 0, shift_lanes(field, side), shift_lanes(res, 1 + side))
        if coupling is not None:
            body = jnp.where(q == 2, shift_lanes(coupling, 2 + side), body)
        for end in (0, 1):
            at = 3 + 4 * end
            body = jnp.where(lane == at, shift_lanes(z_lines[end], at + side), body)
        messages.append((body, shift_lanes(x_lines, side)))
    return messages


def first_y_kernel(
    xodd, zeven, zodd, xeven, xp, zp, yp,
    xh, zh, even, odd,
    stage,
):
    take_in(xh, xeven, xodd, "gx")
    take_in(zh, zeven, zodd, "gz")
    messages = y_part(yp[0:32, :], yp[32:64, :], yp[64:96, :], zp, zh, xp, xh)
    for side in (0, 1):
        stage[side, 0:32, :], stage[side, 32:40, :] = messages[side]
    put_out(stage, even, odd, "gy")


def z_halo_residual(side, res, zh1, yh, mine):
    _, lane = plane()
    at = 3 + 4 * side
    low, high = yh[0, 0:32, at : at + 1], yh[1, 0:32, at : at + 1]
    corner = jnp.where(lane == 0, low, 0.0) + jnp.where(lane == NY - 1, high, 0.0)
    return res + zh1[side, 64:96, :] * mine + columns(zh1[side, 96:97, :]) * corner


def x_halo_residual(side, res, xh1, zh, lines, yh, mine):
    row, _ = plane()
    total = res + xh1[side, 64:96, :] * mine
    if zh is not None:
        for end, at in ((0, 0), (1, NZ - 1)):
            total += jnp.where(row == at, xh1[side, 96 + end : 97 + end, :] * zh[end, lines + side : lines + side + 1, :], 0.0)
    corner = combine(yh[0, 32 + side : 33 + side, :], yh[1, 32 + side : 33 + side, :], 0)
    return total + columns(xh1[side, 98:99, :] * corner)


def group_sums(x):
    return jnp.sum(x.reshape(4, 8, NY), axis=1)


def exact_dot(a, b):
    return jnp.dot(a, b, precision=lax.Precision.HIGHEST, preferred_element_type=F32)


def second_kernel(
    u, g, diag, s1, perm_sum, zp, yp, xp, last_coupling, xh, zh, yodd, yeven,
    yh, s0, d0, b, xp2, cross2, zy2, even, odd, line_even, line_odd,
    cross, rsum, rows, edge_s, edge_d, stage, lines,
):
    take_in(yh, yeven, yodd, "gy")
    scale = 1.0 / THETA
    low, high = yh[0, 0:32, :], yh[1, 0:32, :]
    own_y = yp[64:96, :]
    yq = own_y * combine(low, high, 0)
    yq2 = own_y * (scale * (combine(low, high, 1) + combine(low, high, 2) * yp[0:32, :]))
    zy2[2] = yq2
    zq = []
    for side, z in ((0, 0), (1, NZ - 1)):
        zq.append(zp[side, 64:96, :] * zh[side, 0:32, :])
        zy2[side] = zp[side, 64:96, :] * (scale * z_halo_residual(side, zh[side, 32:64, :], zh, yh, u[z]))
        gx = xp[side, 64:96, :]
        cross[side] = gx * xh[side, 0:32, :]
        cross2[side] = gx * (scale * x_halo_residual(side, xh[side, 32:64, :], xh, None, 0, yh, xp[side, 0:32, :]))
    rsum[...] = jnp.zeros_like(rsum)

    def start(z, carry):
        res = s1[z] + from_faces(z, cross, yq)
        s0[z] = res
        d0[z] = res * scale
        rsum[z // 8] += res * diag[z]
        return carry

    lax.fori_loop(0, NZ, start, 0, unroll=32)
    for side, z in ((0, 0), (1, NZ - 1)):
        s0[z] += zq[side]
        d0[z] += zq[side] * scale
        rsum[z // 8] += zq[side] * diag[z]
    for block in range(4):
        rows[0, 4 * block : 4 * block + 4, :] = group_sums(rsum[block])
        rows[1, 4 * block : 4 * block + 4, :] = group_sums(perm_sum[block])
    select = jnp.where(iota((NY, NY), 0) // 8 == iota((NY, NY), 1), 1.0, 0.0)
    lane16 = iota((16, NY), 1)
    weights = jnp.where(lane16 < 16, exact_dot(rows[1], select), 1.0)
    rhs = jnp.where(lane16 < 16, (OMEGA * 8.0 / 6.0) * exact_dot(rows[0], select) / weights, 0.0)
    b[...] = rhs

    def edge(z, carry):
        for side in (0, 1):
            at, _ = face_rows(side)
            before = d0[z, at, :]
            near = edge_neighbours(lambda k: d0[k, at, :], [g[k, z, at, :] for k in range(6)], z)
            res = s0[z, at, :] - before + near + from_faces_rows(z, cross2, yq2, side)
            edge_s[side, z] = res
            edge_d[side, z] = A[0] * before + B[0] * res
        return carry

    lax.fori_loop(0, NZ, edge, 0, unroll=32)
    for side in (0, 1):
        at, _ = face_rows(side)
        for end, z in ((0, 0), (1, NZ - 1)):
            edge_s[side, z] += zy2[end, at, :]
            edge_d[side, z] += B[0] * zy2[end, at, :]

    def face(z, carry):
        for side in (0, 1):
            at, r = face_rows(side)
            here = edge_d[side, z]
            near = edge_neighbours(lambda k: edge_d[side, k], [g[k, z, at, :] for k in range(6)], z)
            res = edge_s[side, z] - here + near
            xp2[side, pl.ds(z, 1), :] = here[r : r + 1]
            xp2[side, pl.ds(NZ + z, 1), :] = res[r : r + 1]
        return carry

    lax.fori_loop(0, NZ, face, 0, unroll=32)
    for side in (0, 1):
        stage[side, 0:64, :] = xp2[side]
        for z in range(4):
            stage[side, 64 + 3 * z : 67 + 3 * z, :] = rhs[4 * z + side : 4 * z + side + 3]
        stage[side, 76:80, :] = last_coupling[side, 0:4, :]
    put_out(stage, even, odd, "gx")
    for side, z in ((0, 0), (1, NZ - 1)):
        for end in (0, 1):
            lines[side, end : end + 1, :] = xh[end, z : z + 1, :]
            lines[side, 2 + end : 3 + end, :] = xh[end, 64 + z : 65 + z, :]
        lines[side, 4:LINES, :] = jnp.zeros((LINES - 4, NY), F32)
    put_out(lines, line_even, line_odd, "gz")


def edge_neighbours(rows_of, g, z):
    here = rows_of(z)
    total = g[0] * rows_of(jnp.maximum(z - 1, 0)) + g[1] * rows_of(jnp.minimum(z + 1, NZ - 1))
    total += g[2] * pltpu.roll(here, 1, 0) + g[3] * pltpu.roll(here, 7, 0)
    return total + g[4] * pltpu.roll(here, 1, 1) + g[5] * pltpu.roll(here, NY - 1, 1)


def edge_change(coupling_x, edge_z, coupling_z, edge_x, corner):
    return (coupling_x * edge_z + coupling_z * edge_x) * corner * (1.0 / THETA)


def second_block_kernel(
    u, g, s0, d0, cross2, zy2, xp, xp2, zp, xh, zh, line_even, line_odd,
    s, d, acc, zp2, yp2, xm, lh,
    s1,
):
    yq2 = zy2[2]

    def step(z, carry):
        before = d0[z]
        res = s0[z] - before + own_neighbours(d0, g, z) + from_faces(z, cross2, yq2)
        after = A[0] * before + B[0] * res
        s1[z] = res
        d[z] = after
        acc[z] = u[z] + before + after
        return carry

    lax.fori_loop(0, NZ, step, 0, unroll=32)
    for side, z in ((0, 0), (1, NZ - 1)):
        s1[z] += zy2[side]
        d[z] += B[0] * zy2[side]
        acc[z] += B[0] * zy2[side]
    take_in(lh, line_even, line_odd, "gz")
    xm[...] = xp2[:, 0:32, :]
    for end, z in ((0, 0), (1, NZ - 1)):
        for side, x in ((0, 0), (1, NX - 1)):
            change = edge_change(
                xp[side, 64 + z : 65 + z, :], xh[side, 96 + end : 97 + end, :],
                zp[end, 64 + x : 65 + x, :], zh[end, 97 + side : 98 + side, :],
                lh[end, side : side + 1, :],
            )
            s1[z, x : x + 1, :] += change
            d[z, x : x + 1, :] += B[0] * change
            acc[z, x : x + 1, :] += B[0] * change
            xm[side, z : z + 1, :] += B[0] * change

    def partial(z, carry):
        pu, ps = carry
        here = d[z]
        res = s1[z] - here + own_neighbours(d, g, z)
        s[z] = res
        mine = layer_lanes(z)
        return jnp.where(mine, pltpu.roll(here, 4 * z, 1), pu), jnp.where(mine, pltpu.roll(res, 4 * z, 1), ps)

    zero = jnp.zeros((NX, NY), F32)
    pu, ps = lax.fori_loop(0, NZ, partial, (zero, zero), unroll=8)
    yp2[0:32, :] = pu
    yp2[32:64, :] = ps
    for side, z in ((0, 0), (1, NZ - 1)):
        zp2[side, 0:32, :] = d[z]
        zp2[side, 32:64, :] = s[z]


def second_z_kernel(xodd, xeven, xp, zp, zp2, b, xh, zh, lh, xh2, even, odd, b3, stage, rows):
    take_in(xh2, xeven, xodd, "gx")
    for side, x in ((0, 0), (1, NX - 1)):
        for end, z, inner in ((0, 0, 1), (1, NZ - 1, NZ - 2)):
            change = edge_change(
                xh[side, 64 + z : 65 + z, :], zp[end, 64 + x : 65 + x, :],
                xh[side, 96 + end : 97 + end, :], lh[end, 2 + side : 3 + side, :],
                zh[end, x : x + 1, :],
            )
            turn = B[0] * change
            at = 99 + 2 * end
            beside = xh[side, at : at + 1, :] * pltpu.roll(turn, 1, 1) + xh[side, at + 1 : at + 2, :] * pltpu.roll(turn, NY - 1, 1)
            inward = xh[side, 103:104, :] if end == 0 else xh2[side, 76:77, :]
            xh2[side, z : z + 1, :] += turn
            xh2[side, 32 + z : 33 + z, :] += change - turn + beside
            xh2[side, 32 + inner : 33 + inner, :] += inward * turn
    lines = z_part(stage, zp2, xp, xh2)
    lane16 = iota((16, NY), 1)
    wide = b[...]
    for end in (0, 1):
        first = 1 - end
        rows[...] = jnp.zeros_like(rows)
        for z in range(4):
            rows[4 * z + first : 4 * z + first + 3, :] = xh2[end, 64 + 3 * z : 67 + 3 * z, :]
        base = 32 * (end + 1)
        wide = jnp.where((lane16 >= base) & (lane16 < base + 16), pltpu.roll(rows[...], base, 1), wide)
    b3[...] = wide
    for side in (0, 1):
        stage[side, 64:72, :] = lines[side]
        stage[side, 72:88, :] = wide
    put_out(stage, even, odd, "gz")


def second_y_kernel(zeven, zodd, xp, zp, yp2, xh2, b3, zh2, even, odd, stage):
    take_in(zh2, zeven, zodd, "gz")
    messages = y_part(yp2[0:32, :], yp2[32:64, :], None, zp, zh2, xp, xh2)
    within = lax.rem(iota((16, NY), 1), 32)
    parts = (b3[...], zh2[0, 72:88, :], zh2[1, 72:88, :])
    for side in (0, 1):
        stage[side, 0:32, :], stage[side, 32:40, :] = messages[side]
        coarse = jnp.zeros((16, NY), F32)
        for k in range(3):
            at = 4 * k
            moved = shift_lanes(parts[k], at - 13 * side)
            coarse = jnp.where((within >= at) & (within < at + 3), moved, coarse)
        stage[side, 40:56, :] = coarse
    put_out(stage, even, odd, "gy")


def coarse_solve(b3, zh2, yh2, ext, err, spread):
    ext[...] = jnp.zeros_like(ext)
    lane4 = iota((4, NY), 1)
    within = lax.rem(iota((16, NY), 1), 32)
    wide = []
    for k, part in enumerate((b3[...], zh2[0, 72:88, :], zh2[1, 72:88, :])):
        full = jnp.where((within >= 3) & (within < 19), shift_lanes(part, 3), 0.0)
        full = jnp.where(within < 3, shift_lanes(yh2[0, 40:56, :], -4 * k), full)
        wide.append(jnp.where((within >= 19) & (within < 22), shift_lanes(yh2[1, 40:56, :], 19 - 4 * k), full))

    for z in range(10):
        values, at = (wide[1], 4 * (z + 1)) if z < 3 else (wide[0], 4 * (z - 3)) if z < 7 else (wide[2], 4 * (z - 7))
        four = values[at : at + 4]
        own, low, high = [jnp.where(lane4 < 22, shift_lanes(four, -32 * k), 0.0) for k in range(3)]
        ext[z, 0:3, :] = low[1:4]
        ext[z, 3:7, :] = own
        ext[z, 7:10, :] = high[0:3]
    x, y = iota((16, NY), 0), iota((16, NY), 1)
    at_z, at_x, at_y = lax.axis_index("gz"), lax.axis_index("gx"), lax.axis_index("gy")
    last_z, last_x, last_y = lax.axis_size("gz") - 1, lax.axis_size("gx") - 1, lax.axis_size("gy") - 1
    inside = (x < 10) & (y < 22)
    inside &= ((x >= 3) | (at_x > 0)) & ((x < 7) | (at_x < last_x))
    inside &= ((y >= 3) | (at_y > 0)) & ((y < 19) | (at_y < last_y))
    keep = jnp.where(inside, 1.0, 0.0)
    keep_low = jnp.where(at_z > 0, keep, 0.0)
    keep_high = jnp.where(at_z < last_z, keep, 0.0)
    rhs = [ext[z] for z in range(10)]
    e = rhs
    for sweep in range(3):
        lo, hi = sweep + 1, 9 - sweep
        new = []
        for z in range(10):
            if z < lo or z >= hi:
                new.append(e[z])
                continue
            c = e[z]
            beside = e[z - 1] + e[z + 1] + pltpu.roll(c, 1, 0) + pltpu.roll(c, 15, 0) + pltpu.roll(c, 1, 1) + pltpu.roll(c, NY - 1, 1)
            v = (1.0 - OMEGA) * c + (OMEGA / 6.0) * beside + rhs[z]
            new.append(v * (keep_low if z < 3 else keep_high if z >= 7 else keep))
        e = new
    for z in range(4):
        err[4 * z : 4 * z + 4, :] = e[z + 3][3:7]
    select = jnp.where(iota((NY, NY), 0) == iota((NY, NY), 1) // 8 + 3, 1.0, 0.0)
    fine = exact_dot(err[...], select)
    for z in range(4):
        spread[z] = jnp.broadcast_to(fine[4 * z : 4 * z + 4][:, None, :], (4, 8, NY)).reshape(NX, NY)


def third_kernel(
    g, s2, d1, acc, zp, yp, xp, xh, zh, yh, xm, zp2, yp2, xh2, zh2, b3, yodd, yeven,
    far_out,
    yh2, s, d, cross, cross2, ext, err, spread, out, sems,
):
    take_in(yh2, yeven, yodd, "gy")
    low, high = yh2[0, 0:32, :], yh2[1, 0:32, :]
    own_y = yp[64:96, :]
    yu = combine(low, high, 0)
    yq = own_y * yu
    yq2 = own_y * (A[1] * yu + B[1] * (combine(low, high, 1) + combine(yh[0, 0:32, :], yh[1, 0:32, :], 2) * yp2[0:32, :]))
    zq, zq2 = [], []
    for side, z in ((0, 0), (1, NZ - 1)):
        zu, xu = zh2[side, 0:32, :], xh2[side, 0:32, :]
        zq.append(zp[side, 64:96, :] * zu)
        dz = A[1] * zu + B[1] * z_halo_residual(side, zh2[side, 32:64, :], zh, yh2, zp2[side, 0:32, :])
        zq2.append(zp[side, 64:96, :] * dz)
        gx = xp[side, 64:96, :]
        cross[side] = gx * xu
        dx = A[1] * xu + B[1] * x_halo_residual(side, xh2[side, 32:64, :], xh, zh2, 64, yh2, xm[side])
        cross2[side] = gx * dx
    coarse_solve(b3, zh2, yh2, ext, err, spread)

    def step(z, carry):
        res = s2[z] + from_faces(z, cross, yq)
        s[z] = res
        d[z] = A[1] * d1[z] + B[1] * res
        return carry

    lax.fori_loop(0, NZ, step, 0, unroll=32)
    for side, z in ((0, 0), (1, NZ - 1)):
        s[z] += zq[side]
        d[z] += B[1] * zq[side]

    def finish(z, carry):
        before = d[z]
        res = s[z] - before + own_neighbours(d, g, z) + from_faces(z, cross2, yq2)
        out[z] = acc[z] + before + (A[2] * before + B[2] * res) + spread[z // 8]
        return carry

    copies = []
    for part in range(4):
        lax.fori_loop(8 * part, 8 * part + 8, finish, 0, unroll=8)
        if part == 0:
            out[0] += B[2] * zq2[0]
        if part == 3:
            out[NZ - 1] += B[2] * zq2[1]
        rows = pl.ds(8 * part, 8)
        copies.append(pltpu.make_async_copy(out.at[rows], far_out.at[rows], sems.at[part]))
        copies[part].start()
    for copy in copies:
        copy.wait()


VM = pl.BlockSpec(memory_space=pltpu.VMEM)
HBM = pl.BlockSpec(memory_space=pltpu.HBM)
BF16_FIELD = jax.ShapeDtypeStruct((3,) + FULL, jnp.bfloat16)


def call(kernel, name, n_in, outs, scratch=(), us=0.2, place=VM, more=(), results=VM):
    return pl.pallas_call(
        kernel,
        out_shape=[x if isinstance(x, jax.ShapeDtypeStruct) else jax.ShapeDtypeStruct(x, F32) for x in outs],
        in_specs=[place] * n_in,
        out_specs=[results] * len(outs),
        scratch_shapes=[pltpu.VMEM(shape, F32) for shape in scratch] + list(more),
        compiler_params=pltpu.CompilerParams(vmem_limit_bytes=32 * 2**20),
        cost_estimate=pl.CostEstimate(flops=0, transcendentals=0, bytes_accessed=int(us * 3e6)),
        name=name,
    )


def swap(even, odd, axis):
    count = lax.axis_size(axis)
    results = []
    for first, values in ((1, odd), (0, even)):
        pairs = []
        for i in range(first, count - 1, 2):
            pairs += [(i, i + 1), (i + 1, i)]
        results.append(lax.ppermute(values, axis, pairs))
    return results[::-1]


def per_device(u, f, p, w):
    face = (2, 32, NY)
    far = [pltpu.with_memory_space_constraint(x, pltpu.HBM) for x in (u, f, p, w)]
    u, f, p, w, xp, zp, last_coupling, even, odd, zeven, zodd = call(
        face_kernel, "faces", 4,
        [FULL, FULL, FULL, BF16_FIELD, (2, XM1, NY), (2, ZM1, NY), (2, 8, NY), (XM1, NY), (XM1, NY), (ZM1, NY), (ZM1, NY)],
        (), 2.0, HBM, [pltpu.SemaphoreType.DMA((4, 4))],
    )(*far)
    g, diag, s, perm_sum, yp = call(
        block_kernel, "block", 4, [(6,) + FULL, FULL, FULL, (4, NX, NY), (96, NY)], (), 2.5
    )(u, f, p, w)
    even, odd = swap(even, odd, "gx")
    zeven, zodd = swap(zeven, zodd, "gz")
    xh, zh, yeven, yodd = call(
        first_y_kernel, "y_message", 7,
        [(2, XM1, NY), (2, ZM1, NY), (YM1, NY), (YM1, NY)],
        [(2, YM1, NY)],
    )(odd, zeven, zodd, even, xp, zp, yp)
    yeven, yodd = swap(yeven, yodd, "gy")
    yh, s, d, b, xp2, cross2, zy2, even, odd, line_even, line_odd = call(
        second_kernel, "two_steps", 13,
        [(2, YM1, NY), FULL, FULL, (16, NY), (2, 64, NY), face, (3, NX, NY), (XE2, NY), (XM2, NY), (LINES, NY), (LINES, NY)],
        [face, (4, NX, NY), (2, 16, NY), (2, NZ, 8, NY), (2, NZ, 8, NY), (2, XM2, NY), (2, LINES, NY)], 1.5,
    )(u, g, diag, s, perm_sum, zp, yp, xp, last_coupling, xh, zh, yodd, yeven)
    even, odd = swap(even, odd, "gx")
    line_even, line_odd = swap(line_even, line_odd, "gz")
    s, d1, acc, zp2, yp2, xm, lh = call(
        second_block_kernel, "block_2", 13, [FULL, FULL, FULL, (2, 64, NY), (64, NY), face, (2, LINES, NY)], [FULL], 0.01
    )(u, g, s, d, cross2, zy2, xp, xp2, zp, xh, zh, line_even, line_odd)
    xh2, even, odd, b3 = call(
        second_z_kernel, "z_message_2", 9, [(2, XM2, NY), (ZM2, NY), (ZM2, NY), (16, NY)], [(2, ZM2, NY), (16, NY)]
    )(odd, even, xp, zp, zp2, b, xh, zh, lh)
    even, odd = swap(even, odd, "gz")
    zh2, even, odd = call(
        second_y_kernel, "y_message_2", 7, [(2, ZM2, NY), (YM2, NY), (YM2, NY)], [(2, YM2, NY)]
    )(even, odd, xp, zp, yp2, xh2, b3)
    even, odd = swap(even, odd, "gy")
    (out,) = call(
        third_kernel, "last_steps", 18, [FULL],
        [(2, YM2, NY), FULL, FULL, face, face, (10, 16, NY), (16, NY), (4, NX, NY), FULL], 2.5, VM,
        [pltpu.SemaphoreType.DMA((4,))], HBM,
    )(g, s, d1, acc, zp, yp, xp, xh, zh, yh, xm, zp2, yp2, xh2, zh2, b3, odd, even)
    return out


def solution(mesh):
    placed = (
        P("gz", "gx", "gy"),
        P("gz", "gx", "gy"),
        P("gz", "gx", "gy"),
        P(None, "gz", "gx", "gy"),
    )
    return jax.shard_map(
        per_device, mesh=mesh, in_specs=placed, out_specs=P("gz", "gx", "gy"), check_vma=False
    )
```

```python
import jax
import jax.numpy as jnp
from jax import lax
from jax.experimental import pallas as pl
from jax.experimental.pallas import tpu as pltpu
from jax.sharding import PartitionSpec as P

THETA = 1.15
DELTA = 0.85
OMEGA = 0.8
F32 = jnp.float32

NZ, NX, NY = 32, 32, 128
FULL = (NZ, NX, NY)

SIGMA = THETA / DELTA
RHO0 = 1.0 / SIGMA
RHO1 = 1.0 / (2.0 * SIGMA - RHO0)
RHO2 = 1.0 / (2.0 * SIGMA - RHO1)
RHO3 = 1.0 / (2.0 * SIGMA - RHO2)
A = (RHO1 * RHO0, RHO2 * RHO1, RHO3 * RHO2)
B = (2.0 * RHO1 / DELTA, 2.0 * RHO2 / DELTA, 2.0 * RHO3 / DELTA)

XM1 = 104
ZM1 = 104
YM1 = 40
XM2 = 80
XE2 = 77
LINES = 78
ZM2 = 88
YM2 = 56


def iota(shape, dim):
    return lax.broadcasted_iota(jnp.int32, shape, dim)


def plane():
    return iota((NX, NY), 0), iota((NX, NY), 1)


def parity(axis):
    return lax.rem(lax.axis_index(axis), 2)


def put_out(stage, even, odd, axis):
    odd_one = parity(axis)
    even[...] = stage[1 - odd_one, 0 : even.shape[0], :]
    odd[...] = stage[odd_one]


def take_in(halo, even, odd, axis):
    odd_one = parity(axis)
    halo[1 - odd_one, 0 : even.shape[0], :] = even[...]
    halo[odd_one] = odd[...]


def fourths(shape=(NX, NY)):
    return lax.rem(iota(shape, 1), 4)


def layer_lanes(z, shape=(NX, NY)):
    lane = iota(shape, 1)
    return (lane == 4 * z) | (lane == lax.rem(4 * z + NY - 1, NY))


def ends(lane):
    return (lane == 0) | (lane == NY - 1)


def shift_lanes(x, amount):
    return pltpu.roll(x, amount % NY, 1)


def columns(row_values):
    row, lane = plane()
    wide = jnp.broadcast_to(row_values, (NX, NY))
    low = jnp.sum(jnp.where(lane == 4 * row, wide, 0.0), axis=1, keepdims=True)
    high = jnp.sum(jnp.where(lane == lax.rem(4 * row + NY - 1, NY), wide, 0.0), axis=1, keepdims=True)
    return jnp.where(lane == 0, low, 0.0) + jnp.where(lane == NY - 1, high, 0.0)


def combined_row(values):
    row, lane = plane()
    low = jnp.where(lane == 4 * row, jnp.broadcast_to(values[:, 0:1], (NX, NY)), 0.0)
    high = jnp.where(lane == lax.rem(4 * row + NY - 1, NY), jnp.broadcast_to(values[:, NY - 1 :], (NX, NY)), 0.0)
    return jnp.sum(low + high, axis=0, keepdims=True)


def combine(low, high, q):
    return jnp.where(fourths(low.shape) == 0, shift_lanes(low, -q), shift_lanes(high, -q - 1))


def own_neighbours(field, g, z):
    here = field[z]
    total = g[0, z] * field[jnp.maximum(z - 1, 0)] + g[1, z] * field[jnp.minimum(z + 1, NZ - 1)]
    total += g[2, z] * pltpu.roll(here, 1, 0) + g[3, z] * pltpu.roll(here, NX - 1, 0)
    total += g[4, z] * pltpu.roll(here, 1, 1) + g[5, z] * pltpu.roll(here, NY - 1, 1)
    return total


def from_faces(z, xp, yp):
    row8 = iota((8, NY), 0)
    total = jnp.where(ends(iota((NX, NY), 1)), pltpu.roll(yp, lax.rem(NY - 4 * z, NY), 1), 0.0)
    first = total[0:8] + jnp.where(row8 == 0, xp[0, pl.ds(z, 1), :], 0.0)
    last = total[NX - 8 :] + jnp.where(row8 == 7, xp[1, pl.ds(z, 1), :], 0.0)
    return jnp.concatenate([first, total[8 : NX - 8], last], axis=0)


def from_faces_rows(z, xp, yp, side):
    rows, r = face_rows(side)
    total = jnp.where(ends(iota((8, NY), 1)), pltpu.roll(yp[rows], lax.rem(NY - 4 * z, NY), 1), 0.0)
    return total + jnp.where(iota((8, NY), 0) == r, xp[side, pl.ds(z, 1), :], 0.0)


def couplings(perm, speeds):
    total = 6.0 * perm + jnp.abs(speeds[0]) + jnp.abs(speeds[1]) + jnp.abs(speeds[2])
    inverse = 1.0 / total
    pairs = []
    for speed in speeds:
        pairs.append((perm + jnp.maximum(speed, 0.0)) * inverse)
        pairs.append((perm - jnp.minimum(speed, 0.0)) * inverse)
    return total, inverse, pairs


def face_rows(side):
    return (slice(0, 8), 0) if side == 0 else (slice(NX - 8, NX), 7)


def inner_neighbours(field, c, z, side):
    rows, _ = face_rows(side)
    lane = iota((8, NY), 1)
    here = field[z, rows, :]
    total = jnp.where(z == 0, 0.0, c[0]) * field[jnp.maximum(z - 1, 0), rows, :]
    total += jnp.where(z == NZ - 1, 0.0, c[1]) * field[jnp.minimum(z + 1, NZ - 1), rows, :]
    total += c[3 - side] * pltpu.roll(here, 7 if side == 0 else 1, 0)
    total += jnp.where(lane == 0, 0.0, c[4]) * pltpu.roll(here, 1, 1)
    total += jnp.where(lane == NY - 1, 0.0, c[5]) * pltpu.roll(here, NY - 1, 1)
    return total


def face_kernel(u_far, f_far, p_far, w_far, u, f, p, w, xp, zp, last_coupling, even, odd, z_even, z_odd, sems):
    lane8 = iota((8, NY), 1)
    copies = []
    for part in range(4):
        rows = pl.ds(8 * part, 8)
        copies.append([
            pltpu.make_async_copy(u_far.at[rows], u.at[rows], sems.at[part, 0]),
            pltpu.make_async_copy(f_far.at[rows], f.at[rows], sems.at[part, 1]),
            pltpu.make_async_copy(p_far.at[rows], p.at[rows], sems.at[part, 2]),
            pltpu.make_async_copy(w_far.at[:, rows], w.at[:, rows], sems.at[part, 3]),
        ])
    for part in range(4):
        copies[part][0].start()
    for part in range(4):
        for copy in copies[part][1:]:
            copy.start()

    def face(z, side):
        rows, _ = face_rows(side)
        half = slice(0, 16) if side == 0 else slice(NX - 16, NX)
        speeds = [w[k, z, half, :].astype(F32)[8 * side : 8 * side + 8] for k in range(3)]
        return couplings(p[z, rows, :], speeds)

    def layer(z, carry):
        edges = []
        for side in (0, 1):
            rows, r = face_rows(side)
            _, inverse, c = face(z, side)
            here = u[z, rows, :]
            res = f[z, rows, :] * inverse - here + inner_neighbours(u, c, z, side)
            for base, values in ((0, here), (NZ, res), (2 * NZ, c[2 + side])):
                xp[side, pl.ds(base + z, 1), :] = values[r : r + 1]
            merged = pltpu.roll(jnp.where(lane8 == 0, c[4], c[5]), 4 * z, 1)
            edges.append(jnp.where(layer_lanes(z, (8, NY)), merged, carry[side]))
        return tuple(edges)

    edges = (jnp.zeros((8, NY), F32),) * 2
    for part in range(4):
        copies[part][0].wait()
    for part in range(4):
        for copy in copies[part][1:]:
            copy.wait()
        edges = lax.fori_loop(8 * part, 8 * part + 8, layer, edges, unroll=8)
    for side in (0, 1):
        _, r = face_rows(side)
        for end, z in ((0, 0), (1, NZ - 1)):
            _, _, c = face(z, side)
            xp[side, 96 + end : 97 + end, :] = c[end][r : r + 1]
            xp[side, 99 + 2 * end : 100 + 2 * end, :] = jnp.where(lane8 == 0, 0.0, c[4])[r : r + 1]
            xp[side, 100 + 2 * end : 101 + 2 * end, :] = jnp.where(lane8 == NY - 1, 0.0, c[5])[r : r + 1]
        xp[side, 98:99, :] = edges[side][r : r + 1]
        _, _, c = face(1, side)
        xp[side, 103:104, :] = c[0][r : r + 1]
        _, _, c = face(NZ - 2, side)
        last_coupling[side] = jnp.broadcast_to(c[1][r : r + 1], (8, NY))
    put_out(xp, even, odd, "gx")
    row, lane = plane()
    for side, z, inner in ((0, 0, 1), (1, NZ - 1, NZ - 2)):
        here = u[z]
        _, inverse, c = couplings(p[z], [w[k, z].astype(F32) for k in range(3)])
        res = f[z] * inverse - here + c[1 - side] * u[inner]
        res += jnp.where(row == 0, 0.0, c[2]) * pltpu.roll(here, 1, 0)
        res += jnp.where(row == NX - 1, 0.0, c[3]) * pltpu.roll(here, NX - 1, 0)
        res += jnp.where(lane == 0, 0.0, c[4]) * pltpu.roll(here, 1, 1)
        res += jnp.where(lane == NY - 1, 0.0, c[5]) * pltpu.roll(here, NY - 1, 1)
        zp[side, 0:32, :] = here
        zp[side, 32:64, :] = res
        zp[side, 64:96, :] = c[side]
        zp[side, 96:97, :] = combined_row(jnp.where(lane == 0, c[4], c[5]))
        zp[side, 97:98, :] = c[2][0:1]
        zp[side, 98:99, :] = c[3][NX - 1 :]
        zp[side, 99:ZM1, :] = jnp.zeros((ZM1 - 99, NY), F32)
    put_out(zp, z_even, z_odd, "gz")


def block_kernel(u, f, p, w, g, diag, s, perm_sum, yp):
    row, lane = plane()
    perm_sum[...] = jnp.zeros_like(perm_sum)

    def layer(z, carry):
        pu, ps, pg = carry
        perm = p[z]
        total, inverse, c = couplings(perm, [w[k, z].astype(F32) for k in range(3)])
        g[0, z] = jnp.where(z == 0, 0.0, c[0])
        g[1, z] = jnp.where(z == NZ - 1, 0.0, c[1])
        g[2, z] = jnp.where(row == 0, 0.0, c[2])
        g[3, z] = jnp.where(row == NX - 1, 0.0, c[3])
        g[4, z] = jnp.where(lane == 0, 0.0, c[4])
        g[5, z] = jnp.where(lane == NY - 1, 0.0, c[5])
        diag[z] = total
        here = u[z]
        res = f[z] * inverse - here + own_neighbours(u, g, z)
        s[z] = res
        perm_sum[z // 8] += perm
        mine = layer_lanes(z)
        pu = jnp.where(mine, pltpu.roll(here, 4 * z, 1), pu)
        ps = jnp.where(mine, pltpu.roll(res, 4 * z, 1), ps)
        pg = jnp.where(mine, pltpu.roll(jnp.where(lane == 0, c[4], c[5]), 4 * z, 1), pg)
        return pu, ps, pg

    zero = jnp.zeros((NX, NY), F32)
    pu, ps, pg = lax.fori_loop(0, NZ, layer, (zero, zero, zero), unroll=8)
    yp[0:32, :] = pu
    yp[32:64, :] = ps
    yp[64:96, :] = pg


def z_part(stage, faces, xp, xh):
    row, _ = plane()
    row8 = iota((8, NY), 0)
    all_lines = []
    for side, z in ((0, 0), (1, NZ - 1)):
        res = faces[side, 32:64, :]
        lines = jnp.zeros((8, NY), F32)
        for end, at in ((0, 0), (1, NX - 1)):
            line = xh[end, z : z + 1, :]
            res += jnp.where(row == at, xp[end, 64 + z : 65 + z, :] * line, 0.0)
            lines = jnp.where(row8 == end, line, lines)
        stage[side, 0:32, :] = faces[side, 0:32, :]
        stage[side, 32:64, :] = res
        all_lines.append(lines)
    return all_lines


def y_part(field, res, coupling, zp, zh, xp, xh):
    row, lane = plane()
    row8 = iota((8, NY), 0)
    z_lines = [zh[end, 0:32, :] for end in (0, 1)]
    res += jnp.where(ends(lane), zp[0, 64:96, :] * z_lines[0], 0.0)
    last = 4 * (NZ - 1)
    res += jnp.where(layer_lanes(NZ - 1), pltpu.roll(zp[1, 64:96, :] * z_lines[1], last, 1), 0.0)
    x_lines = jnp.zeros((8, NY), F32)
    for end, at in ((0, 0), (1, NX - 1)):
        line = xh[end, 0:32, :]
        res += jnp.where(row == at, combined_row(xp[end, 64:96, :] * line), 0.0)
        x_lines = jnp.where(row8 == end, combined_row(line), x_lines)
    messages = []
    q = fourths()
    for side in (0, 1):
        body = jnp.where(q == 0, shift_lanes(field, side), shift_lanes(res, 1 + side))
        if coupling is not None:
            body = jnp.where(q == 2, shift_lanes(coupling, 2 + side), body)
        for end in (0, 1):
            at = 3 + 4 * end
            body = jnp.where(lane == at, shift_lanes(z_lines[end], at + side), body)
        messages.append((body, shift_lanes(x_lines, side)))
    return messages


def first_y_kernel(
    xodd, zodd, zeven, xeven, xp, zp, yp,
    xh, zh, even, odd,
    stage,
):
    take_in(xh, xeven, xodd, "gx")
    take_in(zh, zeven, zodd, "gz")
    messages = y_part(yp[0:32, :], yp[32:64, :], yp[64:96, :], zp, zh, xp, xh)
    for side in (0, 1):
        stage[side, 0:32, :], stage[side, 32:40, :] = messages[side]
    put_out(stage, even, odd, "gy")


def z_halo_residual(side, res, zh1, yh, mine):
    _, lane = plane()
    at = 3 + 4 * side
    low, high = yh[0, 0:32, at : at + 1], yh[1, 0:32, at : at + 1]
    corner = jnp.where(lane == 0, low, 0.0) + jnp.where(lane == NY - 1, high, 0.0)
    return res + zh1[side, 64:96, :] * mine + columns(zh1[side, 96:97, :]) * corner


def x_halo_residual(side, res, xh1, zh, lines, yh, mine):
    row, _ = plane()
    total = res + xh1[side, 64:96, :] * mine
    if zh is not None:
        for end, at in ((0, 0), (1, NZ - 1)):
            total += jnp.where(row == at, xh1[side, 96 + end : 97 + end, :] * zh[end, lines + side : lines + side + 1, :], 0.0)
    corner = combine(yh[0, 32 + side : 33 + side, :], yh[1, 32 + side : 33 + side, :], 0)
    return total + columns(xh1[side, 98:99, :] * corner)


def group_sums(x):
    return jnp.sum(x.reshape(4, 8, NY), axis=1)


def exact_dot(a, b):
    return jnp.dot(a, b, precision=lax.Precision.HIGHEST, preferred_element_type=F32)


def second_kernel(
    u, g, diag, s1, perm_sum, zp, yp, xp, last_coupling, xh, zh, yodd, yeven,
    yh, s0, d0, b, xp2, cross2, zy2, even, odd, line_even, line_odd,
    cross, rsum, rows, edge_s, edge_d, stage, lines,
):
    take_in(yh, yeven, yodd, "gy")
    scale = 1.0 / THETA
    low, high = yh[0, 0:32, :], yh[1, 0:32, :]
    own_y = yp[64:96, :]
    yq = own_y * combine(low, high, 0)
    yq2 = own_y * (scale * (combine(low, high, 1) + combine(low, high, 2) * yp[0:32, :]))
    zy2[2] = yq2
    zq = []
    for side, z in ((0, 0), (1, NZ - 1)):
        zq.append(zp[side, 64:96, :] * zh[side, 0:32, :])
        zy2[side] = zp[side, 64:96, :] * (scale * z_halo_residual(side, zh[side, 32:64, :], zh, yh, u[z]))
        gx = xp[side, 64:96, :]
        cross[side] = gx * xh[side, 0:32, :]
        cross2[side] = gx * (scale * x_halo_residual(side, xh[side, 32:64, :], xh, None, 0, yh, xp[side, 0:32, :]))
    rsum[...] = jnp.zeros_like(rsum)

    def start(z, carry):
        res = s1[z] + from_faces(z, cross, yq)
        s0[z] = res
        d0[z] = res * scale
        rsum[z // 8] += res * diag[z]
        return carry

    lax.fori_loop(0, NZ, start, 0, unroll=32)
    for side, z in ((0, 0), (1, NZ - 1)):
        s0[z] += zq[side]
        d0[z] += zq[side] * scale
        rsum[z // 8] += zq[side] * diag[z]
    for block in range(4):
        rows[0, 4 * block : 4 * block + 4, :] = group_sums(rsum[block])
        rows[1, 4 * block : 4 * block + 4, :] = group_sums(perm_sum[block])
    select = jnp.where(iota((NY, NY), 0) // 8 == iota((NY, NY), 1), 1.0, 0.0)
    lane16 = iota((16, NY), 1)
    weights = jnp.where(lane16 < 16, exact_dot(rows[1], select), 1.0)
    rhs = jnp.where(lane16 < 16, (OMEGA * 8.0 / 6.0) * exact_dot(rows[0], select) / weights, 0.0)
    b[...] = rhs

    def edge(z, carry):
        for side in (0, 1):
            at, _ = face_rows(side)
            before = d0[z, at, :]
            near = edge_neighbours(lambda k: d0[k, at, :], [g[k, z, at, :] for k in range(6)], z)
            res = s0[z, at, :] - before + near + from_faces_rows(z, cross2, yq2, side)
            edge_s[side, z] = res
            edge_d[side, z] = A[0] * before + B[0] * res
        return carry

    lax.fori_loop(0, NZ, edge, 0, unroll=32)
    for side in (0, 1):
        at, _ = face_rows(side)
        for end, z in ((0, 0), (1, NZ - 1)):
            edge_s[side, z] += zy2[end, at, :]
            edge_d[side, z] += B[0] * zy2[end, at, :]

    def face(z, carry):
        for side in (0, 1):
            at, r = face_rows(side)
            here = edge_d[side, z]
            near = edge_neighbours(lambda k: edge_d[side, k], [g[k, z, at, :] for k in range(6)], z)
            res = edge_s[side, z] - here + near
            xp2[side, pl.ds(z, 1), :] = here[r : r + 1]
            xp2[side, pl.ds(NZ + z, 1), :] = res[r : r + 1]
        return carry

    lax.fori_loop(0, NZ, face, 0, unroll=32)
    for side in (0, 1):
        stage[side, 0:64, :] = xp2[side]
        for z in range(4):
            stage[side, 64 + 3 * z : 67 + 3 * z, :] = rhs[4 * z + side : 4 * z + side + 3]
        stage[side, 76:80, :] = last_coupling[side, 0:4, :]
    put_out(stage, even, odd, "gx")
    for side, z in ((0, 0), (1, NZ - 1)):
        for end in (0, 1):
            lines[side, end : end + 1, :] = xh[end, z : z + 1, :]
            lines[side, 2 + end : 3 + end, :] = xh[end, 64 + z : 65 + z, :]
        lines[side, 4:LINES, :] = jnp.zeros((LINES - 4, NY), F32)
    put_out(lines, line_even, line_odd, "gz")


def edge_neighbours(rows_of, g, z):
    here = rows_of(z)
    total = g[0] * rows_of(jnp.maximum(z - 1, 0)) + g[1] * rows_of(jnp.minimum(z + 1, NZ - 1))
    total += g[2] * pltpu.roll(here, 1, 0) + g[3] * pltpu.roll(here, 7, 0)
    return total + g[4] * pltpu.roll(here, 1, 1) + g[5] * pltpu.roll(here, NY - 1, 1)


def edge_change(coupling_x, edge_z, coupling_z, edge_x, corner):
    return (coupling_x * edge_z + coupling_z * edge_x) * corner * (1.0 / THETA)


def second_block_kernel(
    u, g, s0, d0, cross2, zy2, xp, xp2, zp, xh, zh, line_odd, line_even,
    s, d, acc, zp2, yp2, xm, lh,
    s1,
):
    yq2 = zy2[2]

    def step(z, carry):
        before = d0[z]
        res = s0[z] - before + own_neighbours(d0, g, z) + from_faces(z, cross2, yq2)
        after = A[0] * before + B[0] * res
        s1[z] = res
        d[z] = after
        acc[z] = u[z] + before + after
        return carry

    lax.fori_loop(0, NZ, step, 0, unroll=32)
    for side, z in ((0, 0), (1, NZ - 1)):
        s1[z] += zy2[side]
        d[z] += B[0] * zy2[side]
        acc[z] += B[0] * zy2[side]
    take_in(lh, line_even, line_odd, "gz")
    xm[...] = xp2[:, 0:32, :]
    for end, z in ((0, 0), (1, NZ - 1)):
        for side, x in ((0, 0), (1, NX - 1)):
            change = edge_change(
                xp[side, 64 + z : 65 + z, :], xh[side, 96 + end : 97 + end, :],
                zp[end, 64 + x : 65 + x, :], zh[end, 97 + side : 98 + side, :],
                lh[end, side : side + 1, :],
            )
            s1[z, x : x + 1, :] += change
            d[z, x : x + 1, :] += B[0] * change
            acc[z, x : x + 1, :] += B[0] * change
            xm[side, z : z + 1, :] += B[0] * change

    def partial(z, carry):
        pu, ps = carry
        here = d[z]
        res = s1[z] - here + own_neighbours(d, g, z)
        s[z] = res
        mine = layer_lanes(z)
        return jnp.where(mine, pltpu.roll(here, 4 * z, 1), pu), jnp.where(mine, pltpu.roll(res, 4 * z, 1), ps)

    zero = jnp.zeros((NX, NY), F32)
    pu, ps = lax.fori_loop(0, NZ, partial, (zero, zero), unroll=8)
    yp2[0:32, :] = pu
    yp2[32:64, :] = ps
    for side, z in ((0, 0), (1, NZ - 1)):
        zp2[side, 0:32, :] = d[z]
        zp2[side, 32:64, :] = s[z]


def second_z_kernel(xodd, xeven, xp, zp, zp2, b, xh, zh, lh, xh2, even, odd, b3, stage, rows):
    take_in(xh2, xeven, xodd, "gx")
    for side, x in ((0, 0), (1, NX - 1)):
        for end, z, inner in ((0, 0, 1), (1, NZ - 1, NZ - 2)):
            change = edge_change(
                xh[side, 64 + z : 65 + z, :], zp[end, 64 + x : 65 + x, :],
                xh[side, 96 + end : 97 + end, :], lh[end, 2 + side : 3 + side, :],
                zh[end, x : x + 1, :],
            )
            turn = B[0] * change
            at = 99 + 2 * end
            beside = xh[side, at : at + 1, :] * pltpu.roll(turn, 1, 1) + xh[side, at + 1 : at + 2, :] * pltpu.roll(turn, NY - 1, 1)
            inward = xh[side, 103:104, :] if end == 0 else xh2[side, 76:77, :]
            xh2[side, z : z + 1, :] += turn
            xh2[side, 32 + z : 33 + z, :] += change - turn + beside
            xh2[side, 32 + inner : 33 + inner, :] += inward * turn
    lines = z_part(stage, zp2, xp, xh2)
    lane16 = iota((16, NY), 1)
    wide = b[...]
    for end in (0, 1):
        first = 1 - end
        rows[...] = jnp.zeros_like(rows)
        for z in range(4):
            rows[4 * z + first : 4 * z + first + 3, :] = xh2[end, 64 + 3 * z : 67 + 3 * z, :]
        base = 32 * (end + 1)
        wide = jnp.where((lane16 >= base) & (lane16 < base + 16), pltpu.roll(rows[...], base, 1), wide)
    b3[...] = wide
    for side in (0, 1):
        stage[side, 64:72, :] = lines[side]
        stage[side, 72:88, :] = wide
    put_out(stage, even, odd, "gz")


def second_y_kernel(zodd, zeven, xp, zp, yp2, xh2, b3, zh2, even, odd, stage):
    take_in(zh2, zeven, zodd, "gz")
    messages = y_part(yp2[0:32, :], yp2[32:64, :], None, zp, zh2, xp, xh2)
    within = lax.rem(iota((16, NY), 1), 32)
    parts = (b3[...], zh2[0, 72:88, :], zh2[1, 72:88, :])
    for side in (0, 1):
        stage[side, 0:32, :], stage[side, 32:40, :] = messages[side]
        coarse = jnp.zeros((16, NY), F32)
        for k in range(3):
            at = 4 * k
            moved = shift_lanes(parts[k], at - 13 * side)
            coarse = jnp.where((within >= at) & (within < at + 3), moved, coarse)
        stage[side, 40:56, :] = coarse
    put_out(stage, even, odd, "gy")


def coarse_solve(b3, zh2, yh2, ext, err, spread):
    ext[...] = jnp.zeros_like(ext)
    lane4 = iota((4, NY), 1)
    within = lax.rem(iota((16, NY), 1), 32)
    wide = []
    for k, part in enumerate((b3[...], zh2[0, 72:88, :], zh2[1, 72:88, :])):
        full = jnp.where((within >= 3) & (within < 19), shift_lanes(part, 3), 0.0)
        full = jnp.where(within < 3, shift_lanes(yh2[0, 40:56, :], -4 * k), full)
        wide.append(jnp.where((within >= 19) & (within < 22), shift_lanes(yh2[1, 40:56, :], 19 - 4 * k), full))

    for z in range(10):
        values, at = (wide[1], 4 * (z + 1)) if z < 3 else (wide[0], 4 * (z - 3)) if z < 7 else (wide[2], 4 * (z - 7))
        four = values[at : at + 4]
        own, low, high = [jnp.where(lane4 < 22, shift_lanes(four, -32 * k), 0.0) for k in range(3)]
        ext[z, 0:3, :] = low[1:4]
        ext[z, 3:7, :] = own
        ext[z, 7:10, :] = high[0:3]
    x, y = iota((16, NY), 0), iota((16, NY), 1)
    at_z, at_x, at_y = lax.axis_index("gz"), lax.axis_index("gx"), lax.axis_index("gy")
    last_z, last_x, last_y = lax.axis_size("gz") - 1, lax.axis_size("gx") - 1, lax.axis_size("gy") - 1
    inside = (x < 10) & (y < 22)
    inside &= ((x >= 3) | (at_x > 0)) & ((x < 7) | (at_x < last_x))
    inside &= ((y >= 3) | (at_y > 0)) & ((y < 19) | (at_y < last_y))
    keep = jnp.where(inside, 1.0, 0.0)
    keep_low = jnp.where(at_z > 0, keep, 0.0)
    keep_high = jnp.where(at_z < last_z, keep, 0.0)
    rhs = [ext[z] for z in range(10)]
    e = rhs
    for sweep in range(3):
        lo, hi = sweep + 1, 9 - sweep
        new = []
        for z in range(10):
            if z < lo or z >= hi:
                new.append(e[z])
                continue
            c = e[z]
            beside = e[z - 1] + e[z + 1] + pltpu.roll(c, 1, 0) + pltpu.roll(c, 15, 0) + pltpu.roll(c, 1, 1) + pltpu.roll(c, NY - 1, 1)
            v = (1.0 - OMEGA) * c + (OMEGA / 6.0) * beside + rhs[z]
            new.append(v * (keep_low if z < 3 else keep_high if z >= 7 else keep))
        e = new
    for z in range(4):
        err[4 * z : 4 * z + 4, :] = e[z + 3][3:7]
    select = jnp.where(iota((NY, NY), 0) == iota((NY, NY), 1) // 8 + 3, 1.0, 0.0)
    fine = exact_dot(err[...], select)
    for z in range(4):
        spread[z] = jnp.broadcast_to(fine[4 * z : 4 * z + 4][:, None, :], (4, 8, NY)).reshape(NX, NY)


def third_kernel(
    g, s2, d1, acc, zp, yp, xp, xh, zh, yh, xm, zp2, yp2, xh2, zh2, b3, yodd, yeven,
    far_out,
    yh2, s, d, cross, cross2, ext, err, spread, out, sems,
):
    take_in(yh2, yeven, yodd, "gy")
    low, high = yh2[0, 0:32, :], yh2[1, 0:32, :]
    own_y = yp[64:96, :]
    yu = combine(low, high, 0)
    yq = own_y * yu
    yq2 = own_y * (A[1] * yu + B[1] * (combine(low, high, 1) + combine(yh[0, 0:32, :], yh[1, 0:32, :], 2) * yp2[0:32, :]))
    zq, zq2 = [], []
    for side, z in ((0, 0), (1, NZ - 1)):
        zu, xu = zh2[side, 0:32, :], xh2[side, 0:32, :]
        zq.append(zp[side, 64:96, :] * zu)
        dz = A[1] * zu + B[1] * z_halo_residual(side, zh2[side, 32:64, :], zh, yh2, zp2[side, 0:32, :])
        zq2.append(zp[side, 64:96, :] * dz)
        gx = xp[side, 64:96, :]
        cross[side] = gx * xu
        dx = A[1] * xu + B[1] * x_halo_residual(side, xh2[side, 32:64, :], xh, zh2, 64, yh2, xm[side])
        cross2[side] = gx * dx
    coarse_solve(b3, zh2, yh2, ext, err, spread)

    def step(z, carry):
        res = s2[z] + from_faces(z, cross, yq)
        s[z] = res
        d[z] = A[1] * d1[z] + B[1] * res
        return carry

    lax.fori_loop(0, NZ, step, 0, unroll=32)
    for side, z in ((0, 0), (1, NZ - 1)):
        s[z] += zq[side]
        d[z] += B[1] * zq[side]

    def finish(z, carry):
        before = d[z]
        res = s[z] - before + own_neighbours(d, g, z) + from_faces(z, cross2, yq2)
        out[z] = acc[z] + before + (A[2] * before + B[2] * res) + spread[z // 8]
        return carry

    copies = []
    for part in range(4):
        lax.fori_loop(8 * part, 8 * part + 8, finish, 0, unroll=8)
        if part == 0:
            out[0] += B[2] * zq2[0]
        if part == 3:
            out[NZ - 1] += B[2] * zq2[1]
        rows = pl.ds(8 * part, 8)
        copies.append(pltpu.make_async_copy(out.at[rows], far_out.at[rows], sems.at[part]))
        copies[part].start()
    for copy in copies:
        copy.wait()


VM = pl.BlockSpec(memory_space=pltpu.VMEM)
HBM = pl.BlockSpec(memory_space=pltpu.HBM)
BF16_FIELD = jax.ShapeDtypeStruct((3,) + FULL, jnp.bfloat16)


def call(kernel, name, n_in, outs, scratch=(), us=0.2, place=VM, more=(), results=VM):
    return pl.pallas_call(
        kernel,
        out_shape=[x if isinstance(x, jax.ShapeDtypeStruct) else jax.ShapeDtypeStruct(x, F32) for x in outs],
        in_specs=[place] * n_in,
        out_specs=[results] * len(outs),
        scratch_shapes=[pltpu.VMEM(shape, F32) for shape in scratch] + list(more),
        compiler_params=pltpu.CompilerParams(vmem_limit_bytes=32 * 2**20),
        cost_estimate=pl.CostEstimate(flops=0, transcendentals=0, bytes_accessed=int(us * 3e6)),
        name=name,
    )


def swap(even, odd, axis):
    count = lax.axis_size(axis)
    results = []
    for first, values in ((1, odd), (0, even)):
        pairs = []
        for i in range(first, count - 1, 2):
            pairs += [(i, i + 1), (i + 1, i)]
        results.append(lax.ppermute(values, axis, pairs))
    return results[::-1]


def per_device(u, f, p, w):
    face = (2, 32, NY)
    far = [pltpu.with_memory_space_constraint(x, pltpu.HBM) for x in (u, f, p, w)]
    u, f, p, w, xp, zp, last_coupling, even, odd, zeven, zodd = call(
        face_kernel, "faces", 4,
        [FULL, FULL, FULL, BF16_FIELD, (2, XM1, NY), (2, ZM1, NY), (2, 8, NY), (XM1, NY), (XM1, NY), (ZM1, NY), (ZM1, NY)],
        (), 2.0, HBM, [pltpu.SemaphoreType.DMA((4, 4))],
    )(*far)
    g, diag, s, perm_sum, yp = call(
        block_kernel, "block", 4, [(6,) + FULL, FULL, FULL, (4, NX, NY), (96, NY)], (), 2.5
    )(u, f, p, w)
    even, odd = swap(even, odd, "gx")
    zeven, zodd = swap(zeven, zodd, "gz")
    xh, zh, yeven, yodd = call(
        first_y_kernel, "y_message", 7,
        [(2, XM1, NY), (2, ZM1, NY), (YM1, NY), (YM1, NY)],
        [(2, YM1, NY)],
    )(odd, zodd, zeven, even, xp, zp, yp)
    yeven, yodd = swap(yeven, yodd, "gy")
    yh, s, d, b, xp2, cross2, zy2, even, odd, line_even, line_odd = call(
        second_kernel, "two_steps", 13,
        [(2, YM1, NY), FULL, FULL, (16, NY), (2, 64, NY), face, (3, NX, NY), (XE2, NY), (XM2, NY), (LINES, NY), (LINES, NY)],
        [face, (4, NX, NY), (2, 16, NY), (2, NZ, 8, NY), (2, NZ, 8, NY), (2, XM2, NY), (2, LINES, NY)], 1.5,
    )(u, g, diag, s, perm_sum, zp, yp, xp, last_coupling, xh, zh, yodd, yeven)
    even, odd = swap(even, odd, "gx")
    line_even, line_odd = swap(line_even, line_odd, "gz")
    s, d1, acc, zp2, yp2, xm, lh = call(
        second_block_kernel, "block_2", 13, [FULL, FULL, FULL, (2, 64, NY), (64, NY), face, (2, LINES, NY)], [FULL], 0.01
    )(u, g, s, d, cross2, zy2, xp, xp2, zp, xh, zh, line_odd, line_even)
    xh2, even, odd, b3 = call(
        second_z_kernel, "z_message_2", 9, [(2, XM2, NY), (ZM2, NY), (ZM2, NY), (16, NY)], [(2, ZM2, NY), (16, NY)]
    )(odd, even, xp, zp, zp2, b, xh, zh, lh)
    even, odd = swap(even, odd, "gz")
    zh2, even, odd = call(
        second_y_kernel, "y_message_2", 7, [(2, ZM2, NY), (YM2, NY), (YM2, NY)], [(2, YM2, NY)]
    )(odd, even, xp, zp, yp2, xh2, b3)
    even, odd = swap(even, odd, "gy")
    (out,) = call(
        third_kernel, "last_steps", 18, [FULL],
        [(2, YM2, NY), FULL, FULL, face, face, (10, 16, NY), (16, NY), (4, NX, NY), FULL], 2.5, VM,
        [pltpu.SemaphoreType.DMA((4,))], HBM,
    )(g, s, d1, acc, zp, yp, xp, xh, zh, yh, xm, zp2, yp2, xh2, zh2, b3, odd, even)
    return out


def solution(mesh):
    placed = (
        P("gz", "gx", "gy"),
        P("gz", "gx", "gy"),
        P("gz", "gx", "gy"),
        P(None, "gz", "gx", "gy"),
    )
    return jax.shard_map(
        per_device, mesh=mesh, in_specs=placed, out_specs=P("gz", "gx", "gy"), check_vma=False
    )
```

```python
import jax
import jax.numpy as jnp
from jax import lax
from jax.experimental import pallas as pl
from jax.experimental.pallas import tpu as pltpu
from jax.sharding import PartitionSpec as P

THETA = 1.15
DELTA = 0.85
OMEGA = 0.8
F32 = jnp.float32

NZ, NX, NY = 32, 32, 128
FULL = (NZ, NX, NY)

SIGMA = THETA / DELTA
RHO0 = 1.0 / SIGMA
RHO1 = 1.0 / (2.0 * SIGMA - RHO0)
RHO2 = 1.0 / (2.0 * SIGMA - RHO1)
RHO3 = 1.0 / (2.0 * SIGMA - RHO2)
A = (RHO1 * RHO0, RHO2 * RHO1, RHO3 * RHO2)
B = (2.0 * RHO1 / DELTA, 2.0 * RHO2 / DELTA, 2.0 * RHO3 / DELTA)

XM1 = 104
ZM1 = 104
YM1 = 40
XM2 = 80
XE2 = 77
LINES = 78
ZM2 = 88
YM2 = 56


def iota(shape, dim):
    return lax.broadcasted_iota(jnp.int32, shape, dim)


def plane():
    return iota((NX, NY), 0), iota((NX, NY), 1)


def parity(axis):
    return lax.rem(lax.axis_index(axis), 2)


def put_out(stage, even, odd, axis):
    odd_one = parity(axis)
    even[...] = stage[1 - odd_one, 0 : even.shape[0], :]
    odd[...] = stage[odd_one]


def take_in(halo, even, odd, axis):
    odd_one = parity(axis)
    halo[1 - odd_one, 0 : even.shape[0], :] = even[...]
    halo[odd_one] = odd[...]


def fourths(shape=(NX, NY)):
    return lax.rem(iota(shape, 1), 4)


def layer_lanes(z, shape=(NX, NY)):
    lane = iota(shape, 1)
    return (lane == 4 * z) | (lane == lax.rem(4 * z + NY - 1, NY))


def ends(lane):
    return (lane == 0) | (lane == NY - 1)


def shift_lanes(x, amount):
    return pltpu.roll(x, amount % NY, 1)


def columns(row_values):
    row, lane = plane()
    wide = jnp.broadcast_to(row_values, (NX, NY))
    low = jnp.sum(jnp.where(lane == 4 * row, wide, 0.0), axis=1, keepdims=True)
    high = jnp.sum(jnp.where(lane == lax.rem(4 * row + NY - 1, NY), wide, 0.0), axis=1, keepdims=True)
    return jnp.where(lane == 0, low, 0.0) + jnp.where(lane == NY - 1, high, 0.0)


def combined_row(values):
    row, lane = plane()
    low = jnp.where(lane == 4 * row, jnp.broadcast_to(values[:, 0:1], (NX, NY)), 0.0)
    high = jnp.where(lane == lax.rem(4 * row + NY - 1, NY), jnp.broadcast_to(values[:, NY - 1 :], (NX, NY)), 0.0)
    return jnp.sum(low + high, axis=0, keepdims=True)


def combine(low, high, q):
    return jnp.where(fourths(low.shape) == 0, shift_lanes(low, -q), shift_lanes(high, -q - 1))


def own_neighbours(field, g, z):
    here = field[z]
    total = g[0, z] * field[jnp.maximum(z - 1, 0)] + g[1, z] * field[jnp.minimum(z + 1, NZ - 1)]
    total += g[2, z] * pltpu.roll(here, 1, 0) + g[3, z] * pltpu.roll(here, NX - 1, 0)
    total += g[4, z] * pltpu.roll(here, 1, 1) + g[5, z] * pltpu.roll(here, NY - 1, 1)
    return total


def from_faces(z, xp, yp):
    row8 = iota((8, NY), 0)
    total = jnp.where(ends(iota((NX, NY), 1)), pltpu.roll(yp, lax.rem(NY - 4 * z, NY), 1), 0.0)
    first = total[0:8] + jnp.where(row8 == 0, xp[0, pl.ds(z, 1), :], 0.0)
    last = total[NX - 8 :] + jnp.where(row8 == 7, xp[1, pl.ds(z, 1), :], 0.0)
    return jnp.concatenate([first, total[8 : NX - 8], last], axis=0)


def from_faces_rows(z, xp, yp, side):
    rows, r = face_rows(side)
    total = jnp.where(ends(iota((8, NY), 1)), pltpu.roll(yp[rows], lax.rem(NY - 4 * z, NY), 1), 0.0)
    return total + jnp.where(iota((8, NY), 0) == r, xp[side, pl.ds(z, 1), :], 0.0)


def couplings(perm, speeds):
    total = 6.0 * perm + jnp.abs(speeds[0]) + jnp.abs(speeds[1]) + jnp.abs(speeds[2])
    inverse = 1.0 / total
    pairs = []
    for speed in speeds:
        pairs.append((perm + jnp.maximum(speed, 0.0)) * inverse)
        pairs.append((perm - jnp.minimum(speed, 0.0)) * inverse)
    return total, inverse, pairs


def face_rows(side):
    return (slice(0, 8), 0) if side == 0 else (slice(NX - 8, NX), 7)


def inner_neighbours(field, c, z, side):
    rows, _ = face_rows(side)
    lane = iota((8, NY), 1)
    here = field[z, rows, :]
    total = jnp.where(z == 0, 0.0, c[0]) * field[jnp.maximum(z - 1, 0), rows, :]
    total += jnp.where(z == NZ - 1, 0.0, c[1]) * field[jnp.minimum(z + 1, NZ - 1), rows, :]
    total += c[3 - side] * pltpu.roll(here, 7 if side == 0 else 1, 0)
    total += jnp.where(lane == 0, 0.0, c[4]) * pltpu.roll(here, 1, 1)
    total += jnp.where(lane == NY - 1, 0.0, c[5]) * pltpu.roll(here, NY - 1, 1)
    return total


def face_kernel(u_far, f_far, p_far, w_far, u, f, p, w, xp, zp, last_coupling, even, odd, z_even, z_odd, sems):
    lane8 = iota((8, NY), 1)
    copies = []
    for part in range(4):
        rows = pl.ds(8 * part, 8)
        copies.append([
            pltpu.make_async_copy(u_far.at[rows], u.at[rows], sems.at[part, 0]),
            pltpu.make_async_copy(f_far.at[rows], f.at[rows], sems.at[part, 1]),
            pltpu.make_async_copy(p_far.at[rows], p.at[rows], sems.at[part, 2]),
            pltpu.make_async_copy(w_far.at[:, rows], w.at[:, rows], sems.at[part, 3]),
        ])
    for part in range(4):
        copies[part][0].start()
    for part in range(4):
        for copy in copies[part][1:]:
            copy.start()

    def face(z, side):
        rows, _ = face_rows(side)
        half = slice(0, 16) if side == 0 else slice(NX - 16, NX)
        speeds = [w[k, z, half, :].astype(F32)[8 * side : 8 * side + 8] for k in range(3)]
        return couplings(p[z, rows, :], speeds)

    def layer(z, carry):
        edges = []
        for side in (0, 1):
            rows, r = face_rows(side)
            _, inverse, c = face(z, side)
            here = u[z, rows, :]
            res = f[z, rows, :] * inverse - here + inner_neighbours(u, c, z, side)
            for base, values in ((0, here), (NZ, res), (2 * NZ, c[2 + side])):
                xp[side, pl.ds(base + z, 1), :] = values[r : r + 1]
            merged = pltpu.roll(jnp.where(lane8 == 0, c[4], c[5]), 4 * z, 1)
            edges.append(jnp.where(layer_lanes(z, (8, NY)), merged, carry[side]))
        return tuple(edges)

    edges = (jnp.zeros((8, NY), F32),) * 2
    for part in range(4):
        copies[part][0].wait()
    for part in range(4):
        for copy in copies[part][1:]:
            copy.wait()
        edges = lax.fori_loop(8 * part, 8 * part + 8, layer, edges, unroll=8)
    for side in (0, 1):
        _, r = face_rows(side)
        for end, z in ((0, 0), (1, NZ - 1)):
            _, _, c = face(z, side)
            xp[side, 96 + end : 97 + end, :] = c[end][r : r + 1]
            xp[side, 99 + 2 * end : 100 + 2 * end, :] = jnp.where(lane8 == 0, 0.0, c[4])[r : r + 1]
            xp[side, 100 + 2 * end : 101 + 2 * end, :] = jnp.where(lane8 == NY - 1, 0.0, c[5])[r : r + 1]
        xp[side, 98:99, :] = edges[side][r : r + 1]
        _, _, c = face(1, side)
        xp[side, 103:104, :] = c[0][r : r + 1]
        _, _, c = face(NZ - 2, side)
        last_coupling[side] = jnp.broadcast_to(c[1][r : r + 1], (8, NY))
    put_out(xp, even, odd, "gx")
    row, lane = plane()
    for side, z, inner in ((0, 0, 1), (1, NZ - 1, NZ - 2)):
        here = u[z]
        _, inverse, c = couplings(p[z], [w[k, z].astype(F32) for k in range(3)])
        res = f[z] * inverse - here + c[1 - side] * u[inner]
        res += jnp.where(row == 0, 0.0, c[2]) * pltpu.roll(here, 1, 0)
        res += jnp.where(row == NX - 1, 0.0, c[3]) * pltpu.roll(here, NX - 1, 0)
        res += jnp.where(lane == 0, 0.0, c[4]) * pltpu.roll(here, 1, 1)
        res += jnp.where(lane == NY - 1, 0.0, c[5]) * pltpu.roll(here, NY - 1, 1)
        zp[side, 0:32, :] = here
        zp[side, 32:64, :] = res
        zp[side, 64:96, :] = c[side]
        zp[side, 96:97, :] = combined_row(jnp.where(lane == 0, c[4], c[5]))
        zp[side, 97:98, :] = c[2][0:1]
        zp[side, 98:99, :] = c[3][NX - 1 :]
        zp[side, 99:ZM1, :] = jnp.zeros((ZM1 - 99, NY), F32)
    put_out(zp, z_even, z_odd, "gz")


def block_kernel(u, f, p, w, g, diag, s, perm_sum, yp):
    row, lane = plane()
    perm_sum[...] = jnp.zeros_like(perm_sum)

    def layer(z, carry):
        pu, ps, pg = carry
        perm = p[z]
        total, inverse, c = couplings(perm, [w[k, z].astype(F32) for k in range(3)])
        g[0, z] = jnp.where(z == 0, 0.0, c[0])
        g[1, z] = jnp.where(z == NZ - 1, 0.0, c[1])
        g[2, z] = jnp.where(row == 0, 0.0, c[2])
        g[3, z] = jnp.where(row == NX - 1, 0.0, c[3])
        g[4, z] = jnp.where(lane == 0, 0.0, c[4])
        g[5, z] = jnp.where(lane == NY - 1, 0.0, c[5])
        diag[z] = total
        here = u[z]
        res = f[z] * inverse - here + own_neighbours(u, g, z)
        s[z] = res
        perm_sum[z // 8] += perm
        mine = layer_lanes(z)
        pu = jnp.where(mine, pltpu.roll(here, 4 * z, 1), pu)
        ps = jnp.where(mine, pltpu.roll(res, 4 * z, 1), ps)
        pg = jnp.where(mine, pltpu.roll(jnp.where(lane == 0, c[4], c[5]), 4 * z, 1), pg)
        return pu, ps, pg

    zero = jnp.zeros((NX, NY), F32)
    pu, ps, pg = lax.fori_loop(0, NZ, layer, (zero, zero, zero), unroll=8)
    yp[0:32, :] = pu
    yp[32:64, :] = ps
    yp[64:96, :] = pg


def z_part(stage, faces, xp, xh):
    row, _ = plane()
    row8 = iota((8, NY), 0)
    all_lines = []
    for side, z in ((0, 0), (1, NZ - 1)):
        res = faces[side, 32:64, :]
        lines = jnp.zeros((8, NY), F32)
        for end, at in ((0, 0), (1, NX - 1)):
            line = xh[end, z : z + 1, :]
            res += jnp.where(row == at, xp[end, 64 + z : 65 + z, :] * line, 0.0)
            lines = jnp.where(row8 == end, line, lines)
        stage[side, 0:32, :] = faces[side, 0:32, :]
        stage[side, 32:64, :] = res
        all_lines.append(lines)
    return all_lines


def y_part(field, res, coupling, zp, zh, xp, xh):
    row, lane = plane()
    row8 = iota((8, NY), 0)
    z_lines = [zh[end, 0:32, :] for end in (0, 1)]
    res += jnp.where(ends(lane), zp[0, 64:96, :] * z_lines[0], 0.0)
    last = 4 * (NZ - 1)
    res += jnp.where(layer_lanes(NZ - 1), pltpu.roll(zp[1, 64:96, :] * z_lines[1], last, 1), 0.0)
    x_lines = jnp.zeros((8, NY), F32)
    for end, at in ((0, 0), (1, NX - 1)):
        line = xh[end, 0:32, :]
        res += jnp.where(row == at, combined_row(xp[end, 64:96, :] * line), 0.0)
        x_lines = jnp.where(row8 == end, combined_row(line), x_lines)
    messages = []
    q = fourths()
    for side in (0, 1):
        body = jnp.where(q == 0, shift_lanes(field, side), shift_lanes(res, 1 + side))
        if coupling is not None:
            body = jnp.where(q == 2, shift_lanes(coupling, 2 + side), body)
        for end in (0, 1):
            at = 3 + 4 * end
            body = jnp.where(lane == at, shift_lanes(z_lines[end], at + side), body)
        messages.append((body, shift_lanes(x_lines, side)))
    return messages


def first_y_kernel(
    xodd, zodd, zeven, xeven, xp, zp, yp,
    xh, zh, even, odd,
    stage,
):
    take_in(xh, xeven, xodd, "gx")
    take_in(zh, zeven, zodd, "gz")
    messages = y_part(yp[0:32, :], yp[32:64, :], yp[64:96, :], zp, zh, xp, xh)
    for side in (0, 1):
        stage[side, 0:32, :], stage[side, 32:40, :] = messages[side]
    put_out(stage, even, odd, "gy")


def z_halo_residual(side, res, zh1, yh, mine):
    _, lane = plane()
    at = 3 + 4 * side
    low, high = yh[0, 0:32, at : at + 1], yh[1, 0:32, at : at + 1]
    corner = jnp.where(lane == 0, low, 0.0) + jnp.where(lane == NY - 1, high, 0.0)
    return res + zh1[side, 64:96, :] * mine + columns(zh1[side, 96:97, :]) * corner


def x_halo_residual(side, res, xh1, zh, lines, yh, mine):
    row, _ = plane()
    total = res + xh1[side, 64:96, :] * mine
    if zh is not None:
        for end, at in ((0, 0), (1, NZ - 1)):
            total += jnp.where(row == at, xh1[side, 96 + end : 97 + end, :] * zh[end, lines + side : lines + side + 1, :], 0.0)
    corner = combine(yh[0, 32 + side : 33 + side, :], yh[1, 32 + side : 33 + side, :], 0)
    return total + columns(xh1[side, 98:99, :] * corner)


def group_sums(x):
    return jnp.sum(x.reshape(4, 8, NY), axis=1)


def exact_dot(a, b):
    return jnp.dot(a, b, precision=lax.Precision.HIGHEST, preferred_element_type=F32)


def second_kernel(
    u, g, diag, s1, perm_sum, zp, yp, xp, last_coupling, xh, zh, yodd, yeven,
    yh, s0, d0, b, xp2, cross2, zy2, even, odd, line_even, line_odd,
    cross, rsum, rows, edge_s, edge_d, stage, lines,
):
    take_in(yh, yeven, yodd, "gy")
    scale = 1.0 / THETA
    low, high = yh[0, 0:32, :], yh[1, 0:32, :]
    own_y = yp[64:96, :]
    yq = own_y * combine(low, high, 0)
    yq2 = own_y * (scale * (combine(low, high, 1) + combine(low, high, 2) * yp[0:32, :]))
    zy2[2] = yq2
    zq = []
    for side, z in ((0, 0), (1, NZ - 1)):
        zq.append(zp[side, 64:96, :] * zh[side, 0:32, :])
        zy2[side] = zp[side, 64:96, :] * (scale * z_halo_residual(side, zh[side, 32:64, :], zh, yh, u[z]))
        gx = xp[side, 64:96, :]
        cross[side] = gx * xh[side, 0:32, :]
        cross2[side] = gx * (scale * x_halo_residual(side, xh[side, 32:64, :], xh, None, 0, yh, xp[side, 0:32, :]))
    rsum[...] = jnp.zeros_like(rsum)

    def start(z, carry):
        res = s1[z] + from_faces(z, cross, yq)
        s0[z] = res
        d0[z] = res * scale
        rsum[z // 8] += res * diag[z]
        return carry

    lax.fori_loop(0, NZ, start, 0, unroll=32)
    for side, z in ((0, 0), (1, NZ - 1)):
        s0[z] += zq[side]
        d0[z] += zq[side] * scale
        rsum[z // 8] += zq[side] * diag[z]
    for block in range(4):
        rows[0, 4 * block : 4 * block + 4, :] = group_sums(rsum[block])
        rows[1, 4 * block : 4 * block + 4, :] = group_sums(perm_sum[block])
    select = jnp.where(iota((NY, NY), 0) // 8 == iota((NY, NY), 1), 1.0, 0.0)
    lane16 = iota((16, NY), 1)
    weights = jnp.where(lane16 < 16, exact_dot(rows[1], select), 1.0)
    rhs = jnp.where(lane16 < 16, (OMEGA * 8.0 / 6.0) * exact_dot(rows[0], select) / weights, 0.0)
    b[...] = rhs

    def edge(z, carry):
        for side in (0, 1):
            at, _ = face_rows(side)
            before = d0[z, at, :]
            near = edge_neighbours(lambda k: d0[k, at, :], [g[k, z, at, :] for k in range(6)], z)
            res = s0[z, at, :] - before + near + from_faces_rows(z, cross2, yq2, side)
            edge_s[side, z] = res
            edge_d[side, z] = A[0] * before + B[0] * res
        return carry

    lax.fori_loop(0, NZ, edge, 0, unroll=32)
    for side in (0, 1):
        at, _ = face_rows(side)
        for end, z in ((0, 0), (1, NZ - 1)):
            edge_s[side, z] += zy2[end, at, :]
            edge_d[side, z] += B[0] * zy2[end, at, :]

    def face(z, carry):
        for side in (0, 1):
            at, r = face_rows(side)
            here = edge_d[side, z]
            near = edge_neighbours(lambda k: edge_d[side, k], [g[k, z, at, :] for k in range(6)], z)
            res = edge_s[side, z] - here + near
            xp2[side, pl.ds(z, 1), :] = here[r : r + 1]
            xp2[side, pl.ds(NZ + z, 1), :] = res[r : r + 1]
        return carry

    lax.fori_loop(0, NZ, face, 0, unroll=32)
    for side in (0, 1):
        stage[side, 0:64, :] = xp2[side]
        for z in range(4):
            stage[side, 64 + 3 * z : 67 + 3 * z, :] = rhs[4 * z + side : 4 * z + side + 3]
        stage[side, 76:80, :] = last_coupling[side, 0:4, :]
    put_out(stage, even, odd, "gx")
    for side, z in ((0, 0), (1, NZ - 1)):
        for end in (0, 1):
            lines[side, end : end + 1, :] = xh[end, z : z + 1, :]
            lines[side, 2 + end : 3 + end, :] = xh[end, 64 + z : 65 + z, :]
        lines[side, 4:LINES, :] = jnp.zeros((LINES - 4, NY), F32)
    put_out(lines, line_even, line_odd, "gz")


def edge_neighbours(rows_of, g, z):
    here = rows_of(z)
    total = g[0] * rows_of(jnp.maximum(z - 1, 0)) + g[1] * rows_of(jnp.minimum(z + 1, NZ - 1))
    total += g[2] * pltpu.roll(here, 1, 0) + g[3] * pltpu.roll(here, 7, 0)
    return total + g[4] * pltpu.roll(here, 1, 1) + g[5] * pltpu.roll(here, NY - 1, 1)


def edge_change(coupling_x, edge_z, coupling_z, edge_x, corner):
    return (coupling_x * edge_z + coupling_z * edge_x) * corner * (1.0 / THETA)


def second_step_kernel(u, g, s0, d0, cross2, zy2, s1, d, acc):
    yq2 = zy2[2]

    def step(z, carry):
        before = d0[z]
        res = s0[z] - before + own_neighbours(d0, g, z) + from_faces(z, cross2, yq2)
        after = A[0] * before + B[0] * res
        s1[z] = res
        d[z] = after
        acc[z] = u[z] + before + after
        return carry

    lax.fori_loop(0, NZ, step, 0, unroll=32)
    for side, z in ((0, 0), (1, NZ - 1)):
        s1[z] += zy2[side]
        d[z] += B[0] * zy2[side]
        acc[z] += B[0] * zy2[side]


def second_block_kernel(
    g, s1_in, d_in, acc_in, xp, xp2, zp, xh, zh, line_odd, line_even,
    s, d, acc, zp2, yp2, xm, lh,
    s1,
):
    def keep(z, carry):
        s1[z], d[z], acc[z] = s1_in[z], d_in[z], acc_in[z]
        return carry

    lax.fori_loop(0, NZ, keep, 0, unroll=32)
    take_in(lh, line_even, line_odd, "gz")
    xm[...] = xp2[:, 0:32, :]
    for end, z in ((0, 0), (1, NZ - 1)):
        for side, x in ((0, 0), (1, NX - 1)):
            change = edge_change(
                xp[side, 64 + z : 65 + z, :], xh[side, 96 + end : 97 + end, :],
                zp[end, 64 + x : 65 + x, :], zh[end, 97 + side : 98 + side, :],
                lh[end, side : side + 1, :],
            )
            s1[z, x : x + 1, :] += change
            d[z, x : x + 1, :] += B[0] * change
            acc[z, x : x + 1, :] += B[0] * change
            xm[side, z : z + 1, :] += B[0] * change

    def partial(z, carry):
        pu, ps = carry
        here = d[z]
        res = s1[z] - here + own_neighbours(d, g, z)
        s[z] = res
        mine = layer_lanes(z)
        return jnp.where(mine, pltpu.roll(here, 4 * z, 1), pu), jnp.where(mine, pltpu.roll(res, 4 * z, 1), ps)

    zero = jnp.zeros((NX, NY), F32)
    pu, ps = lax.fori_loop(0, NZ, partial, (zero, zero), unroll=8)
    yp2[0:32, :] = pu
    yp2[32:64, :] = ps
    for side, z in ((0, 0), (1, NZ - 1)):
        zp2[side, 0:32, :] = d[z]
        zp2[side, 32:64, :] = s[z]


def second_z_kernel(xodd, xeven, xp, zp, zp2, b, xh, zh, lh, xh2, even, odd, b3, stage, rows):
    take_in(xh2, xeven, xodd, "gx")
    for side, x in ((0, 0), (1, NX - 1)):
        for end, z, inner in ((0, 0, 1), (1, NZ - 1, NZ - 2)):
            change = edge_change(
                xh[side, 64 + z : 65 + z, :], zp[end, 64 + x : 65 + x, :],
                xh[side, 96 + end : 97 + end, :], lh[end, 2 + side : 3 + side, :],
                zh[end, x : x + 1, :],
            )
            turn = B[0] * change
            at = 99 + 2 * end
            beside = xh[side, at : at + 1, :] * pltpu.roll(turn, 1, 1) + xh[side, at + 1 : at + 2, :] * pltpu.roll(turn, NY - 1, 1)
            inward = xh[side, 103:104, :] if end == 0 else xh2[side, 76:77, :]
            xh2[side, z : z + 1, :] += turn
            xh2[side, 32 + z : 33 + z, :] += change - turn + beside
            xh2[side, 32 + inner : 33 + inner, :] += inward * turn
    lines = z_part(stage, zp2, xp, xh2)
    lane16 = iota((16, NY), 1)
    wide = b[...]
    for end in (0, 1):
        first = 1 - end
        rows[...] = jnp.zeros_like(rows)
        for z in range(4):
            rows[4 * z + first : 4 * z + first + 3, :] = xh2[end, 64 + 3 * z : 67 + 3 * z, :]
        base = 32 * (end + 1)
        wide = jnp.where((lane16 >= base) & (lane16 < base + 16), pltpu.roll(rows[...], base, 1), wide)
    b3[...] = wide
    for side in (0, 1):
        stage[side, 64:72, :] = lines[side]
        stage[side, 72:88, :] = wide
    put_out(stage, even, odd, "gz")


def second_y_kernel(zodd, zeven, xp, zp, yp2, xh2, b3, zh2, even, odd, stage):
    take_in(zh2, zeven, zodd, "gz")
    messages = y_part(yp2[0:32, :], yp2[32:64, :], None, zp, zh2, xp, xh2)
    within = lax.rem(iota((16, NY), 1), 32)
    parts = (b3[...], zh2[0, 72:88, :], zh2[1, 72:88, :])
    for side in (0, 1):
        stage[side, 0:32, :], stage[side, 32:40, :] = messages[side]
        coarse = jnp.zeros((16, NY), F32)
        for k in range(3):
            at = 4 * k
            moved = shift_lanes(parts[k], at - 13 * side)
            coarse = jnp.where((within >= at) & (within < at + 3), moved, coarse)
        stage[side, 40:56, :] = coarse
    put_out(stage, even, odd, "gy")


def coarse_solve(b3, zh2, yh2, ext, err, spread):
    ext[...] = jnp.zeros_like(ext)
    lane4 = iota((4, NY), 1)
    within = lax.rem(iota((16, NY), 1), 32)
    wide = []
    for k, part in enumerate((b3[...], zh2[0, 72:88, :], zh2[1, 72:88, :])):
        full = jnp.where((within >= 3) & (within < 19), shift_lanes(part, 3), 0.0)
        full = jnp.where(within < 3, shift_lanes(yh2[0, 40:56, :], -4 * k), full)
        wide.append(jnp.where((within >= 19) & (within < 22), shift_lanes(yh2[1, 40:56, :], 19 - 4 * k), full))

    for z in range(10):
        values, at = (wide[1], 4 * (z + 1)) if z < 3 else (wide[0], 4 * (z - 3)) if z < 7 else (wide[2], 4 * (z - 7))
        four = values[at : at + 4]
        own, low, high = [jnp.where(lane4 < 22, shift_lanes(four, -32 * k), 0.0) for k in range(3)]
        ext[z, 0:3, :] = low[1:4]
        ext[z, 3:7, :] = own
        ext[z, 7:10, :] = high[0:3]
    x, y = iota((16, NY), 0), iota((16, NY), 1)
    at_z, at_x, at_y = lax.axis_index("gz"), lax.axis_index("gx"), lax.axis_index("gy")
    last_z, last_x, last_y = lax.axis_size("gz") - 1, lax.axis_size("gx") - 1, lax.axis_size("gy") - 1
    inside = (x < 10) & (y < 22)
    inside &= ((x >= 3) | (at_x > 0)) & ((x < 7) | (at_x < last_x))
    inside &= ((y >= 3) | (at_y > 0)) & ((y < 19) | (at_y < last_y))
    keep = jnp.where(inside, 1.0, 0.0)
    keep_low = jnp.where(at_z > 0, keep, 0.0)
    keep_high = jnp.where(at_z < last_z, keep, 0.0)
    rhs = [ext[z] for z in range(10)]
    e = rhs
    for sweep in range(3):
        lo, hi = sweep + 1, 9 - sweep
        new = []
        for z in range(10):
            if z < lo or z >= hi:
                new.append(e[z])
                continue
            c = e[z]
            beside = e[z - 1] + e[z + 1] + pltpu.roll(c, 1, 0) + pltpu.roll(c, 15, 0) + pltpu.roll(c, 1, 1) + pltpu.roll(c, NY - 1, 1)
            v = (1.0 - OMEGA) * c + (OMEGA / 6.0) * beside + rhs[z]
            new.append(v * (keep_low if z < 3 else keep_high if z >= 7 else keep))
        e = new
    for z in range(4):
        err[4 * z : 4 * z + 4, :] = e[z + 3][3:7]
    select = jnp.where(iota((NY, NY), 0) == iota((NY, NY), 1) // 8 + 3, 1.0, 0.0)
    fine = exact_dot(err[...], select)
    for z in range(4):
        spread[z] = jnp.broadcast_to(fine[4 * z : 4 * z + 4][:, None, :], (4, 8, NY)).reshape(NX, NY)


def third_kernel(
    g, s2, d1, acc, zp, yp, xp, xh, zh, yh, xm, zp2, yp2, xh2, zh2, b3, yodd, yeven,
    far_out,
    yh2, s, d, cross, cross2, ext, err, spread, out, sems,
):
    take_in(yh2, yeven, yodd, "gy")
    low, high = yh2[0, 0:32, :], yh2[1, 0:32, :]
    own_y = yp[64:96, :]
    yu = combine(low, high, 0)
    yq = own_y * yu
    yq2 = own_y * (A[1] * yu + B[1] * (combine(low, high, 1) + combine(yh[0, 0:32, :], yh[1, 0:32, :], 2) * yp2[0:32, :]))
    zq, zq2 = [], []
    for side, z in ((0, 0), (1, NZ - 1)):
        zu, xu = zh2[side, 0:32, :], xh2[side, 0:32, :]
        zq.append(zp[side, 64:96, :] * zu)
        dz = A[1] * zu + B[1] * z_halo_residual(side, zh2[side, 32:64, :], zh, yh2, zp2[side, 0:32, :])
        zq2.append(zp[side, 64:96, :] * dz)
        gx = xp[side, 64:96, :]
        cross[side] = gx * xu
        dx = A[1] * xu + B[1] * x_halo_residual(side, xh2[side, 32:64, :], xh, zh2, 64, yh2, xm[side])
        cross2[side] = gx * dx
    coarse_solve(b3, zh2, yh2, ext, err, spread)

    def step(z, carry):
        res = s2[z] + from_faces(z, cross, yq)
        s[z] = res
        d[z] = A[1] * d1[z] + B[1] * res
        return carry

    lax.fori_loop(0, NZ, step, 0, unroll=32)
    for side, z in ((0, 0), (1, NZ - 1)):
        s[z] += zq[side]
        d[z] += B[1] * zq[side]

    def finish(z, carry):
        before = d[z]
        res = s[z] - before + own_neighbours(d, g, z) + from_faces(z, cross2, yq2)
        out[z] = acc[z] + before + (A[2] * before + B[2] * res) + spread[z // 8]
        return carry

    copies = []
    for part in range(4):
        lax.fori_loop(8 * part, 8 * part + 8, finish, 0, unroll=8)
        if part == 0:
            out[0] += B[2] * zq2[0]
        if part == 3:
            out[NZ - 1] += B[2] * zq2[1]
        rows = pl.ds(8 * part, 8)
        copies.append(pltpu.make_async_copy(out.at[rows], far_out.at[rows], sems.at[part]))
        copies[part].start()
    for copy in copies:
        copy.wait()


VM = pl.BlockSpec(memory_space=pltpu.VMEM)
HBM = pl.BlockSpec(memory_space=pltpu.HBM)
BF16_FIELD = jax.ShapeDtypeStruct((3,) + FULL, jnp.bfloat16)


def call(kernel, name, n_in, outs, scratch=(), us=0.2, place=VM, more=(), results=VM):
    return pl.pallas_call(
        kernel,
        out_shape=[x if isinstance(x, jax.ShapeDtypeStruct) else jax.ShapeDtypeStruct(x, F32) for x in outs],
        in_specs=[place] * n_in,
        out_specs=[results] * len(outs),
        scratch_shapes=[pltpu.VMEM(shape, F32) for shape in scratch] + list(more),
        compiler_params=pltpu.CompilerParams(vmem_limit_bytes=32 * 2**20),
        cost_estimate=pl.CostEstimate(flops=0, transcendentals=0, bytes_accessed=int(us * 3e6)),
        name=name,
    )


def swap(even, odd, axis):
    count = lax.axis_size(axis)
    results = []
    for first, values in ((1, odd), (0, even)):
        pairs = []
        for i in range(first, count - 1, 2):
            pairs += [(i, i + 1), (i + 1, i)]
        results.append(lax.ppermute(values, axis, pairs))
    return results[::-1]


def per_device(u, f, p, w):
    face = (2, 32, NY)
    far = [pltpu.with_memory_space_constraint(x, pltpu.HBM) for x in (u, f, p, w)]
    u, f, p, w, xp, zp, last_coupling, even, odd, zeven, zodd = call(
        face_kernel, "faces", 4,
        [FULL, FULL, FULL, BF16_FIELD, (2, XM1, NY), (2, ZM1, NY), (2, 8, NY), (XM1, NY), (XM1, NY), (ZM1, NY), (ZM1, NY)],
        (), 2.0, HBM, [pltpu.SemaphoreType.DMA((4, 4))],
    )(*far)
    g, diag, s, perm_sum, yp = call(
        block_kernel, "block", 4, [(6,) + FULL, FULL, FULL, (4, NX, NY), (96, NY)], (), 2.5
    )(u, f, p, w)
    even, odd = swap(even, odd, "gx")
    zeven, zodd = swap(zeven, zodd, "gz")
    xh, zh, yeven, yodd = call(
        first_y_kernel, "y_message", 7,
        [(2, XM1, NY), (2, ZM1, NY), (YM1, NY), (YM1, NY)],
        [(2, YM1, NY)],
    )(odd, zodd, zeven, even, xp, zp, yp)
    yeven, yodd = swap(yeven, yodd, "gy")
    yh, s, d, b, xp2, cross2, zy2, even, odd, line_even, line_odd = call(
        second_kernel, "two_steps", 13,
        [(2, YM1, NY), FULL, FULL, (16, NY), (2, 64, NY), face, (3, NX, NY), (XE2, NY), (XM2, NY), (LINES, NY), (LINES, NY)],
        [face, (4, NX, NY), (2, 16, NY), (2, NZ, 8, NY), (2, NZ, 8, NY), (2, XM2, NY), (2, LINES, NY)], 1.5,
    )(u, g, diag, s, perm_sum, zp, yp, xp, last_coupling, xh, zh, yodd, yeven)
    even, odd = swap(even, odd, "gx")
    line_even, line_odd = swap(line_even, line_odd, "gz")
    s, d, acc = call(second_step_kernel, "step", 6, [FULL, FULL, FULL], (), 0.01)(u, g, s, d, cross2, zy2)
    s, d1, acc, zp2, yp2, xm, lh = call(
        second_block_kernel, "block_2", 11, [FULL, FULL, FULL, (2, 64, NY), (64, NY), face, (2, LINES, NY)], [FULL], 0.01
    )(g, s, d, acc, xp, xp2, zp, xh, zh, line_odd, line_even)
    xh2, even, odd, b3 = call(
        second_z_kernel, "z_message_2", 9, [(2, XM2, NY), (ZM2, NY), (ZM2, NY), (16, NY)], [(2, ZM2, NY), (16, NY)]
    )(odd, even, xp, zp, zp2, b, xh, zh, lh)
    even, odd = swap(even, odd, "gz")
    zh2, even, odd = call(
        second_y_kernel, "y_message_2", 7, [(2, ZM2, NY), (YM2, NY), (YM2, NY)], [(2, YM2, NY)]
    )(odd, even, xp, zp, yp2, xh2, b3)
    even, odd = swap(even, odd, "gy")
    (out,) = call(
        third_kernel, "last_steps", 18, [FULL],
        [(2, YM2, NY), FULL, FULL, face, face, (10, 16, NY), (16, NY), (4, NX, NY), FULL], 2.5, VM,
        [pltpu.SemaphoreType.DMA((4,))], HBM,
    )(g, s, d1, acc, zp, yp, xp, xh, zh, yh, xm, zp2, yp2, xh2, zh2, b3, odd, even)
    return out


def solution(mesh):
    placed = (
        P("gz", "gx", "gy"),
        P("gz", "gx", "gy"),
        P("gz", "gx", "gy"),
        P(None, "gz", "gx", "gy"),
    )
    return jax.shard_map(
        per_device, mesh=mesh, in_specs=placed, out_specs=P("gz", "gx", "gy"), check_vma=False
    )
```
